512 devices in a mesh: seq: 32 (over y, x), vocab: 16 (over z, core).
Axes of the slice: x: 4, y: 8, z: 8, core: 2. Of those that a mesh axis runs over, the one named last changes fastest.
Arguments:
- queries: bfloat16 [16384, 4096], P('seq', 'vocab'), may hold values from -220 to 220
- keys: bfloat16 [16384, 512], P('seq'), may hold values from -6 to 6
- values: bfloat16 [16384, 512], P('seq'), may hold values from -6 to 6
- sinks: float32 [64], P('vocab'), may hold values from 0 to 3
- doc_ids: int32 [16384], P('seq'), may hold values from 0 to 63, never falling along the last dimension, each value on 1 to 512 neighbouring positions
- upper_grad: bfloat16 [16384, 4096], P('seq', 'vocab'), may hold values from -6 to 6
- out_proj: bfloat16 [4096, 2880], P('vocab'), may hold values from -0.09375 to 0.09375
- final_hidden: bfloat16 [256, 2880], P('seq'), may hold values from -70 to 70
- advantages: bfloat16 [256], P('seq'), may hold values from -4 to 4
- slot_pos: int32 [256], P('seq'), may hold values from 0 to 511, as said below
- slot_live: int32 [256], P('seq'), may hold values 0 or 1
- sampled_ids: int32 [256], P('seq'), may hold values from 0 to 102399
- policy_head: bfloat16 [102400, 2880], P(('seq', 'vocab')), may hold values from -0.109375 to 0.109375
- reference_head: bfloat16 [102400, 2880], P(('seq', 'vocab')), may hold values from -0.109375 to 0.109375
Outputs:
- grad_queries: bfloat16 [16384, 4096], P('seq', 'vocab')
- grad_kv: bfloat16 [2, 512, 16384], P(None, 'vocab', 'seq')
- grad_sinks: float32 [64], P('vocab')
- hidden_grad: float32 [256, 2880], P('seq')
The draws below stay inside these ranges and needn't reach their ends.
Inputs may be any that keep to these rules, and one draw needn't show every extreme that they name: `slot_pos`: within one owner's 8 slots the positions are distinct.
All inputs are finite; a program needn't handle non-finite values. No bound on the sum of `slot_live` on one device may be relied on, other than what follows from the above.
Results may differ from the reference program's by a relative error of at most 0.022.
Values may be sent and summed in bfloat16 or wider, within the bound.
A program may use at most 64 MiB of HBM per device.

```python
import math
import jax
import jax.numpy as jnp
import numpy as np
from jax import lax

D = 2880
HD = 64
WINDOW = 128
RSLOT = 8
TOK_DEV = 512
VOCAB = 102400
Q_HEADS = 64
KV_HEADS = 8
TOKENS = 16384
ROWS = 256
N_SEQ = 32


def shared_keys(key):
    return jnp.clip(jax.random.normal(jax.random.fold_in(key, 77), (TOKENS, KV_HEADS * HD), jnp.float32), -6.0, 6.0)


def draw_keys(key, part):
    return shared_keys(key).astype(jnp.bfloat16)


def draw_queries(key, part):
    key = jax.random.fold_in(key, 3)
    result = jnp.clip(jax.random.normal(key, (TOKENS, Q_HEADS * HD), jnp.float32), -6.0, 6.0)
    return result.astype(jnp.bfloat16)


def draw_final_hidden(key, part):
    key = jax.random.fold_in(key, 4)
    first_key = jax.random.fold_in(key, 0)
    result = jnp.clip(3.0 * jax.random.normal(first_key, (ROWS, D), jnp.float32), -16.0, 16.0)
    return result.astype(jnp.bfloat16)


def draw_slot_pos(key, part):
    key = jax.random.fold_in(key, 6)
    owner_keys = jax.random.split(key, ROWS // RSLOT)

    def one_owner(subkey):
        order = jax.random.permutation(subkey, TOK_DEV - 1).astype(jnp.int32)
        return jnp.concatenate([jnp.full((1,), TOK_DEV - 1, jnp.int32), order[:RSLOT - 1]])
    return jax.vmap(one_owner)(owner_keys).reshape(ROWS)


def place_ends(entries, rng, least, largest):
    shape = entries.shape
    spot = [jax.random.randint(jax.random.fold_in(rng, axis), (), 0, shape[axis]) for axis in range(len(shape))]
    entries = entries.at[tuple(spot)].set(least)
    longest = shape.index(max(shape))
    spot[longest] = (spot[longest] + 1) % shape[longest]
    return entries.at[tuple(spot)].set(largest)


def levels(rng, extent, cuts, least, high):
    factor_of = 1.0
    for axis_at, blocks in cuts:
        draws = jax.random.uniform(jax.random.fold_in(jax.random.fold_in(rng, 6), axis_at), (blocks,), jnp.float32, least / len(cuts), high / len(cuts))
        factor_of = factor_of * jnp.repeat(jnp.exp(draws), extent[axis_at] // blocks).reshape((-1,) + (1,) * (len(extent) - 1 - axis_at))
    return factor_of


def ranked_wide(own_key, extent, number_of, skew):
    weights = [min(1 << octave, number_of + 1 - (1 << octave)) * (1 << 20) // math.isqrt((1 << octave) ** skew) + 1 for octave in range((number_of + 1).bit_length()) if 1 << octave <= number_of]
    scale = 1 + sum(weights) // (1 << 30)
    grid = np.cumsum(np.array([max(1, weight // scale) for weight in weights]))
    ticket = jax.random.randint(jax.random.fold_in(own_key, 1), extent, 0, int(grid[len(weights) - 1]))
    start = jnp.left_shift(1, jnp.searchsorted(jnp.asarray(grid, jnp.int32), ticket, side="right").astype(jnp.int32))
    rank = start - 1 + jax.random.randint(jax.random.fold_in(own_key, 4), extent, 0, 1 << 30) % jnp.minimum(start, number_of + 1 - start)
    return jax.random.permutation(jax.random.fold_in(own_key, 2), number_of)[rank].astype(jnp.int32)


def length_profile(count, total, limit, lean):
    loads = [(1 << 20) // math.isqrt(rank ** lean) + 1 for rank in range(2, count + 1)]
    surplus, counts = total - limit - (count - 1), [1] * (count - 1)
    while surplus > 0:
        candidates = [i for i in range(count - 1) if counts[i] < limit]
        whole, left = sum([loads[i] for i in candidates]), surplus
        for i in candidates:
            extra = min(limit - counts[i], max(1, left * loads[i] // whole), surplus)
            counts[i] = counts[i] + extra
            surplus = surplus - extra
    return np.array([limit] + counts)


def uneven_parts(stream_key, amount, total, most, slope):
    if amount == 2:
        one = jax.random.randint(stream_key, (), max(1, total - most), min(most, total - 1) + 1)
        return jnp.stack([one, total - one])
    tallies = jnp.asarray(length_profile(amount, total, most, slope), jnp.int32)
    twos = (amount - 1) // 2
    giver, sink = tallies[1:1 + 2 * twos:2], tallies[2:2 + 2 * twos:2]
    margin = jnp.minimum(giver - 1, most - sink)
    passed = jax.random.randint(jax.random.fold_in(stream_key, 1), (twos,), 0, 1 << 20) % (margin + 1)
    tallies = tallies.at[1:1 + 2 * twos:2].set(giver - passed).at[2:2 + 2 * twos:2].set(sink + passed)
    return tallies[jax.random.permutation(jax.random.fold_in(stream_key, 2), amount)]


def scatter_about(stream_key, dims, scale, most, cuts=(), kind=jnp.bfloat16):
    factor_of = levels(stream_key, dims, cuts, -0.22, 0.18) if cuts else 1.0
    values = jax.random.normal(stream_key, dims, jnp.float32) * scale * factor_of
    return jnp.minimum(jnp.maximum(values, -most), most).astype(kind)


def setup_inputs(seed: int = 0) -> dict:
    splits = jax.random.split(jax.random.key(seed), 15)
    return {
        "queries": draw_queries(jax.random.fold_in(splits[14], 71), 0),
        "keys": draw_keys(jax.random.fold_in(splits[14], 71), 0),
        "values": scatter_about(splits[2], (TOKENS, KV_HEADS * HD), 1.0, 6.0, ((0, 32),)),
        "sinks": jnp.clip(3.0 * jax.random.uniform(splits[3], (Q_HEADS,), jnp.float32) ** levels(splits[3], (Q_HEADS,), ((0, 16),), -0.2, 0.2), 0.0, 3.0),
        "doc_ids": jnp.searchsorted(jnp.cumsum(uneven_parts(splits[4], TOKENS // (2 * WINDOW), TOKENS, 4 * WINDOW, 2)), jnp.arange(TOKENS), side="right").astype(jnp.int32),
        "upper_grad": scatter_about(splits[5], (TOKENS, Q_HEADS * HD), 1.0, 6.0, ((0, 32), (1, 16))),
        "out_proj": scatter_about(splits[6], (Q_HEADS * HD, D), (Q_HEADS * HD) ** -0.5, 0.09375, ((0, 16),)),
        "final_hidden": draw_final_hidden(jax.random.fold_in(splits[14], 71), 0),
        "advantages": scatter_about(splits[8], (ROWS,), 1.0, 4.0, ((0, 32),)),
        "slot_pos": draw_slot_pos(jax.random.fold_in(splits[14], 71), 0),
        "slot_live": place_ends((jax.random.randint(splits[10], (ROWS,), 0, 4) < 3).astype(jnp.int32), jax.random.fold_in(splits[10], 1), 0, 1),
        "sampled_ids": place_ends(ranked_wide(splits[11], (ROWS,), VOCAB, 2), jax.random.fold_in(splits[11], 3), 0, VOCAB - 1).astype(jnp.int32),
        "policy_head": scatter_about(splits[12], (VOCAB, D), D ** -0.5, 0.109375, ((0, 512),)),
        "reference_head": scatter_about(splits[13], (VOCAB, D), D ** -0.5, 0.109375, ((0, 512),)),
    }


loss_scale = 64.0
kl_weight = 1.0
masked_score = -1.0e30


def head_gradient(final_hidden, advantages, slot_live, sampled_ids, policy_head, reference_head):
    contract = (((1,), (1,)), ((), ()))
    policy_logits = lax.dot_general(final_hidden, policy_head, contract, preferred_element_type=jnp.float32)
    frozen_logits = lax.dot_general(final_hidden, reference_head, contract, preferred_element_type=jnp.float32)
    policy_peak = jnp.max(policy_logits, axis=1, keepdims=True)
    frozen_peak = jnp.max(frozen_logits, axis=1, keepdims=True)
    policy_lognorm = policy_peak + jnp.log(jnp.sum(jnp.exp(policy_logits - policy_peak), axis=1, keepdims=True))
    frozen_lognorm = frozen_peak + jnp.log(jnp.sum(jnp.exp(frozen_logits - frozen_peak), axis=1, keepdims=True))
    policy_prob = jnp.exp(policy_logits - policy_lognorm)
    divergence = jnp.sum(policy_prob * (policy_logits - frozen_logits), axis=1, keepdims=True) - policy_lognorm + frozen_lognorm
    vocab_ids = jnp.arange(VOCAB, dtype=jnp.int32)
    picked = (vocab_ids[None, :] == sampled_ids[:, None]).astype(jnp.float32)
    weight = loss_scale * slot_live.astype(jnp.float32)[:, None]
    advantage_rows = advantages.astype(jnp.float32)[:, None]
    log_ratio = (policy_logits - policy_lognorm) - (frozen_logits - frozen_lognorm) - divergence
    logit_grad = weight * (-advantage_rows * (picked - policy_prob) + kl_weight * policy_prob * log_ratio)
    logit_grad = logit_grad.astype(jnp.bfloat16)
    return jnp.dot(logit_grad, policy_head, preferred_element_type=jnp.float32)


def reference(queries, keys, values, sinks, doc_ids, upper_grad, out_proj, final_hidden, advantages, slot_pos, slot_live, sampled_ids, policy_head, reference_head):
    hidden_grad = head_gradient(final_hidden, advantages, slot_live, sampled_ids, policy_head, reference_head)
    slot_grad = lax.dot_general(hidden_grad.astype(jnp.bfloat16), out_proj, (((1,), (1,)), ((), ())), preferred_element_type=jnp.float32)
    owners = jnp.arange(ROWS, dtype=jnp.int32) // RSLOT
    landing = owners * TOK_DEV + slot_pos
    grad_out = upper_grad.astype(jnp.float32).at[landing].add(slot_grad).astype(jnp.bfloat16)

    group = Q_HEADS // KV_HEADS
    scale = HD ** -0.5
    width = KV_HEADS * HD
    key_pad = jnp.concatenate([jnp.zeros((WINDOW, width), jnp.bfloat16), keys], axis=0)
    value_pad = jnp.concatenate([jnp.zeros((WINDOW, width), jnp.bfloat16), values], axis=0)
    doc_pad = jnp.concatenate([jnp.full((WINDOW,), -1, jnp.int32), doc_ids], axis=0)
    offsets = jnp.arange(TOK_DEV, dtype=jnp.int32)[:, None] + WINDOW - jnp.arange(TOK_DEV + WINDOW, dtype=jnp.int32)[None, :]
    band = (offsets >= 0) & (offsets < WINDOW)
    sink_col = sinks[:, None, None]

    def block_step(carry, block):
        key_acc, value_acc, sink_acc = carry
        start = (block * TOK_DEV).astype(jnp.int32)
        query_blk = lax.dynamic_slice_in_dim(queries, start, TOK_DEV, 0).astype(jnp.float32).reshape(TOK_DEV, Q_HEADS, HD)
        grad_blk = lax.dynamic_slice_in_dim(grad_out, start, TOK_DEV, 0).astype(jnp.float32).reshape(TOK_DEV, Q_HEADS, HD)
        key_blk = lax.dynamic_slice_in_dim(key_pad, start, TOK_DEV + WINDOW, 0).astype(jnp.float32).reshape(TOK_DEV + WINDOW, KV_HEADS, HD)
        value_blk = lax.dynamic_slice_in_dim(value_pad, start, TOK_DEV + WINDOW, 0).astype(jnp.float32).reshape(TOK_DEV + WINDOW, KV_HEADS, HD)
        key_rep = jnp.repeat(key_blk, group, axis=1)
        value_rep = jnp.repeat(value_blk, group, axis=1)
        doc_keys = lax.dynamic_slice_in_dim(doc_pad, start, TOK_DEV + WINDOW, 0)
        doc_query = lax.dynamic_slice_in_dim(doc_pad, start + WINDOW, TOK_DEV, 0)
        allowed = (band & (doc_query[:, None] == doc_keys[None, :]))[None]
        scores = jnp.einsum("qhd,khd->hqk", query_blk, key_rep) * scale
        masked = jnp.where(allowed, scores, masked_score)
        row_top = jnp.maximum(jnp.max(masked, axis=2, keepdims=True), sink_col)
        exp_terms = jnp.where(allowed, jnp.exp(masked - row_top), 0.0)
        sink_term = jnp.exp(sink_col - row_top)
        total = jnp.sum(exp_terms, axis=2, keepdims=True) + sink_term
        attn_prob = exp_terms / total
        sink_share = sink_term / total
        attn_low = lax.optimization_barrier(attn_prob.astype(jnp.bfloat16)).astype(jnp.float32)
        attended = jnp.einsum("hqk,khd->qhd", attn_low, value_rep)
        delta = jnp.transpose(jnp.sum(grad_blk * attended, axis=2))[:, :, None]
        dprob = jnp.einsum("qhd,khd->hqk", grad_blk, value_rep)
        dscore = lax.optimization_barrier((attn_prob * (dprob - delta)).astype(jnp.bfloat16)).astype(jnp.float32)
        grad_query = (jnp.einsum("hqk,khd->qhd", dscore, key_rep) * scale).astype(jnp.bfloat16).reshape(TOK_DEV, Q_HEADS * HD)
        key_heads = jnp.einsum("hqk,qhd->khd", dscore, query_blk) * scale
        value_heads = jnp.einsum("hqk,qhd->khd", attn_low, grad_blk)
        key_part = jnp.sum(key_heads.reshape(TOK_DEV + WINDOW, KV_HEADS, group, HD), axis=2).reshape(TOK_DEV + WINDOW, width)
        value_part = jnp.sum(value_heads.reshape(TOK_DEV + WINDOW, KV_HEADS, group, HD), axis=2).reshape(TOK_DEV + WINDOW, width)
        key_acc = lax.dynamic_update_slice_in_dim(key_acc, lax.dynamic_slice_in_dim(key_acc, start, TOK_DEV + WINDOW, 0) + key_part, start, 0)
        value_acc = lax.dynamic_update_slice_in_dim(value_acc, lax.dynamic_slice_in_dim(value_acc, start, TOK_DEV + WINDOW, 0) + value_part, start, 0)
        sink_acc = sink_acc - jnp.sum(sink_share * delta, axis=(1, 2))
        return (key_acc, value_acc, sink_acc), grad_query

    start_carry = (jnp.zeros((TOKENS + WINDOW, width), jnp.float32), jnp.zeros((TOKENS + WINDOW, width), jnp.float32), jnp.zeros((Q_HEADS,), jnp.float32))
    final_carry, query_blocks = lax.scan(block_step, start_carry, jnp.arange(N_SEQ, dtype=jnp.int32))
    key_acc, value_acc, grad_sinks = final_carry
    grad_queries = query_blocks.reshape(TOKENS, Q_HEADS * HD)
    grad_kv = jnp.stack([jnp.transpose(key_acc[WINDOW:]), jnp.transpose(value_acc[WINDOW:])]).astype(jnp.bfloat16)
    return grad_queries, grad_kv, grad_sinks, hidden_grad
```

```python
import jax
import jax.numpy as jnp
from jax import lax
from jax.experimental import pallas as pl
from jax.experimental.pallas import tpu as pltpu
from jax.sharding import PartitionSpec as P

HD = 64
WINDOW = 128
NX, NY, NZ, NC = 4, 8, 8, 2
D = 2880
QUARTER = 768
HALF = 2 * QUARTER
SLOTS = 8

loss_scale = 64.0
kl_weight = 1.0
masked_score = -1e30
contract_last = (((1,), (1,)), ((), ()))
contract_first = (((0,), (0,)), ((), ()))
MESH = pl.DeviceIdType.MESH
f32 = jnp.float32
bf16 = jnp.bfloat16


def wrap(value, size):
    return lax.rem(value + size, size)


def position():
    seq, vocab = lax.axis_index("seq"), lax.axis_index("vocab")
    return lax.rem(seq, NX), lax.div(seq, NX), lax.div(vocab, NC), lax.rem(vocab, NC)


def device(x, y, z, c):
    return (y * NX + x, z * NC + c)


def unfold(block, row):
    return jnp.concatenate([block[row : row + 1], block[row + 3 : row + 4]], axis=1)


def fold(rows):
    half = rows[0].shape[1] // 2
    parts = [row[:, :half] for row in rows] + [row[:, half:] for row in rows]
    return jnp.concatenate(parts + [jnp.zeros((2, half), f32)], axis=0)


def merged(blocks):
    rows = [[unfold(block, k) for block in blocks] for k in range(3)]
    tops = [rows[0][0], rows[1][0]]
    for k in range(2):
        for row in rows[k][1:]:
            tops[k] = jnp.maximum(tops[k], row)
    mass, cross, frozen = 0.0, 0.0, 0.0
    for policy, other, mean in zip(*rows):
        share = jnp.exp(policy - tops[0])
        mass += share
        cross += share * mean
        frozen += jnp.exp(other - tops[1])
    return [tops[0] + jnp.log(mass), tops[1] + jnp.log(frozen), cross / mass]


def head_kernel(
    hidden_ref,
    meta_ref,
    policy_hbm,
    frozen_hbm,
    out_ref,
    policy_ref,
    frozen_ref,
    wide,
    gathered,
    rows_ref,
    meta_y,
    meta_x,
    stat_xc,
    stat_y,
    stat_z,
    total,
    outgoing,
    from_core,
    send_x,
    from_x,
    send_y,
    from_y,
    from_z,
    final,
    load_sem,
    gy_s,
    gy_r,
    gx_s,
    gx_r,
    gc_s,
    gc_r,
    my_s,
    my_r,
    mx_s,
    mx_r,
    sx_s,
    sx_r,
    sy_s,
    sy_r,
    sz_s,
    sz_r,
    rc_s,
    rc_r,
    rx_s,
    rx_r,
    ry_s,
    ry_r,
    rz_s,
    rz_r,
    fc_s,
    fc_r,
):
    x, y, z, c = position()
    vocab_rows = policy_ref.shape[0]
    load_policy = pltpu.make_async_copy(policy_hbm, policy_ref, load_sem.at[0])
    load_frozen = pltpu.make_async_copy(frozen_hbm, frozen_ref, load_sem.at[1])
    load_policy.start()
    load_frozen.start()

    def along_x(d, other):
        return device(wrap(x + d, NX), y, z, c if other == 0 else 1 - c)

    def along_y(d):
        return device(x, wrap(y + d, NY), z, c)

    def along_z(d):
        return device(x, y, wrap(z + d, NZ), c)

    across = device(x, y, z, 1 - c)
    xc_steps = [(d, o) for d in range(NX) for o in range(NC) if d or o]

    def send(src, dst, send_sem, recv_sem, target):
        copy = pltpu.make_async_remote_copy(
            src_ref=src,
            dst_ref=dst,
            send_sem=send_sem,
            recv_sem=recv_sem,
            device_id=target,
            device_id_type=MESH,
        )
        copy.start()
        return copy

    barrier = pltpu.get_barrier_semaphore()
    peers = [along_x(d, o) for d, o in xc_steps]
    peers += [along_y(d) for d in range(1, NY)] + [along_z(d) for d in range(1, NZ)]
    for peer in peers:
        pl.semaphore_signal(barrier, inc=1, device_id=peer, device_id_type=MESH)

    hidden = hidden_ref[...].astype(f32)
    wide[3] = jnp.zeros((SLOTS, QUARTER), f32)
    for q in range(4):
        stop = min(D, (q + 1) * QUARTER)
        wide[q, :, : stop - q * QUARTER] = hidden[:, q * QUARTER : stop]
    gathered[c, x, y] = jnp.concatenate([wide[2 * c], wide[2 * c + 1]], axis=0).astype(bf16)
    meta_y[y] = meta_ref[...]
    pl.semaphore_wait(barrier, len(peers))

    copies_y = [
        send(gathered.at[c, x, y], gathered.at[c, x, y], gy_s.at[d], gy_r.at[d], along_y(d))
        for d in range(1, NY)
    ]
    metas_y = [
        send(meta_y.at[y], meta_y.at[y], my_s.at[d], my_r.at[d], along_y(d)) for d in range(1, NY)
    ]
    for copy in copies_y:
        copy.wait()
    copies_x = [
        send(gathered.at[c, x], gathered.at[c, x], gx_s.at[d], gx_r.at[d], along_x(d, 0))
        for d in range(1, NX)
    ]

    def cross_send(group):
        return send(
            gathered.at[c, group], gathered.at[c, group], gc_s.at[group], gc_r.at[group], across
        )

    def arrange(half, group):
        block = gathered[half, group].astype(f32).reshape(NY, 2, SLOTS, QUARTER)
        start = pl.multiple_of(group * (NY * SLOTS), NY * SLOTS)
        for part in range(2):
            rows_ref[2 * half + part, pl.ds(start, NY * SLOTS), :] = (
                block[:, part].reshape(NY * SLOTS, QUARTER).astype(bf16)
            )

    copies_c = [cross_send(x)]
    arrange(c, x)
    for copy in metas_y:
        copy.wait()
    meta = meta_y[0]
    for k in range(1, NY):
        meta += meta_y[k]
    meta_x[x] = meta
    metas_x = [
        send(meta_x.at[x], meta_x.at[x], mx_s.at[d], mx_r.at[d], along_x(d, 0))
        for d in range(1, NX)
    ]
    for d in range(1, NX):
        copies_x[d - 1].wait()
        group = wrap(x - d, NX)
        copies_c.append(cross_send(group))
        arrange(c, group)
    for d, copy in enumerate(copies_c):
        group = wrap(x - d, NX)
        pltpu.make_async_remote_copy(
            src_ref=gathered.at[1 - c, group],
            dst_ref=gathered.at[1 - c, group],
            send_sem=gc_s.at[group],
            recv_sem=gc_r.at[group],
            device_id=across,
            device_id_type=MESH,
        ).wait_recv()
        arrange(1 - c, group)
    for copy in copies_c:
        copy.wait_send()
    for copy in metas_x:
        copy.wait()
    meta = meta_x[0]
    for k in range(1, NX):
        meta += meta_x[k]

    load_policy.wait()
    load_frozen.wait()

    def logits_of(head):
        result = 0.0
        for q in range(4):
            stop = min(D, (q + 1) * QUARTER)
            result += lax.dot_general(
                head[:, q * QUARTER : stop],
                rows_ref[q, :, : stop - q * QUARTER],
                contract_last,
                preferred_element_type=f32,
            )
        return result

    policy_logits = logits_of(policy_ref)
    frozen_logits = logits_of(frozen_ref)
    policy_peak = jnp.max(policy_logits, axis=0, keepdims=True)
    frozen_peak = jnp.max(frozen_logits, axis=0, keepdims=True)
    logit_diff = policy_logits - frozen_logits
    policy_terms = jnp.exp(policy_logits - policy_peak)
    mass = jnp.sum(policy_terms, axis=0, keepdims=True)
    mean = jnp.sum(policy_terms * logit_diff, axis=0, keepdims=True) / mass
    frozen_mass = jnp.sum(jnp.exp(frozen_logits - frozen_peak), axis=0, keepdims=True)
    stats = [policy_peak + jnp.log(mass), frozen_peak + jnp.log(frozen_mass), mean]

    stat_xc[0] = fold(stats)
    copies = [
        send(stat_xc.at[0], stat_xc.at[k + 1], sx_s.at[k], sx_r.at[k], along_x(d, o))
        for k, (d, o) in enumerate(xc_steps)
    ]
    for copy in copies:
        copy.wait()
    stat_y[0] = fold(merged([stat_xc[k] for k in range(NX * NC)]))
    copies = [
        send(stat_y.at[0], stat_y.at[d], sy_s.at[d], sy_r.at[d], along_y(d)) for d in range(1, NY)
    ]
    for copy in copies:
        copy.wait()
    stat_z[0] = fold(merged([stat_y[k] for k in range(NY)]))
    copies = [
        send(stat_z.at[0], stat_z.at[d], sz_s.at[d], sz_r.at[d], along_z(d)) for d in range(1, NZ)
    ]
    for copy in copies:
        copy.wait()
    policy_lognorm, frozen_lognorm, cross_total = merged([stat_z[k] for k in range(NZ)])

    divergence = cross_total - policy_lognorm + frozen_lognorm
    policy_prob = jnp.exp(policy_logits - policy_lognorm)
    first_id = (lax.axis_index("seq") * (NZ * NC) + lax.axis_index("vocab")) * vocab_rows
    ids_here = (first_id + lax.broadcasted_iota(jnp.int32, policy_logits.shape, 0)).astype(f32)
    picked = (ids_here == unfold(meta, 1)).astype(f32)
    weight = loss_scale * unfold(meta, 2)
    log_ratio = policy_logits - policy_lognorm - (frozen_logits - frozen_lognorm) - divergence
    logit_grad = (
        weight * (-unfold(meta, 0) * (picked - policy_prob) + kl_weight * policy_prob * log_ratio)
    ).astype(bf16)

    total[1, :, QUARTER:] = jnp.zeros((total.shape[1], QUARTER), f32)
    for q in range(4):
        stop = min(D, (q + 1) * QUARTER)
        half, low = q // 2, (q % 2) * QUARTER
        total[half, :, low : low + stop - q * QUARTER] = lax.dot_general(
            logit_grad, policy_ref[:, q * QUARTER : stop], contract_first, preferred_element_type=f32
        )
    outgoing[...] = total[1 - c].astype(bf16)
    copy = send(outgoing, from_core, rc_s, rc_r, across)
    copy.wait()
    group_rows = NY * SLOTS
    for g in range(NX):
        rows = slice(g * group_rows, (g + 1) * group_rows)
        both = total[c, rows, :] + from_core[rows, :].astype(f32)
        total[c, rows, :] = both
        send_x[g] = both.astype(bf16)
    copies = [
        send(send_x.at[wrap(x + d, NX)], from_x.at[d - 1], rx_s.at[d], rx_r.at[d], along_x(d, 0))
        for d in range(1, NX)
    ]
    for copy in copies:
        copy.wait()
    mine = total[c, pl.ds(pl.multiple_of(x * group_rows, group_rows), group_rows), :]
    for k in range(NX - 1):
        mine += from_x[k].astype(f32)
    mine = mine.reshape(NY, SLOTS, HALF)
    packed = jnp.concatenate([mine[:, :, :QUARTER], mine[:, :, QUARTER:]], axis=1)
    send_y[...] = packed.astype(bf16)
    copies = [
        send(send_y.at[wrap(y + d, NY)], from_y.at[d - 1], ry_s.at[d], ry_r.at[d], along_y(d))
        for d in range(1, NY)
    ]
    for copy in copies:
        copy.wait()
    summed = send_y[y].astype(f32)
    for k in range(NY - 1):
        summed += from_y[k].astype(f32)
    from_z[z] = summed.astype(bf16)
    copies = [
        send(from_z.at[z], from_z.at[z], rz_s.at[d], rz_r.at[d], along_z(d)) for d in range(1, NZ)
    ]
    for copy in copies:
        copy.wait()
    summed = from_z[0].astype(f32)
    for k in range(1, NZ):
        summed += from_z[k].astype(f32)
    final[c] = summed
    copy = send(final.at[c], final.at[c], fc_s, fc_r, across)
    copy.wait()
    for q in range(4):
        stop = min(D, (q + 1) * QUARTER)
        part = final[q // 2, (q % 2) * SLOTS : (q % 2 + 1) * SLOTS, :]
        out_ref[:, q * QUARTER : stop] = part[:, : stop - q * QUARTER]


def head_gradient(final_hidden, advantages, slot_live, sampled_ids, policy_head, reference_head):
    x, y, _, _ = position()
    rows = NX * NY * SLOTS
    values = jnp.stack([advantages.astype(f32), sampled_ids.astype(f32), slot_live.astype(f32)])
    here = lax.broadcasted_iota(jnp.int32, (3, rows), 1) // SLOTS == x * NY + y
    placed = jnp.where(here, jnp.tile(values, (1, NX * NY)), 0.0)
    meta = jnp.concatenate(
        [placed[:, : rows // 2], placed[:, rows // 2 :], jnp.zeros((2, rows // 2), f32)], axis=0
    )
    dma = pltpu.SemaphoreType.DMA
    vmem = pl.BlockSpec(memory_space=pltpu.VMEM)
    stat = (8, rows // 2)
    scratch = [
        pltpu.VMEM(policy_head.shape, bf16),
        pltpu.VMEM(reference_head.shape, bf16),
        pltpu.VMEM((4, SLOTS, QUARTER), f32),
        pltpu.VMEM((2, NX, NY, 2 * SLOTS, QUARTER), bf16),
        pltpu.VMEM((4, rows, QUARTER), bf16),
        pltpu.VMEM((NY,) + stat, f32),
        pltpu.VMEM((NX,) + stat, f32),
        pltpu.VMEM((NX * NC,) + stat, f32),
        pltpu.VMEM((NY,) + stat, f32),
        pltpu.VMEM((NZ,) + stat, f32),
        pltpu.VMEM((2, rows, HALF), f32),
        pltpu.VMEM((rows, HALF), bf16),
        pltpu.VMEM((rows, HALF), bf16),
        pltpu.VMEM((NX, NY * SLOTS, HALF), bf16),
        pltpu.VMEM((NX - 1, NY * SLOTS, HALF), bf16),
        pltpu.VMEM((NY, 2 * SLOTS, QUARTER), bf16),
        pltpu.VMEM((NY - 1, 2 * SLOTS, QUARTER), bf16),
        pltpu.VMEM((NZ, 2 * SLOTS, QUARTER), bf16),
        pltpu.VMEM((2, 2 * SLOTS, QUARTER), f32),
        dma((2,)),
    ]
    for size in (NY, NX, NX, NY, NX, NX * NC, NY, NZ):
        scratch += [dma((size,)), dma((size,))]
    scratch += [dma, dma]
    for size in (NX, NY, NZ):
        scratch += [dma((size,)), dma((size,))]
    scratch += [dma, dma]
    return pl.pallas_call(
        head_kernel,
        out_shape=jax.ShapeDtypeStruct(final_hidden.shape, f32),
        in_specs=[vmem, vmem, pl.BlockSpec(memory_space=pl.ANY), pl.BlockSpec(memory_space=pl.ANY)],
        out_specs=vmem,
        scratch_shapes=scratch,
        compiler_params=pltpu.CompilerParams(
            collective_id=0, has_side_effects=True, vmem_limit_bytes=48 * 2**20
        ),
    )(final_hidden, meta, policy_head, reference_head)


def passed_along(value, axis, steps):
    count = lax.axis_size(axis)
    leading, last = (max(0, -steps), min(count, count - steps))
    return lax.ppermute(value, axis, [(source, source + steps) for source in range(leading, last)])


def partner(shard, axis, distance):
    return lax.ppermute(shard, axis, [(i, i ^ 1 << distance) for i in range(lax.axis_size(axis))])


def strip_rows(extended, tiles, window):
    shaped = extended.reshape((tiles + 1, window) + extended.shape[1:])
    return jnp.concatenate([shaped[:-1], shaped[1:]], axis=1)


def shards(
    queries,
    keys,
    values,
    sinks,
    doc_ids,
    upper_grad,
    out_proj,
    final_hidden,
    advantages,
    slot_pos,
    slot_live,
    sampled_ids,
    policy_head,
    reference_head,
):
    hidden_grad = head_gradient(
        final_hidden, advantages, slot_live, sampled_ids, policy_head, reference_head
    )
    tokens_here = queries.shape[0]
    heads_here = sinks.shape[0]
    owner_rows = final_hidden.shape[0]
    tiles = tokens_here // WINDOW
    scale = HD ** (-0.5)
    kv_index = lax.axis_index("vocab") // 2
    own_keys = lax.dynamic_slice_in_dim(keys, kv_index * HD, HD, 1)
    own_values = lax.dynamic_slice_in_dim(values, kv_index * HD, HD, 1)
    doc_marks = (doc_ids + 1).astype(jnp.bfloat16)
    tail_keys, tail_values, tail_marks = passed_along(
        (own_keys[-WINDOW:], own_values[-WINDOW:], doc_marks[-WINDOW:]), "seq", 1
    )
    ext_keys = jnp.concatenate([tail_keys, own_keys], axis=0)
    ext_values = jnp.concatenate([tail_values, own_values], axis=0)
    ext_marks = jnp.concatenate([tail_marks, doc_marks], axis=0)
    slot_grad = lax.dot_general(
        hidden_grad.astype(jnp.bfloat16),
        out_proj,
        contract_last,
        preferred_element_type=jnp.float32,
    )
    positions = lax.broadcasted_iota(jnp.int32, (tokens_here, owner_rows), 0)
    landing = (positions == slot_pos[None, :]).astype(jnp.float32)
    grad_out = (
        upper_grad.astype(jnp.float32)
        + jnp.dot(landing, slot_grad, preferred_element_type=jnp.float32)
    ).astype(jnp.bfloat16)
    query_tiles = queries.reshape(tiles, WINDOW, heads_here, HD)
    grad_tiles = grad_out.reshape(tiles, WINDOW, heads_here, HD)
    key_strips = strip_rows(ext_keys, tiles, WINDOW)
    value_strips = strip_rows(ext_values, tiles, WINDOW)
    mark_strips = strip_rows(ext_marks, tiles, WINDOW)
    query_marks = doc_marks.reshape(tiles, WINDOW)
    offsets = (
        lax.broadcasted_iota(jnp.int32, (WINDOW, 2 * WINDOW), 0)
        + WINDOW
        - lax.broadcasted_iota(jnp.int32, (WINDOW, 2 * WINDOW), 1)
    )
    band = (offsets >= 0) & (offsets < WINDOW)
    allowed = (band[None] & (query_marks[:, :, None] == mark_strips[:, None, :]))[:, None]
    sink_col = sinks[None, :, None, None]
    scores = (
        jnp.einsum("tqhd,tkd->thqk", query_tiles, key_strips, preferred_element_type=jnp.float32)
        * scale
    )
    masked = jnp.where(allowed, scores, masked_score)
    row_top = jnp.maximum(jnp.max(masked, axis=3, keepdims=True), sink_col)
    exp_terms = jnp.where(allowed, jnp.exp(masked - row_top), 0.0)
    sink_term = jnp.exp(sink_col - row_top)
    total = jnp.sum(exp_terms, axis=3, keepdims=True) + sink_term
    attn_prob = exp_terms / total
    attn_low = attn_prob.astype(jnp.bfloat16)
    attended = jnp.einsum(
        "thqk,tkd->tqhd", attn_low, value_strips, preferred_element_type=jnp.float32
    )
    delta = jnp.transpose(jnp.sum(grad_tiles.astype(jnp.float32) * attended, axis=3), (0, 2, 1))[
        ..., None
    ]
    dprob = jnp.einsum(
        "tqhd,tkd->thqk", grad_tiles, value_strips, preferred_element_type=jnp.float32
    )
    dscore = (attn_prob * (dprob - delta)).astype(jnp.bfloat16)
    grad_queries = (
        (
            jnp.einsum("thqk,tkd->tqhd", dscore, key_strips, preferred_element_type=jnp.float32)
            * scale
        )
        .astype(jnp.bfloat16)
        .reshape(tokens_here, heads_here * HD)
    )
    key_strip_grad = (
        jnp.einsum("thqk,tqhd->tkd", dscore, query_tiles, preferred_element_type=jnp.float32)
        * scale
    )
    value_strip_grad = jnp.einsum(
        "thqk,tqhd->tkd", attn_low, grad_tiles, preferred_element_type=jnp.float32
    )
    edge = jnp.zeros((1, WINDOW, HD), jnp.float32)
    key_grad = (
        jnp.concatenate([key_strip_grad[:, :WINDOW], edge], axis=0)
        + jnp.concatenate([edge, key_strip_grad[:, WINDOW:]], axis=0)
    ).reshape(tokens_here + WINDOW, HD)
    value_grad = (
        jnp.concatenate([value_strip_grad[:, :WINDOW], edge], axis=0)
        + jnp.concatenate([edge, value_strip_grad[:, WINDOW:]], axis=0)
    ).reshape(tokens_here + WINDOW, HD)
    sink_grad = -jnp.sum(sink_term / total * delta, axis=(0, 2, 3))
    back_key, back_value = (
        passed_along(key_grad[:WINDOW].astype(jnp.bfloat16), "seq", -1).astype(jnp.float32),
        passed_along(value_grad[:WINDOW].astype(jnp.bfloat16), "seq", -1).astype(jnp.float32),
    )
    filler = jnp.zeros((tokens_here - WINDOW, HD), jnp.float32)
    own_key = key_grad[WINDOW:] + jnp.concatenate([filler, back_key], axis=0)
    own_value = value_grad[WINDOW:] + jnp.concatenate([filler, back_value], axis=0)
    stacked = jnp.stack([own_key, own_value])
    half_width = HD // 2
    parity = lax.axis_index("vocab") % 2
    outgoing = lax.dynamic_slice_in_dim(stacked, (1 - parity) * half_width, half_width, 2)
    kept_half = lax.dynamic_slice_in_dim(stacked, parity * half_width, half_width, 2)
    received = partner(outgoing.astype(jnp.bfloat16), "vocab", 0).astype(outgoing.dtype)
    grad_kv = jnp.swapaxes(kept_half + received, 1, 2).astype(jnp.bfloat16)
    grad_sinks = lax.psum(sink_grad, "seq")
    return (grad_queries, grad_kv, grad_sinks, hidden_grad)


def solution(mesh):
    in_specs = (
        P("seq", "vocab"),
        P("seq", None),
        P("seq", None),
        P("vocab"),
        P("seq"),
        P("seq", "vocab"),
        P("vocab", None),
        P("seq", None),
        P("seq"),
        P("seq"),
        P("seq"),
        P("seq"),
        P(("seq", "vocab"), None),
        P(("seq", "vocab"), None),
    )
    out_specs = (P("seq", "vocab"), P(None, "vocab", "seq"), P("vocab"), P("seq", None))
    return jax.shard_map(shards, mesh=mesh, in_specs=in_specs, out_specs=out_specs, check_vma=False)
```

```python
import jax
import jax.numpy as jnp
from jax import lax
from jax.experimental import pallas as pl
from jax.experimental.pallas import tpu as pltpu
from jax.sharding import PartitionSpec as P

HD = 64
WINDOW = 128
NX, NY, NZ, NC = 4, 8, 8, 2
D = 2880
QUARTER = 768
HALF = 2 * QUARTER
SLOTS = 8
PART = NY // 2

loss_scale = 64.0
kl_weight = 1.0
masked_score = -1e30
contract_last = (((1,), (1,)), ((), ()))
contract_first = (((0,), (0,)), ((), ()))
MESH = pl.DeviceIdType.MESH
f32 = jnp.float32
bf16 = jnp.bfloat16


def wrap(value, size):
    return lax.rem(value + size, size)


def device(x, y, z, c):
    return (y * NX + x, z * NC + c)


def unfold(block, row):
    return jnp.concatenate([block[row : row + 1], block[row + 3 : row + 4]], axis=1)


def fold(rows):
    half = rows[0].shape[1] // 2
    parts = [row[:, :half] for row in rows] + [row[:, half:] for row in rows]
    return jnp.concatenate(parts + [jnp.zeros((2, half), f32)], axis=0)


def merged(blocks):
    rows = [[unfold(block, k) for block in blocks] for k in range(3)]
    tops = [rows[0][0], rows[1][0]]
    for k in range(2):
        for row in rows[k][1:]:
            tops[k] = jnp.maximum(tops[k], row)
    mass, cross, frozen = 0.0, 0.0, 0.0
    for policy, other, mean in zip(*rows):
        share = jnp.exp(policy - tops[0])
        mass += share
        cross += share * mean
        frozen += jnp.exp(other - tops[1])
    return [tops[0] + jnp.log(mass), tops[1] + jnp.log(frozen), cross / mass]


def quarter_stop(q):
    return min(D, (q + 1) * QUARTER)


def named_scratch(heads, tokens, vocab_rows):
    dma = pltpu.SemaphoreType.DMA
    rows = NX * NY * SLOTS
    stat = (8, rows // 2)
    width = heads * HD
    tiles = tokens // WINDOW
    lanes = heads * WINDOW
    return {
        "policy": pltpu.VMEM((vocab_rows, D), bf16),
        "frozen": pltpu.VMEM((vocab_rows, D), bf16),
        "proj": pltpu.VMEM((width, D), bf16),
        "key_cols": pltpu.VMEM((tokens, 128), bf16),
        "value_cols": pltpu.VMEM((tokens, 128), bf16),
        "kv_own": pltpu.VMEM((tokens, 128), bf16),
        "kv_halo": pltpu.VMEM((WINDOW, 128), bf16),
        "doc_own": pltpu.VMEM((8, WINDOW), f32),
        "doc_halo": pltpu.VMEM((8, WINDOW), f32),
        "key_ext": pltpu.VMEM((tokens + WINDOW, HD), bf16),
        "value_ext": pltpu.VMEM((tokens + WINDOW, HD), bf16),
        "key_marks": pltpu.VMEM((tiles + 1, WINDOW, WINDOW), f32),
        "query_t": pltpu.VMEM((width, tokens), bf16),
        "upper_t": pltpu.VMEM((width, tokens), f32),
        "prob": pltpu.VMEM((tiles, WINDOW, lanes), f32),
        "prob_low": pltpu.VMEM((tiles, 2 * WINDOW, lanes), bf16),
        "share": pltpu.VMEM((tiles, 1, lanes), f32),
        "attended": pltpu.VMEM((tiles, HD, lanes), f32),
        "query_grad": pltpu.VMEM((width, tokens), f32),
        "key_grad": pltpu.VMEM((HD, tokens + WINDOW), f32),
        "value_grad": pltpu.VMEM((HD, tokens + WINDOW), f32),
        "kv_send": pltpu.VMEM((2, HD // 2, tokens), bf16),
        "kv_recv": pltpu.VMEM((2, HD // 2, tokens), bf16),
        "edge_send": pltpu.VMEM((2, 2, HD // 2, WINDOW), bf16),
        "edge_recv": pltpu.VMEM((2, 2, HD // 2, WINDOW), bf16),
        "sink_y": pltpu.VMEM((NY, 8, WINDOW), f32),
        "sink_x": pltpu.VMEM((NX, 8, WINDOW), f32),
        "wide": pltpu.VMEM((4, SLOTS, QUARTER), f32),
        "gathered": pltpu.VMEM((2, NX, 2, PART, 2 * SLOTS, QUARTER), bf16),
        "rows": pltpu.VMEM((4, rows, QUARTER), bf16),
        "meta_y": pltpu.VMEM((NY,) + stat, f32),
        "meta_x": pltpu.VMEM((NX,) + stat, f32),
        "stat_xc": pltpu.VMEM((NX * NC,) + stat, f32),
        "stat_y": pltpu.VMEM((NY,) + stat, f32),
        "stat_z": pltpu.VMEM((NZ,) + stat, f32),
        "total": pltpu.VMEM((2, NX, NY * SLOTS, HALF), f32),
        "outgoing": pltpu.VMEM((NX, NY * SLOTS, HALF), bf16),
        "from_core": pltpu.VMEM((NX, NY * SLOTS, HALF), bf16),
        "send_x": pltpu.VMEM((NX, 2, PART * SLOTS, HALF), bf16),
        "relay": pltpu.VMEM((2, PART * SLOTS, HALF), bf16),
        "from_x": pltpu.VMEM((4, PART * SLOTS, HALF), bf16),
        "send_y": pltpu.VMEM((NY, 2 * SLOTS, QUARTER), bf16),
        "from_y": pltpu.VMEM((NY, 2 * SLOTS, QUARTER), bf16),
        "from_z": pltpu.VMEM((NZ, 2 * SLOTS, QUARTER), bf16),
        "final": pltpu.VMEM((2, 2 * SLOTS, QUARTER), f32),
        "load_sem": dma((5,)),
        "gy": dma((2, NY)),
        "gx": dma((2, 6)),
        "gc": dma((2, 8)),
        "my": dma((2, NY)),
        "mx": dma((2, NX)),
        "sxc": dma((2, NX * NC)),
        "sy": dma((2, NY)),
        "sz": dma((2, NZ)),
        "rc": dma((2, NX)),
        "rx": dma((2, 6)),
        "ry": dma((2, NY)),
        "rz": dma((2, NZ)),
        "fc": dma((2, 1)),
        "halo": dma((2, 2)),
        "kv": dma((2, 3)),
        "ky": dma((2, NY)),
        "kx": dma((2, NX)),
    }


class Names:
    def __init__(self, names, refs):
        for name, ref in zip(names, refs):
            setattr(self, name, ref)


def kernel_of(names):
    def kernel(*refs):
        policy_step(Names(names, refs))

    return kernel


def policy_step(r):
    seq, vocab = lax.axis_index("seq"), lax.axis_index("vocab")
    x, y = lax.rem(seq, NX), lax.div(seq, NX)
    z, c = lax.div(vocab, NC), lax.rem(vocab, NC)
    n_seq = NX * NY
    vocab_rows = r.policy.shape[0]
    tokens = r.queries.shape[0]
    heads = r.queries.shape[1] // HD
    tiles = tokens // WINDOW
    scale = HD ** (-0.5)
    left, right, far = wrap(x - 1, NX), wrap(x + 1, NX), wrap(x + 2, NX)
    y_part, y_sub = lax.div(y, PART), lax.rem(y, PART)

    def load(src, dst, k):
        copy = pltpu.make_async_copy(src, dst, r.load_sem.at[k])
        copy.start()
        return copy

    column = pl.multiple_of(lax.div(z, 2) * 128, 128)
    load_keys = load(r.keys_hbm.at[:, pl.ds(column, 128)], r.key_cols, 0)
    load_values = load(r.values_hbm.at[:, pl.ds(column, 128)], r.value_cols, 1)
    load_policy = load(r.policy_hbm, r.policy, 2)
    load_frozen = load(r.frozen_hbm, r.frozen, 3)
    load_proj = load(r.proj_hbm, r.proj, 4)

    def along_x(d, other=0):
        return device(wrap(x + d, NX), y, z, 1 - c if other else c)

    def along_y(d):
        return device(x, wrap(y + d, NY), z, c)

    def along_z(d):
        return device(x, y, wrap(z + d, NZ), c)

    across = device(x, y, z, 1 - c)
    to_right, to_left = along_x(1), along_x(-1)
    xc_steps = [(d, o) for d in range(NX) for o in range(NC) if d or o]
    prev, after = wrap(seq - 1, n_seq), wrap(seq + 1, n_seq)

    def send(src, dst, sems, k, target):
        copy = pltpu.make_async_remote_copy(
            src_ref=src,
            dst_ref=dst,
            send_sem=sems.at[0, k],
            recv_sem=sems.at[1, k],
            device_id=target,
            device_id_type=MESH,
        )
        copy.start()
        return copy

    def wait_all(copies):
        for copy in copies:
            copy.wait()

    barrier = pltpu.get_barrier_semaphore()
    peers = [along_x(d, o) for d, o in xc_steps]
    peers += [along_y(d) for d in range(1, NY)] + [along_z(d) for d in range(1, NZ)]
    peers += [(owner, z * NC + o) for owner in (prev, after) for o in range(NC)]
    for peer in peers:
        pl.semaphore_signal(barrier, inc=1, device_id=peer, device_id_type=MESH)

    hidden = r.hidden[...].astype(f32)
    r.wide[3] = jnp.zeros((SLOTS, QUARTER), f32)
    for q in range(4):
        r.wide[q, :, : quarter_stop(q) - q * QUARTER] = hidden[:, q * QUARTER : quarter_stop(q)]
    r.gathered[c, x, y_part, y_sub] = jnp.concatenate(
        [r.wide[2 * c], r.wide[2 * c + 1]], axis=0
    ).astype(bf16)
    stat = r.meta_y.shape[1:]
    field = lax.broadcasted_iota(jnp.int32, stat, 0)
    lane = lax.broadcasted_iota(jnp.int32, stat, 1) + jnp.where(field < 3, 0, stat[1])
    field = jnp.where(field < 3, field, field - 3)
    meta = jnp.zeros(stat, f32)
    first_lane = (x * NY + y) * SLOTS
    for k in range(SLOTS):
        values = [r.advantages[k], r.sampled[k].astype(f32), r.live[k].astype(f32)]
        value = jnp.where(field == 0, values[0], jnp.where(field == 1, values[1], values[2]))
        meta = jnp.where(lane == first_lane + k, value, meta)
    r.meta_y[y] = meta
    pl.semaphore_wait(barrier, len(peers))

    own_slot = r.gathered.at[c, x, y_part, y_sub]
    copies_y = [send(own_slot, own_slot, r.gy, d, along_y(d)) for d in range(1, NY)]
    metas_y = [send(r.meta_y.at[y], r.meta_y.at[y], r.my, d, along_y(d)) for d in range(1, NY)]

    load_keys.wait()
    load_values.wait()

    def swapped(block):
        return jnp.concatenate([block[:, HD:], block[:, :HD]], axis=1)

    key_cols, value_cols = r.key_cols[...].astype(f32), r.value_cols[...].astype(f32)
    even = lax.rem(z, 2) == 0
    key_part = jnp.where(even, key_cols, swapped(key_cols))
    value_part = jnp.where(even, swapped(value_cols), value_cols)
    low_lanes = lax.broadcasted_iota(jnp.int32, key_cols.shape, 1) < HD
    r.kv_own[...] = jnp.where(low_lanes, key_part, value_part).astype(bf16)
    docs = r.docs[...].astype(f32)
    r.doc_own[...] = jnp.broadcast_to(docs[tiles - 1 :], r.doc_own.shape)
    after_me = (after, vocab)
    halos = [
        send(r.kv_own.at[pl.ds(tokens - WINDOW, WINDOW)], r.kv_halo, r.halo, 0, after_me),
        send(r.doc_own, r.doc_halo, r.halo, 1, after_me),
    ]
    r.query_t[...] = jnp.transpose(r.queries[...].astype(f32)).astype(bf16)
    r.upper_t[...] = jnp.transpose(r.upper[...].astype(f32))

    key_row = lax.broadcasted_iota(jnp.int32, (WINDOW, WINDOW), 0)
    query_col = lax.broadcasted_iota(jnp.int32, (WINDOW, WINDOW), 1)
    earlier = key_row > query_col

    def per_head(block):
        return jnp.concatenate([block] * heads, axis=1)

    def by_head(ref, t):
        lanes = slice(t * WINDOW, (t + 1) * WINDOW)
        return jnp.concatenate([ref[h * HD : (h + 1) * HD, lanes] for h in range(heads)], axis=1)

    earlier_wide = per_head(earlier.astype(f32)) > 0.5
    sink_row = jnp.concatenate([jnp.full((1, WINDOW), r.sinks[h]) for h in range(heads)], axis=1)

    def both_blocks(block):
        return jnp.concatenate(
            [jnp.where(earlier_wide, block, 0.0), jnp.where(earlier_wide, 0.0, block)], axis=0
        ).astype(bf16)

    def one_block(strip):
        return jnp.where(earlier_wide, strip[:WINDOW], strip[WINDOW:])

    def attention_setup():
        wait_all(halos)
        kv_halo = r.kv_halo[...].astype(f32)
        kv_own = r.kv_own[...].astype(f32)
        r.key_ext[:WINDOW] = kv_halo[:, :HD].astype(bf16)
        r.key_ext[WINDOW:] = kv_own[:, :HD].astype(bf16)
        r.value_ext[:WINDOW] = kv_halo[:, HD:].astype(bf16)
        r.value_ext[WINDOW:] = kv_own[:, HD:].astype(bf16)
        halo_docs = jnp.where(seq == 0, -1.0, r.doc_halo[0:1])
        for t in range(tiles + 1):
            row = halo_docs if t == 0 else docs[t - 1 : t]
            r.key_marks[t] = jnp.transpose(jnp.broadcast_to(row, (WINDOW, WINDOW)))

    def attention_forward(t):
        strip = slice(t * WINDOW, (t + 2) * WINDOW)
        marks = jnp.where(earlier, r.key_marks[t], r.key_marks[t + 1])
        allowed = per_head((marks == docs[t : t + 1]).astype(f32)) > 0.5
        scores = one_block(
            jnp.dot(r.key_ext[strip], by_head(r.query_t, t), preferred_element_type=f32)
        )
        masked = jnp.where(allowed, scores * scale, masked_score)
        row_top = jnp.maximum(jnp.max(masked, axis=0, keepdims=True), sink_row)
        exp_terms = jnp.where(allowed, jnp.exp(masked - row_top), 0.0)
        sink_term = jnp.exp(sink_row - row_top)
        inverse = 1.0 / (jnp.sum(exp_terms, axis=0, keepdims=True) + sink_term)
        prob = exp_terms * inverse
        low = both_blocks(prob)
        r.prob[t] = prob
        r.prob_low[t] = low
        r.share[t] = sink_term * inverse
        r.attended[t] = lax.dot_general(
            r.value_ext[strip], low, contract_first, preferred_element_type=f32
        )

    wait_all(copies_y)
    sent_x = [
        send(r.gathered.at[c, x, part], r.gathered.at[c, x, part], r.gx, k, target)
        for k, (part, target) in enumerate(
            [(0, to_right), (1, to_left), (1, to_right), (0, to_left)]
        )
    ]
    sent_c = []

    def cross_send(group, part):
        block = r.gathered.at[c, group, part]
        sent_c.append(send(block, block, r.gc, len(sent_c), across))

    def arrange(half, group, part):
        block = r.gathered[half, group, part].astype(f32).reshape(PART, 2, SLOTS, QUARTER)
        start = pl.multiple_of((group * 2 + part) * (PART * SLOTS), PART * SLOTS)
        for k in range(2):
            r.rows[2 * half + k, pl.ds(start, PART * SLOTS), :] = (
                block[:, k].reshape(PART * SLOTS, QUARTER).astype(bf16)
            )

    cross_send(x, 0)
    cross_send(x, 1)
    wait_all(metas_y)
    meta = r.meta_y[0]
    for k in range(1, NY):
        meta += r.meta_y[k]
    r.meta_x[x] = meta
    metas_x = [send(r.meta_x.at[x], r.meta_x.at[x], r.mx, d, along_x(d)) for d in range(1, NX)]
    attention_setup()
    sent_x[0].wait_recv()
    sent_x.append(
        send(r.gathered.at[c, left, 0], r.gathered.at[c, left, 0], r.gx, 4, to_right)
    )
    cross_send(left, 0)
    sent_x[1].wait_recv()
    sent_x.append(
        send(r.gathered.at[c, right, 1], r.gathered.at[c, right, 1], r.gx, 5, to_left)
    )
    cross_send(right, 1)
    arrange(c, x, 0)
    arrange(c, x, 1)
    attention_forward(0)
    sent_x[2].wait_recv()
    cross_send(left, 1)
    sent_x[3].wait_recv()
    cross_send(right, 0)
    arrange(c, left, 0)
    arrange(c, right, 1)
    for t in range(1, tiles):
        attention_forward(t)
    sent_x[4].wait_recv()
    cross_send(far, 0)
    sent_x[5].wait_recv()
    cross_send(far, 1)
    arrange(c, left, 1)
    arrange(c, right, 0)
    arrange(c, far, 0)
    arrange(c, far, 1)
    order = [(x, 0), (x, 1), (left, 0), (right, 1), (left, 1), (right, 0), (far, 0), (far, 1)]
    for copy, (group, part) in zip(sent_c, order):
        copy.wait_recv()
        arrange(1 - c, group, part)
    for copy in sent_x + sent_c:
        copy.wait_send()
    wait_all(metas_x)
    meta = r.meta_x[0]
    for k in range(1, NX):
        meta += r.meta_x[k]

    load_policy.wait()
    load_frozen.wait()

    def logits_of(head):
        result = 0.0
        for q in range(4):
            stop = quarter_stop(q)
            result += lax.dot_general(
                head[:, q * QUARTER : stop],
                r.rows[q, :, : stop - q * QUARTER],
                contract_last,
                preferred_element_type=f32,
            )
        return result

    policy_logits = logits_of(r.policy)
    frozen_logits = logits_of(r.frozen)
    policy_peak = jnp.max(policy_logits, axis=0, keepdims=True)
    frozen_peak = jnp.max(frozen_logits, axis=0, keepdims=True)
    logit_diff = policy_logits - frozen_logits
    policy_terms = jnp.exp(policy_logits - policy_peak)
    mass = jnp.sum(policy_terms, axis=0, keepdims=True)
    mean = jnp.sum(policy_terms * logit_diff, axis=0, keepdims=True) / mass
    frozen_mass = jnp.sum(jnp.exp(frozen_logits - frozen_peak), axis=0, keepdims=True)
    stats = [policy_peak + jnp.log(mass), frozen_peak + jnp.log(frozen_mass), mean]

    r.stat_xc[0] = fold(stats)
    wait_all(
        [
            send(r.stat_xc.at[0], r.stat_xc.at[k + 1], r.sxc, k, along_x(d, o))
            for k, (d, o) in enumerate(xc_steps)
        ]
    )
    r.stat_y[0] = fold(merged([r.stat_xc[k] for k in range(NX * NC)]))
    wait_all([send(r.stat_y.at[0], r.stat_y.at[d], r.sy, d, along_y(d)) for d in range(1, NY)])
    r.stat_z[0] = fold(merged([r.stat_y[k] for k in range(NY)]))
    wait_all([send(r.stat_z.at[0], r.stat_z.at[d], r.sz, d, along_z(d)) for d in range(1, NZ)])
    policy_lognorm, frozen_lognorm, cross_total = merged([r.stat_z[k] for k in range(NZ)])

    divergence = cross_total - policy_lognorm + frozen_lognorm
    policy_prob = jnp.exp(policy_logits - policy_lognorm)
    first_id = (seq * (NZ * NC) + vocab) * vocab_rows
    ids_here = (first_id + lax.broadcasted_iota(jnp.int32, policy_logits.shape, 0)).astype(f32)
    picked = (ids_here == unfold(meta, 1)).astype(f32)
    weight = loss_scale * unfold(meta, 2)
    log_ratio = policy_logits - policy_lognorm - (frozen_logits - frozen_lognorm) - divergence
    logit_grad = (
        weight * (-unfold(meta, 0) * (picked - policy_prob) + kl_weight * policy_prob * log_ratio)
    ).astype(bf16)

    group_rows = NY * SLOTS
    r.total[1, :, :, QUARTER:] = jnp.zeros((NX, group_rows, QUARTER), f32)
    for q in range(4):
        stop = quarter_stop(q)
        half, low = q // 2, (q % 2) * QUARTER
        r.total[half, :, :, low : low + stop - q * QUARTER] = lax.dot_general(
            logit_grad, r.policy[:, q * QUARTER : stop], contract_first, preferred_element_type=f32
        ).reshape(NX, group_rows, stop - q * QUARTER)
    cores = []
    for k, group in enumerate([far, right, left, x]):
        r.outgoing[group] = r.total[1 - c, group].astype(bf16)
        cores.append(send(r.outgoing.at[group], r.from_core.at[group], r.rc, k, across))
    part_rows = PART * SLOTS
    low_part, high_part = slice(0, part_rows), slice(part_rows, 2 * part_rows)

    def chip_sum(k, group):
        cores[k].wait_recv()
        return r.total[c, group] + r.from_core[group].astype(f32)

    both = chip_sum(0, far)
    r.send_x[far, 0] = both[low_part].astype(bf16)
    r.send_x[far, 1] = both[high_part].astype(bf16)
    reduced = [
        send(r.send_x.at[far, 0], r.relay.at[0], r.rx, 0, to_right),
        send(r.send_x.at[far, 1], r.relay.at[1], r.rx, 1, to_left),
    ]
    for_right = chip_sum(1, right)
    r.send_x[right, 1] = for_right[high_part].astype(bf16)
    reduced.append(send(r.send_x.at[right, 1], r.from_x.at[0], r.rx, 2, to_right))
    r.total[c, right, low_part] = for_right[low_part]
    for_left = chip_sum(2, left)
    r.send_x[left, 0] = for_left[low_part].astype(bf16)
    reduced.append(send(r.send_x.at[left, 0], r.from_x.at[1], r.rx, 3, to_left))
    r.total[c, left, high_part] = for_left[high_part]
    reduced[0].wait_recv()
    r.send_x[right, 0] = (r.total[c, right, low_part] + r.relay[0].astype(f32)).astype(bf16)
    reduced.append(send(r.send_x.at[right, 0], r.from_x.at[2], r.rx, 4, to_right))
    reduced[1].wait_recv()
    r.send_x[left, 1] = (r.total[c, left, high_part] + r.relay[1].astype(f32)).astype(bf16)
    reduced.append(send(r.send_x.at[left, 1], r.from_x.at[3], r.rx, 5, to_left))
    r.total[c, x] = chip_sum(3, x)
    for copy in reduced[2:]:
        copy.wait_recv()
    pairs = [(low_part, 1, 2), (high_part, 0, 3)]
    for part, (rows, first, second) in enumerate(pairs):
        mine = r.total[c, x, rows] + r.from_x[first].astype(f32) + r.from_x[second].astype(f32)
        mine = mine.reshape(PART, SLOTS, HALF)
        packed = jnp.concatenate([mine[:, :, :QUARTER], mine[:, :, QUARTER:]], axis=1)
        r.send_y[part * PART : (part + 1) * PART] = packed.astype(bf16)
    copies = [
        send(r.send_y.at[wrap(y + d, NY)], r.from_y.at[d], r.ry, d, along_y(d))
        for d in range(1, NY)
    ]
    for copy in cores + reduced:
        copy.wait_send()
    wait_all(copies)
    summed = r.send_y[y].astype(f32)
    for k in range(1, NY):
        summed += r.from_y[k].astype(f32)
    r.from_z[z] = summed.astype(bf16)
    wait_all([send(r.from_z.at[z], r.from_z.at[z], r.rz, d, along_z(d)) for d in range(1, NZ)])
    summed = r.from_z[0].astype(f32)
    for k in range(1, NZ):
        summed += r.from_z[k].astype(f32)
    r.final[c] = summed
    copy = send(r.final.at[c], r.final.at[c], r.fc, 0, across)
    load_proj.wait()
    copy.wait()

    slot_grad = 0.0
    for q in range(4):
        stop = quarter_stop(q)
        part = r.final[q // 2, (q % 2) * SLOTS : (q % 2 + 1) * SLOTS, :][:, : stop - q * QUARTER]
        r.hidden_grad[:, q * QUARTER : stop] = part
        slot_grad += lax.dot_general(
            r.proj[:, q * QUARTER : stop],
            part.astype(bf16),
            contract_last,
            preferred_element_type=f32,
        )
    slot_row = lax.broadcasted_iota(jnp.int32, (SLOTS, tokens), 0)
    token = lax.broadcasted_iota(jnp.int32, (SLOTS, tokens), 1)
    landing = jnp.zeros((SLOTS, tokens), f32)
    for k in range(SLOTS):
        landing = jnp.where((slot_row == k) & (token == r.slot_pos[k]), 1.0, landing)
    added = jnp.dot(slot_grad, landing, preferred_element_type=f32)
    r.upper_t[...] = (r.upper_t[...] + added).astype(bf16).astype(f32)

    deltas = []
    sink_total = 0.0
    for t in range(tiles):
        delta = jnp.sum(by_head(r.upper_t, t) * r.attended[t], axis=0, keepdims=True)
        deltas.append(delta)
        sink_total += r.share[t] * delta
    sink_rows = [-sink_total[:, h * WINDOW : (h + 1) * WINDOW] for h in range(heads)]
    sink_rows.append(jnp.zeros((8 - heads, WINDOW), f32))
    r.sink_y[y] = jnp.concatenate(sink_rows, axis=0)
    sinks_y = [send(r.sink_y.at[y], r.sink_y.at[y], r.ky, d, along_y(d)) for d in range(1, NY)]

    r.key_grad[...] = jnp.zeros(r.key_grad.shape, f32)
    r.value_grad[...] = jnp.zeros(r.value_grad.shape, f32)
    for t in range(tiles):
        strip = slice(t * WINDOW, (t + 2) * WINDOW)
        grads = by_head(r.upper_t, t).astype(bf16)
        dprob = one_block(jnp.dot(r.value_ext[strip], grads, preferred_element_type=f32))
        dscore = both_blocks(r.prob[t] * (dprob - deltas[t]))
        r.key_grad[:, strip] += lax.dot_general(
            by_head(r.query_t, t), dscore, contract_last, preferred_element_type=f32
        )
        r.value_grad[:, strip] += lax.dot_general(
            grads, r.prob_low[t], contract_last, preferred_element_type=f32
        )
        query_grad = scale * lax.dot_general(
            r.key_ext[strip], dscore, contract_first, preferred_element_type=f32
        )
        for h in range(heads):
            r.query_grad[h * HD : (h + 1) * HD, t * WINDOW : (t + 1) * WINDOW] = query_grad[
                :, h * WINDOW : (h + 1) * WINDOW
            ]
    half_width = HD // 2
    mine_rows = pl.ds(pl.multiple_of(c * half_width, half_width), half_width)
    other_rows = pl.ds(pl.multiple_of((1 - c) * half_width, half_width), half_width)
    both_grads = [(r.key_grad, scale), (r.value_grad, 1.0)]
    for k, (grad, factor) in enumerate(both_grads):
        r.kv_send[k] = (grad[other_rows, WINDOW:] * factor).astype(bf16)
        r.edge_send[0, k] = (grad[mine_rows, :WINDOW] * factor).astype(bf16)
        r.edge_send[1, k] = (grad[other_rows, :WINDOW] * factor).astype(bf16)
    kv_copies = [
        send(r.edge_send.at[0], r.edge_recv.at[0], r.kv, 0, (prev, vocab)),
        send(r.edge_send.at[1], r.edge_recv.at[1], r.kv, 1, (prev, z * NC + 1 - c)),
        send(r.kv_send, r.kv_recv, r.kv, 2, across),
    ]
    wait_all(sinks_y)
    sink_sum = r.sink_y[0]
    for k in range(1, NY):
        sink_sum += r.sink_y[k]
    r.sink_x[x] = sink_sum
    sinks_x = [send(r.sink_x.at[x], r.sink_x.at[x], r.kx, d, along_x(d)) for d in range(1, NX)]
    r.grad_queries[...] = jnp.transpose(r.query_grad[...]).astype(bf16)
    wait_all(kv_copies)
    for k, (grad, factor) in enumerate(both_grads):
        own = grad[mine_rows, WINDOW:] * factor + r.kv_recv[k].astype(f32)
        edge = r.edge_recv[0, k].astype(f32) + r.edge_recv[1, k].astype(f32)
        r.grad_kv[k] = jnp.concatenate(
            [own[:, : tokens - WINDOW], own[:, tokens - WINDOW :] + edge], axis=1
        ).astype(bf16)
    wait_all(sinks_x)
    sink_sum = r.sink_x[0]
    for k in range(1, NX):
        sink_sum += r.sink_x[k]
    r.grad_sinks[...] = jnp.broadcast_to(jnp.sum(sink_sum, axis=1, keepdims=True), (8, WINDOW))


def shards(
    queries,
    keys,
    values,
    sinks,
    doc_ids,
    upper_grad,
    out_proj,
    final_hidden,
    advantages,
    slot_pos,
    slot_live,
    sampled_ids,
    policy_head,
    reference_head,
):
    vmem = pl.BlockSpec(memory_space=pltpu.VMEM)
    smem = pl.BlockSpec(memory_space=pltpu.SMEM)
    hbm = pl.BlockSpec(memory_space=pl.ANY)
    heads = sinks.shape[0]
    tokens = queries.shape[0]
    operands = [
        ("hidden", final_hidden, vmem),
        ("advantages", advantages.astype(f32), smem),
        ("sampled", sampled_ids, smem),
        ("live", slot_live, smem),
        ("slot_pos", slot_pos, smem),
        ("sinks", sinks, smem),
        ("queries", queries, vmem),
        ("upper", upper_grad, vmem),
        ("docs", doc_ids.reshape(tokens // WINDOW, WINDOW), vmem),
        ("keys_hbm", keys, hbm),
        ("values_hbm", values, hbm),
        ("proj_hbm", out_proj, hbm),
        ("policy_hbm", policy_head, hbm),
        ("frozen_hbm", reference_head, hbm),
    ]
    results = [
        ("grad_queries", jax.ShapeDtypeStruct(queries.shape, bf16)),
        ("grad_kv", jax.ShapeDtypeStruct((2, HD // 2, tokens), bf16)),
        ("grad_sinks", jax.ShapeDtypeStruct((8, WINDOW), f32)),
        ("hidden_grad", jax.ShapeDtypeStruct(final_hidden.shape, f32)),
    ]
    scratch = named_scratch(heads, tokens, policy_head.shape[0])
    names = [name for name, _, _ in operands] + [name for name, _ in results] + list(scratch)
    grad_queries, grad_kv, grad_sinks, hidden_grad = pl.pallas_call(
        kernel_of(names),
        out_shape=[shape for _, shape in results],
        in_specs=[spec for _, _, spec in operands],
        out_specs=[vmem] * len(results),
        scratch_shapes=list(scratch.values()),
        compiler_params=pltpu.CompilerParams(
            collective_id=0, has_side_effects=True, vmem_limit_bytes=56 * 2**20
        ),
    )(*[value for _, value, _ in operands])
    return (grad_queries, grad_kv, grad_sinks[:heads, 0], hidden_grad)


def solution(mesh):
    in_specs = (
        P("seq", "vocab"),
        P("seq", None),
        P("seq", None),
        P("vocab"),
        P("seq"),
        P("seq", "vocab"),
        P("vocab", None),
        P("seq", None),
        P("seq"),
        P("seq"),
        P("seq"),
        P("seq"),
        P(("seq", "vocab"), None),
        P(("seq", "vocab"), None),
    )
    out_specs = (P("seq", "vocab"), P(None, "vocab", "seq"), P("vocab"), P("seq", None))
    return jax.shard_map(shards, mesh=mesh, in_specs=in_specs, out_specs=out_specs, check_vma=False)
```

```python
import jax
import jax.numpy as jnp
from jax import lax
from jax.experimental import pallas as pl
from jax.experimental.pallas import tpu as pltpu
from jax.sharding import PartitionSpec as P

HD = 64
WINDOW = 128
NX, NY, NZ, NC = 4, 8, 8, 2
D = 2880
QUARTER = 768
HALF = 2 * QUARTER
SLOTS = 8
PART = NY // 2
CHUNK = QUARTER // 2

loss_scale = 64.0
kl_weight = 1.0
masked_score = -1e30
contract_last = (((1,), (1,)), ((), ()))
contract_first = (((0,), (0,)), ((), ()))
MESH = pl.DeviceIdType.MESH
f32 = jnp.float32
bf16 = jnp.bfloat16


def wrap(value, size):
    return lax.rem(value + size, size)


def device(x, y, z, c):
    return (y * NX + x, z * NC + c)


def unfold(block, row):
    return jnp.concatenate([block[row : row + 1], block[row + 3 : row + 4]], axis=1)


def fold(rows):
    half = rows[0].shape[1] // 2
    parts = [row[:, :half] for row in rows] + [row[:, half:] for row in rows]
    return jnp.concatenate(parts + [jnp.zeros((2, half), f32)], axis=0)


def merged(blocks):
    rows = [[unfold(block, k) for block in blocks] for k in range(3)]
    tops = [rows[0][0], rows[1][0]]
    for k in range(2):
        for row in rows[k][1:]:
            tops[k] = jnp.maximum(tops[k], row)
    mass, cross, frozen = 0.0, 0.0, 0.0
    for policy, other, mean in zip(*rows):
        share = jnp.exp(policy - tops[0])
        mass += share
        cross += share * mean
        frozen += jnp.exp(other - tops[1])
    return [tops[0] + jnp.log(mass), tops[1] + jnp.log(frozen), cross / mass]


def far_first(size):
    return sorted(range(1, size), key=lambda d: (-min(d, size - d), d))


def quarter_stop(q):
    return min(D, (q + 1) * QUARTER)


def named_scratch(heads, tokens, vocab_rows):
    dma = pltpu.SemaphoreType.DMA
    rows = NX * NY * SLOTS
    stat = (8, rows // 2)
    width = heads * HD
    tiles = tokens // WINDOW
    lanes = heads * WINDOW
    return {
        "policy": pltpu.VMEM((vocab_rows, D), bf16),
        "frozen": pltpu.VMEM((vocab_rows, D), bf16),
        "proj": pltpu.VMEM((D, width), bf16),
        "key_cols": pltpu.VMEM((tokens, 128), bf16),
        "value_cols": pltpu.VMEM((tokens, 128), bf16),
        "kv_own": pltpu.VMEM((tokens, 128), bf16),
        "kv_halo": pltpu.VMEM((WINDOW, 128), bf16),
        "doc_own": pltpu.VMEM((8, WINDOW), f32),
        "doc_halo": pltpu.VMEM((8, WINDOW), f32),
        "key_ext": pltpu.VMEM((tokens + WINDOW, HD), bf16),
        "value_ext": pltpu.VMEM((tokens + WINDOW, HD), bf16),
        "key_marks": pltpu.VMEM((tiles + 1, WINDOW, WINDOW), f32),
        "query_t": pltpu.VMEM((width, tokens), bf16),
        "upper_t": pltpu.VMEM((width, tokens), f32),
        "prob": pltpu.VMEM((tiles, WINDOW, lanes), f32),
        "prob_low": pltpu.VMEM((tiles, 2 * WINDOW, lanes), bf16),
        "share": pltpu.VMEM((tiles, 1, lanes), f32),
        "attended": pltpu.VMEM((tiles, HD, lanes), f32),
        "query_grad": pltpu.VMEM((width, tokens), f32),
        "key_grad": pltpu.VMEM((HD, tokens + WINDOW), f32),
        "value_grad": pltpu.VMEM((HD, tokens + WINDOW), f32),
        "kv_send": pltpu.VMEM((2, HD // 2, tokens), bf16),
        "kv_recv": pltpu.VMEM((2, HD // 2, tokens), bf16),
        "edge_send": pltpu.VMEM((2, 2, HD // 2, WINDOW), bf16),
        "edge_recv": pltpu.VMEM((2, 2, HD // 2, WINDOW), bf16),
        "sink_y": pltpu.VMEM((NY, 8, WINDOW), f32),
        "sink_x": pltpu.VMEM((NX, 8, WINDOW), f32),
        "wide": pltpu.VMEM((4, SLOTS, QUARTER), f32),
        "gathered": pltpu.VMEM((2, 2, NX, 2, PART, 2 * SLOTS, CHUNK), bf16),
        "rows": pltpu.VMEM((4, rows, QUARTER), bf16),
        "meta_y": pltpu.VMEM((NY,) + stat, f32),
        "meta_x": pltpu.VMEM((NX,) + stat, f32),
        "stat_xc": pltpu.VMEM((NX * NC,) + stat, f32),
        "stat_y": pltpu.VMEM((NY,) + stat, f32),
        "stat_z": pltpu.VMEM((NZ,) + stat, f32),
        "total": pltpu.VMEM((4, NX, NY * SLOTS, QUARTER), f32),
        "outgoing": pltpu.VMEM((2, NX, NY * SLOTS, QUARTER), bf16),
        "from_core": pltpu.VMEM((2, NX, NY * SLOTS, QUARTER), bf16),
        "send_x": pltpu.VMEM((2, NX, 2, PART * SLOTS, QUARTER), bf16),
        "relay": pltpu.VMEM((2, 2, PART * SLOTS, QUARTER), bf16),
        "from_x": pltpu.VMEM((2, 4, PART * SLOTS, QUARTER), bf16),
        "send_y": pltpu.VMEM((2, NY, 2 * SLOTS, CHUNK), bf16),
        "from_y": pltpu.VMEM((2, NY, 2 * SLOTS, CHUNK), bf16),
        "from_z": pltpu.VMEM((2, NZ, 2 * SLOTS, CHUNK), bf16),
        "final": pltpu.VMEM((4, 2 * SLOTS, CHUNK), f32),
        "queries": pltpu.VMEM((tokens, width), bf16),
        "upper": pltpu.VMEM((tokens, width), bf16),
        "dscore": pltpu.VMEM((tiles, 2 * WINDOW, lanes), bf16),
        "load_sem": dma((7,)),
        "gy": dma((2, 2 * NY)),
        "gx": dma((2, 12)),
        "gc": dma((2, 16)),
        "my": dma((2, NY)),
        "mx": dma((2, NX)),
        "sxc": dma((2, NX * NC)),
        "sy": dma((2, NY)),
        "sz": dma((2, NZ)),
        "rc": dma((2, 2 * NX)),
        "rx": dma((2, 12)),
        "ry": dma((2, 2 * NY)),
        "rz": dma((2, 2 * NZ)),
        "fc": dma((2, 2)),
        "halo": dma((2, 2)),
        "kv": dma((2, 3)),
        "ky": dma((2, NY)),
        "kx": dma((2, NX)),
    }


class Names:
    def __init__(self, names, refs):
        for name, ref in zip(names, refs):
            setattr(self, name, ref)


def kernel_of(names):
    def kernel(*refs):
        policy_step(Names(names, refs))

    return kernel


def policy_step(r):
    seq, vocab = lax.axis_index("seq"), lax.axis_index("vocab")
    x, y = lax.rem(seq, NX), lax.div(seq, NX)
    z, c = lax.div(vocab, NC), lax.rem(vocab, NC)
    n_seq = NX * NY
    vocab_rows = r.policy.shape[0]
    tokens = r.queries.shape[0]
    heads = r.queries.shape[1] // HD
    tiles = tokens // WINDOW
    scale = HD ** (-0.5)
    left, right, far = wrap(x - 1, NX), wrap(x + 1, NX), wrap(x + 2, NX)
    y_part, y_sub = lax.div(y, PART), lax.rem(y, PART)

    def load(src, dst, k):
        copy = pltpu.make_async_copy(src, dst, r.load_sem.at[k])
        copy.start()
        return copy

    column = pl.multiple_of(lax.div(z, 2) * 128, 128)
    load_keys = load(r.keys_hbm.at[:, pl.ds(column, 128)], r.key_cols, 0)
    load_values = load(r.values_hbm.at[:, pl.ds(column, 128)], r.value_cols, 1)
    load_policy = load(r.policy_hbm, r.policy, 2)
    load_frozen = load(r.frozen_hbm, r.frozen, 3)
    load_proj = load(r.proj_hbm, r.proj, 4)
    load_queries = load(r.queries_hbm, r.queries, 5)
    load_upper = load(r.upper_hbm, r.upper, 6)

    def along_x(d, other=0):
        return device(wrap(x + d, NX), y, z, 1 - c if other else c)

    def along_y(d):
        return device(x, wrap(y + d, NY), z, c)

    def along_z(d):
        return device(x, y, wrap(z + d, NZ), c)

    across = device(x, y, z, 1 - c)
    to_right, to_left = along_x(1), along_x(-1)
    xc_steps = [(d, o) for d in range(NX) for o in range(NC) if d or o]
    prev, after = wrap(seq - 1, n_seq), wrap(seq + 1, n_seq)

    def send(src, dst, sems, k, target):
        copy = pltpu.make_async_remote_copy(
            src_ref=src,
            dst_ref=dst,
            send_sem=sems.at[0, k],
            recv_sem=sems.at[1, k],
            device_id=target,
            device_id_type=MESH,
        )
        copy.start()
        return copy

    def wait_all(copies):
        for copy in copies:
            copy.wait()

    barrier = pltpu.get_barrier_semaphore()
    peers = [along_x(d, o) for d, o in xc_steps]
    peers += [along_y(d) for d in range(1, NY)] + [along_z(d) for d in range(1, NZ)]
    peers += [(owner, z * NC + o) for owner in (prev, after) for o in range(NC)]
    for peer in peers:
        pl.semaphore_signal(barrier, inc=1, device_id=peer, device_id_type=MESH)

    hidden = r.hidden[...].astype(f32)
    r.wide[3] = jnp.zeros((SLOTS, QUARTER), f32)
    for q in range(4):
        r.wide[q, :, : quarter_stop(q) - q * QUARTER] = hidden[:, q * QUARTER : quarter_stop(q)]
    packed = jnp.concatenate([r.wide[2 * c], r.wide[2 * c + 1]], axis=0).astype(bf16)
    for k in range(2):
        r.gathered[k, c, x, y_part, y_sub] = packed[:, k * CHUNK : (k + 1) * CHUNK]
    stat = r.meta_y.shape[1:]
    field = lax.broadcasted_iota(jnp.int32, stat, 0)
    lane = lax.broadcasted_iota(jnp.int32, stat, 1) + jnp.where(field < 3, 0, stat[1])
    field = jnp.where(field < 3, field, field - 3)
    meta = jnp.zeros(stat, f32)
    first_lane = (x * NY + y) * SLOTS
    for k in range(SLOTS):
        value = jnp.where(field == 1, r.sampled[k].astype(f32), r.live[k].astype(f32))
        meta = jnp.where(lane == first_lane + k, value, meta)
    advantages = jnp.concatenate([r.advantages[...].astype(f32)] * (stat[1] // SLOTS), axis=1)
    mine_here = (lane >= first_lane) & (lane < first_lane + SLOTS) & (field == 0)
    meta = jnp.where(mine_here, jnp.broadcast_to(advantages, stat), meta)
    r.meta_y[y] = meta
    pl.semaphore_wait(barrier, len(peers))

    copies_y = [[], []]
    for k in range(2):
        own_slot = r.gathered.at[k, c, x, y_part, y_sub]
        for d in far_first(NY):
            copies_y[k].append(send(own_slot, own_slot, r.gy, k * NY + d, along_y(d)))
    metas_y = [send(r.meta_y.at[y], r.meta_y.at[y], r.my, d, along_y(d)) for d in range(1, NY)]

    load_keys.wait()
    load_values.wait()

    def swapped(block):
        return jnp.concatenate([block[:, HD:], block[:, :HD]], axis=1)

    key_cols, value_cols = r.key_cols[...].astype(f32), r.value_cols[...].astype(f32)
    even = lax.rem(z, 2) == 0
    key_part = jnp.where(even, key_cols, swapped(key_cols))
    value_part = jnp.where(even, swapped(value_cols), value_cols)
    low_lanes = lax.broadcasted_iota(jnp.int32, key_cols.shape, 1) < HD
    r.kv_own[...] = jnp.where(low_lanes, key_part, value_part).astype(bf16)
    docs = r.docs[...].astype(f32)
    r.doc_own[...] = jnp.broadcast_to(docs[tiles - 1 :], r.doc_own.shape)
    after_me = (after, vocab)
    halos = [
        send(r.kv_own.at[pl.ds(tokens - WINDOW, WINDOW)], r.kv_halo, r.halo, 0, after_me),
        send(r.doc_own, r.doc_halo, r.halo, 1, after_me),
    ]
    load_queries.wait()
    load_upper.wait()
    r.query_t[...] = jnp.transpose(r.queries[...].astype(f32)).astype(bf16)
    r.upper_t[...] = jnp.transpose(r.upper[...].astype(f32))

    key_row = lax.broadcasted_iota(jnp.int32, (WINDOW, WINDOW), 0)
    query_col = lax.broadcasted_iota(jnp.int32, (WINDOW, WINDOW), 1)
    earlier = key_row > query_col

    def per_head(block):
        return jnp.concatenate([block] * heads, axis=1)

    def by_head(ref, t):
        lanes = slice(t * WINDOW, (t + 1) * WINDOW)
        return jnp.concatenate([ref[h * HD : (h + 1) * HD, lanes] for h in range(heads)], axis=1)

    earlier_wide = per_head(earlier.astype(f32)) > 0.5
    sink_row = jnp.concatenate([jnp.full((1, WINDOW), r.sinks[h]) for h in range(heads)], axis=1)

    def both_blocks(block):
        return jnp.concatenate(
            [jnp.where(earlier_wide, block, 0.0), jnp.where(earlier_wide, 0.0, block)], axis=0
        ).astype(bf16)

    def one_block(strip):
        return jnp.where(earlier_wide, strip[:WINDOW], strip[WINDOW:])

    def attention_setup():
        wait_all(halos)
        kv_halo = r.kv_halo[...].astype(f32)
        kv_own = r.kv_own[...].astype(f32)
        r.key_ext[:WINDOW] = kv_halo[:, :HD].astype(bf16)
        r.key_ext[WINDOW:] = kv_own[:, :HD].astype(bf16)
        r.value_ext[:WINDOW] = kv_halo[:, HD:].astype(bf16)
        r.value_ext[WINDOW:] = kv_own[:, HD:].astype(bf16)
        halo_docs = jnp.where(seq == 0, -1.0, r.doc_halo[0:1])
        for t in range(tiles + 1):
            row = halo_docs if t == 0 else docs[t - 1 : t]
            r.key_marks[t] = jnp.transpose(jnp.broadcast_to(row, (WINDOW, WINDOW)))

    def attention_forward(t):
        strip = slice(t * WINDOW, (t + 2) * WINDOW)
        marks = jnp.where(earlier, r.key_marks[t], r.key_marks[t + 1])
        allowed = per_head((marks == docs[t : t + 1]).astype(f32)) > 0.5
        scores = one_block(
            jnp.dot(r.key_ext[strip], by_head(r.query_t, t), preferred_element_type=f32)
        )
        masked = jnp.where(allowed, scores * scale, masked_score)
        row_top = jnp.maximum(jnp.max(masked, axis=0, keepdims=True), sink_row)
        exp_terms = jnp.where(allowed, jnp.exp(masked - row_top), 0.0)
        sink_term = jnp.exp(sink_row - row_top)
        inverse = 1.0 / (jnp.sum(exp_terms, axis=0, keepdims=True) + sink_term)
        prob = exp_terms * inverse
        low = both_blocks(prob)
        r.prob[t] = prob
        r.prob_low[t] = low
        r.share[t] = sink_term * inverse
        r.attended[t] = lax.dot_general(
            r.value_ext[strip], low, contract_first, preferred_element_type=f32
        )

    sent_x, sent_c, order = [[], []], [[], []], [[], []]

    def along(k, group, part, target):
        block = r.gathered.at[k, c, group, part]
        sent_x[k].append(send(block, block, r.gx, 6 * k + len(sent_x[k]), target))

    def cross_send(k, group, part):
        block = r.gathered.at[k, c, group, part]
        sent_c[k].append(send(block, block, r.gc, 8 * k + len(sent_c[k]), across))
        order[k].append((group, part))

    def arrange(k, half, group, part):
        block = r.gathered[k, half, group, part].astype(f32).reshape(PART, 2, SLOTS, CHUNK)
        start = pl.multiple_of((group * 2 + part) * (PART * SLOTS), PART * SLOTS)
        for low in range(2):
            r.rows[
                2 * half + low, pl.ds(start, PART * SLOTS), k * CHUNK : (k + 1) * CHUNK
            ] = block[:, low].reshape(PART * SLOTS, CHUNK).astype(bf16)

    def spread(k):
        wait_all(copies_y[k])
        along(k, x, 0, to_right)
        along(k, x, 1, to_left)
        along(k, x, 1, to_right)
        along(k, x, 0, to_left)
        cross_send(k, x, 0)
        cross_send(k, x, 1)

    def relay_on(k):
        sent_x[k][0].wait_recv()
        along(k, left, 0, to_right)
        cross_send(k, left, 0)
        sent_x[k][1].wait_recv()
        along(k, right, 1, to_left)
        cross_send(k, right, 1)

    def direct_rest(k):
        sent_x[k][2].wait_recv()
        cross_send(k, left, 1)
        sent_x[k][3].wait_recv()
        cross_send(k, right, 0)

    def far_rest(k):
        sent_x[k][4].wait_recv()
        cross_send(k, far, 0)
        sent_x[k][5].wait_recv()
        cross_send(k, far, 1)

    def arrange_own(k):
        for group, part in order[k]:
            arrange(k, c, group, part)

    spread(0)
    wait_all(metas_y)
    meta = r.meta_y[0]
    for k in range(1, NY):
        meta += r.meta_y[k]
    r.meta_x[x] = meta
    metas_x = [send(r.meta_x.at[x], r.meta_x.at[x], r.mx, d, along_x(d)) for d in range(1, NX)]
    attention_setup()
    spread(1)
    relay_on(0)
    attention_forward(0)
    relay_on(1)
    direct_rest(0)
    attention_forward(1)
    direct_rest(1)
    far_rest(0)
    attention_forward(2)
    arrange_own(0)
    far_rest(1)
    for t in range(3, tiles):
        attention_forward(t)
    arrange_own(1)
    for k in range(2):
        for copy, (group, part) in zip(sent_c[k], order[k]):
            copy.wait_recv()
            arrange(k, 1 - c, group, part)
    for copy in sent_x[0] + sent_x[1] + sent_c[0] + sent_c[1]:
        copy.wait_send()
    wait_all(metas_x)
    meta = r.meta_x[0]
    for k in range(1, NX):
        meta += r.meta_x[k]

    load_policy.wait()
    load_frozen.wait()

    def logits_of(head):
        result = 0.0
        for q in range(4):
            stop = quarter_stop(q)
            result += lax.dot_general(
                head[:, q * QUARTER : stop],
                r.rows[q, :, : stop - q * QUARTER],
                contract_last,
                preferred_element_type=f32,
            )
        return result

    policy_logits = logits_of(r.policy)
    frozen_logits = logits_of(r.frozen)
    policy_peak = jnp.max(policy_logits, axis=0, keepdims=True)
    frozen_peak = jnp.max(frozen_logits, axis=0, keepdims=True)
    logit_diff = policy_logits - frozen_logits
    policy_terms = jnp.exp(policy_logits - policy_peak)
    mass = jnp.sum(policy_terms, axis=0, keepdims=True)
    mean = jnp.sum(policy_terms * logit_diff, axis=0, keepdims=True) / mass
    frozen_mass = jnp.sum(jnp.exp(frozen_logits - frozen_peak), axis=0, keepdims=True)
    stats = [policy_peak + jnp.log(mass), frozen_peak + jnp.log(frozen_mass), mean]

    r.stat_xc[0] = fold(stats)
    wait_all(
        [
            send(r.stat_xc.at[0], r.stat_xc.at[k + 1], r.sxc, k, along_x(d, o))
            for k, (d, o) in enumerate(xc_steps)
        ]
    )
    r.stat_y[0] = fold(merged([r.stat_xc[k] for k in range(NX * NC)]))
    wait_all([send(r.stat_y.at[0], r.stat_y.at[d], r.sy, d, along_y(d)) for d in range(1, NY)])
    r.stat_z[0] = fold(merged([r.stat_y[k] for k in range(NY)]))
    wait_all([send(r.stat_z.at[0], r.stat_z.at[d], r.sz, d, along_z(d)) for d in range(1, NZ)])
    policy_lognorm, frozen_lognorm, cross_total = merged([r.stat_z[k] for k in range(NZ)])

    divergence = cross_total - policy_lognorm + frozen_lognorm
    policy_prob = jnp.exp(policy_logits - policy_lognorm)
    first_id = (seq * (NZ * NC) + vocab) * vocab_rows
    ids_here = (first_id + lax.broadcasted_iota(jnp.int32, policy_logits.shape, 0)).astype(f32)
    picked = (ids_here == unfold(meta, 1)).astype(f32)
    weight = loss_scale * unfold(meta, 2)
    log_ratio = policy_logits - policy_lognorm - (frozen_logits - frozen_lognorm) - divergence
    logit_grad = (
        weight * (-unfold(meta, 0) * (picked - policy_prob) + kl_weight * policy_prob * log_ratio)
    ).astype(bf16)

    group_rows = NY * SLOTS
    r.total[3] = jnp.zeros((NX, group_rows, QUARTER), f32)
    for q in range(4):
        width = quarter_stop(q) - q * QUARTER
        r.total[q, :, :, :width] = lax.dot_general(
            logit_grad,
            r.policy[:, q * QUARTER : quarter_stop(q)],
            contract_first,
            preferred_element_type=f32,
        ).reshape(NX, group_rows, width)
    part_rows = PART * SLOTS
    low_part, high_part = slice(0, part_rows), slice(part_rows, 2 * part_rows)
    cores, reduced, copies_y, copies_z = [[], []], [[], []], [[], []], [[], []]
    for k in range(2):
        for i, group in enumerate([far, right, left, x]):
            r.outgoing[k, group] = r.total[2 * (1 - c) + k, group].astype(bf16)
            cores[k].append(
                send(r.outgoing.at[k, group], r.from_core.at[k, group], r.rc, NX * k + i, across)
            )

    def pass_on(k, src, dst, target):
        reduced[k].append(send(src, dst, r.rx, 6 * k + len(reduced[k]), target))

    def chip_sum(k, i, group):
        cores[k][i].wait_recv()
        return r.total[2 * c + k, group] + r.from_core[k, group].astype(f32)

    def start_far(k):
        both = chip_sum(k, 0, far)
        r.send_x[k, far, 0] = both[low_part].astype(bf16)
        r.send_x[k, far, 1] = both[high_part].astype(bf16)
        pass_on(k, r.send_x.at[k, far, 0], r.relay.at[k, 0], to_right)
        pass_on(k, r.send_x.at[k, far, 1], r.relay.at[k, 1], to_left)

    def start_direct(k):
        for_right = chip_sum(k, 1, right)
        r.send_x[k, right, 1] = for_right[high_part].astype(bf16)
        pass_on(k, r.send_x.at[k, right, 1], r.from_x.at[k, 0], to_right)
        r.total[2 * c + k, right, low_part] = for_right[low_part]
        for_left = chip_sum(k, 2, left)
        r.send_x[k, left, 0] = for_left[low_part].astype(bf16)
        pass_on(k, r.send_x.at[k, left, 0], r.from_x.at[k, 1], to_left)
        r.total[2 * c + k, left, high_part] = for_left[high_part]

    def start_summed(k):
        reduced[k][0].wait_recv()
        block = r.total[2 * c + k, right, low_part] + r.relay[k, 0].astype(f32)
        r.send_x[k, right, 0] = block.astype(bf16)
        pass_on(k, r.send_x.at[k, right, 0], r.from_x.at[k, 2], to_right)
        reduced[k][1].wait_recv()
        block = r.total[2 * c + k, left, high_part] + r.relay[k, 1].astype(f32)
        r.send_x[k, left, 1] = block.astype(bf16)
        pass_on(k, r.send_x.at[k, left, 1], r.from_x.at[k, 3], to_left)
        r.total[2 * c + k, x] = chip_sum(k, 3, x)

    def start_y(k):
        for copy in reduced[k][2:]:
            copy.wait_recv()
        for part, (rows, first, second) in enumerate([(low_part, 1, 2), (high_part, 0, 3)]):
            mine = r.total[2 * c + k, x, rows] + r.from_x[k, first].astype(f32)
            mine = (mine + r.from_x[k, second].astype(f32)).reshape(PART, SLOTS, QUARTER)
            packed = jnp.concatenate([mine[:, :, :CHUNK], mine[:, :, CHUNK:]], axis=1)
            r.send_y[k, part * PART : (part + 1) * PART] = packed.astype(bf16)
        for d in far_first(NY):
            copies_y[k].append(
                send(
                    r.send_y.at[k, wrap(y + d, NY)],
                    r.from_y.at[k, d],
                    r.ry,
                    NY * k + d,
                    along_y(d),
                )
            )

    def start_z(k):
        wait_all(copies_y[k])
        summed = r.send_y[k, y].astype(f32)
        for d in range(1, NY):
            summed += r.from_y[k, d].astype(f32)
        r.from_z[k, z] = summed.astype(bf16)
        block = r.from_z.at[k, z]
        for d in far_first(NZ):
            copies_z[k].append(send(block, block, r.rz, NZ * k + d, along_z(d)))

    def start_core(k):
        wait_all(copies_z[k])
        summed = r.from_z[k, 0].astype(f32)
        for d in range(1, NZ):
            summed += r.from_z[k, d].astype(f32)
        r.final[2 * c + k] = summed
        block = r.final.at[2 * c + k]
        return send(block, block, r.fc, k, across)

    start_far(0)
    start_direct(0)
    start_far(1)
    start_summed(0)
    start_direct(1)
    start_summed(1)
    start_y(0)
    start_y(1)
    start_z(0)
    start_z(1)
    slot_row = lax.broadcasted_iota(jnp.int32, (SLOTS, tokens), 0)
    token = lax.broadcasted_iota(jnp.int32, (SLOTS, tokens), 1)
    landing = jnp.zeros((SLOTS, tokens), f32)
    for k in range(SLOTS):
        landing = jnp.where((slot_row == k) & (token == r.slot_pos[k]), 1.0, landing)
    load_proj.wait()
    finals = [start_core(0), start_core(1)]
    slot_grad = 0.0
    for k in range(2):
        finals[k].wait()
        for q in (k, 2 + k):
            stop = quarter_stop(q)
            part = jnp.concatenate([r.final[q, :SLOTS, :], r.final[q, SLOTS:, :]], axis=1)
            part = part[:, : stop - q * QUARTER]
            r.hidden_grad[:, q * QUARTER : stop] = part
            slot_grad += jnp.dot(
                part.astype(bf16), r.proj[q * QUARTER : stop, :], preferred_element_type=f32
            )
    for copy in cores[0] + cores[1] + reduced[0] + reduced[1]:
        copy.wait_send()
    added = lax.dot_general(slot_grad, landing, contract_first, preferred_element_type=f32)
    r.upper_t[...] = (r.upper_t[...] + added).astype(bf16).astype(f32)

    deltas = []
    sink_total = 0.0
    for t in range(tiles):
        delta = jnp.sum(by_head(r.upper_t, t) * r.attended[t], axis=0, keepdims=True)
        deltas.append(delta)
        sink_total += r.share[t] * delta
    sink_rows = [-sink_total[:, h * WINDOW : (h + 1) * WINDOW] for h in range(heads)]
    sink_rows.append(jnp.zeros((8 - heads, WINDOW), f32))
    r.sink_y[y] = jnp.concatenate(sink_rows, axis=0)
    sinks_y = [send(r.sink_y.at[y], r.sink_y.at[y], r.ky, d, along_y(d)) for d in range(1, NY)]

    r.key_grad[...] = jnp.zeros(r.key_grad.shape, f32)
    r.value_grad[...] = jnp.zeros(r.value_grad.shape, f32)
    for t in range(tiles):
        strip = slice(t * WINDOW, (t + 2) * WINDOW)
        grads = by_head(r.upper_t, t).astype(bf16)
        dprob = one_block(jnp.dot(r.value_ext[strip], grads, preferred_element_type=f32))
        dscore = both_blocks(r.prob[t] * (dprob - deltas[t]))
        r.dscore[t] = dscore
        r.key_grad[:, strip] += lax.dot_general(
            by_head(r.query_t, t), dscore, contract_last, preferred_element_type=f32
        )
        r.value_grad[:, strip] += lax.dot_general(
            grads, r.prob_low[t], contract_last, preferred_element_type=f32
        )
    half_width = HD // 2
    mine_rows = pl.ds(pl.multiple_of(c * half_width, half_width), half_width)
    other_rows = pl.ds(pl.multiple_of((1 - c) * half_width, half_width), half_width)
    both_grads = [(r.key_grad, scale), (r.value_grad, 1.0)]
    for k, (grad, factor) in enumerate(both_grads):
        r.kv_send[k] = (grad[other_rows, WINDOW:] * factor).astype(bf16)
        r.edge_send[0, k] = (grad[mine_rows, :WINDOW] * factor).astype(bf16)
        r.edge_send[1, k] = (grad[other_rows, :WINDOW] * factor).astype(bf16)
    kv_copies = [
        send(r.edge_send.at[0], r.edge_recv.at[0], r.kv, 0, (prev, vocab)),
        send(r.edge_send.at[1], r.edge_recv.at[1], r.kv, 1, (prev, z * NC + 1 - c)),
        send(r.kv_send, r.kv_recv, r.kv, 2, across),
    ]
    wait_all(sinks_y)
    sink_sum = r.sink_y[0]
    for k in range(1, NY):
        sink_sum += r.sink_y[k]
    r.sink_x[x] = sink_sum
    sinks_x = [send(r.sink_x.at[x], r.sink_x.at[x], r.kx, d, along_x(d)) for d in range(1, NX)]
    for t in range(tiles):
        strip = slice(t * WINDOW, (t + 2) * WINDOW)
        query_grad = scale * lax.dot_general(
            r.key_ext[strip], r.dscore[t], contract_first, preferred_element_type=f32
        )
        for h in range(heads):
            r.query_grad[h * HD : (h + 1) * HD, t * WINDOW : (t + 1) * WINDOW] = query_grad[
                :, h * WINDOW : (h + 1) * WINDOW
            ]
    r.grad_queries[...] = jnp.transpose(r.query_grad[...]).astype(bf16)
    wait_all(kv_copies)
    for k, (grad, factor) in enumerate(both_grads):
        own = grad[mine_rows, WINDOW:] * factor + r.kv_recv[k].astype(f32)
        edge = r.edge_recv[0, k].astype(f32) + r.edge_recv[1, k].astype(f32)
        r.grad_kv[k] = jnp.concatenate(
            [own[:, : tokens - WINDOW], own[:, tokens - WINDOW :] + edge], axis=1
        ).astype(bf16)
    wait_all(sinks_x)
    sink_sum = r.sink_x[0]
    for k in range(1, NX):
        sink_sum += r.sink_x[k]
    for h in range(heads):
        r.grad_sinks[h] = jnp.sum(sink_sum[h : h + 1])


def hand_over(*refs):
    count = (len(refs) - 1) // 2
    sources, results, sems = refs[:count], refs[count : 2 * count], refs[-1]
    copies = []
    for k in range(count - 1):
        copies.append(pltpu.make_async_copy(sources[k], results[k], sems.at[k]))
        copies[k].start()
    for h in range(results[-1].shape[0]):
        results[-1][h] = sources[-1][h]
    for copy in copies:
        copy.wait()


def shards(
    queries,
    keys,
    values,
    sinks,
    doc_ids,
    upper_grad,
    out_proj,
    final_hidden,
    advantages,
    slot_pos,
    slot_live,
    sampled_ids,
    policy_head,
    reference_head,
):
    vmem = pl.BlockSpec(memory_space=pltpu.VMEM)
    smem = pl.BlockSpec(memory_space=pltpu.SMEM)
    hbm = pl.BlockSpec(memory_space=pl.ANY)
    heads = sinks.shape[0]
    tokens = queries.shape[0]
    operands = [
        ("hidden", final_hidden, vmem),
        ("advantages", advantages.reshape(1, SLOTS), vmem),
        ("sampled", sampled_ids, smem),
        ("live", slot_live, smem),
        ("slot_pos", slot_pos, smem),
        ("sinks", sinks, smem),
        ("queries_hbm", queries, hbm),
        ("upper_hbm", upper_grad, hbm),
        ("docs", doc_ids.reshape(tokens // WINDOW, WINDOW), vmem),
        ("keys_hbm", keys, hbm),
        ("values_hbm", values, hbm),
        ("proj_hbm", out_proj.T, hbm),
        ("policy_hbm", policy_head, hbm),
        ("frozen_hbm", reference_head, hbm),
    ]
    results = [
        ("grad_queries", jax.ShapeDtypeStruct(queries.shape, bf16), vmem),
        ("grad_kv", jax.ShapeDtypeStruct((2, HD // 2, tokens), bf16), vmem),
        ("hidden_grad", jax.ShapeDtypeStruct(final_hidden.shape, f32), vmem),
        ("grad_sinks", jax.ShapeDtypeStruct((heads,), f32), smem),
    ]
    scratch = named_scratch(heads, tokens, policy_head.shape[0])
    names = [name for name, _, _ in operands + results] + list(scratch)
    shapes = [shape for _, shape, _ in results]
    made = pl.pallas_call(
        kernel_of(names),
        out_shape=shapes,
        in_specs=[spec for _, _, spec in operands],
        out_specs=[spec for _, _, spec in results],
        scratch_shapes=list(scratch.values()),
        compiler_params=pltpu.CompilerParams(
            collective_id=0, has_side_effects=True, vmem_limit_bytes=56 * 2**20
        ),
    )(*[value for _, value, _ in operands])
    grad_queries, grad_kv, hidden_grad, grad_sinks = pl.pallas_call(
        hand_over,
        out_shape=shapes,
        in_specs=[hbm] * 3 + [smem],
        out_specs=[hbm] * 3 + [smem],
        scratch_shapes=[pltpu.SemaphoreType.DMA((3,))],
        compiler_params=pltpu.CompilerParams(vmem_limit_bytes=60 * 2**20),
    )(*made)
    return (grad_queries, grad_kv, grad_sinks, hidden_grad)


def solution(mesh):
    in_specs = (
        P("seq", "vocab"),
        P("seq", None),
        P("seq", None),
        P("vocab"),
        P("seq"),
        P("seq", "vocab"),
        P("vocab", None),
        P("seq", None),
        P("seq"),
        P("seq"),
        P("seq"),
        P("seq"),
        P(("seq", "vocab"), None),
        P(("seq", "vocab"), None),
    )
    out_specs = (P("seq", "vocab"), P(None, "vocab", "seq"), P("vocab"), P("seq", None))
    return jax.shard_map(shards, mesh=mesh, in_specs=in_specs, out_specs=out_specs, check_vma=False)
```

```python
import jax
import jax.numpy as jnp
from jax import lax
from jax.experimental import pallas as pl
from jax.experimental.pallas import tpu as pltpu
from jax.sharding import PartitionSpec as P

HD = 64
WINDOW = 128
NX, NY, NZ, NC = 4, 8, 8, 2
D = 2880
QUARTER = 768
HALF = 2 * QUARTER
SLOTS = 8
PART = NY // 2
CHUNK = QUARTER // 2

loss_scale = 64.0
kl_weight = 1.0
masked_score = -1e30
contract_last = (((1,), (1,)), ((), ()))
contract_first = (((0,), (0,)), ((), ()))
MESH = pl.DeviceIdType.MESH
f32 = jnp.float32
bf16 = jnp.bfloat16


def wrap(value, size):
    return lax.rem(value + size, size)


def device(x, y, z, c):
    return (y * NX + x, z * NC + c)


def unfold(block, row):
    return jnp.concatenate([block[row : row + 1], block[row + 3 : row + 4]], axis=1)


def fold(rows):
    half = rows[0].shape[1] // 2
    parts = [row[:, :half] for row in rows] + [row[:, half:] for row in rows]
    return jnp.concatenate(parts + [jnp.zeros((2, half), f32)], axis=0)


def merged(blocks):
    rows = [[unfold(block, k) for block in blocks] for k in range(3)]
    tops = [rows[0][0], rows[1][0]]
    for k in range(2):
        for row in rows[k][1:]:
            tops[k] = jnp.maximum(tops[k], row)
    mass, cross, frozen = 0.0, 0.0, 0.0
    for policy, other, mean in zip(*rows):
        share = jnp.exp(policy - tops[0])
        mass += share
        cross += share * mean
        frozen += jnp.exp(other - tops[1])
    return [tops[0] + jnp.log(mass), tops[1] + jnp.log(frozen), cross / mass]


def far_first(size):
    return sorted(range(1, size), key=lambda d: (-min(d, size - d), d))


def quarter_stop(q):
    return min(D, (q + 1) * QUARTER)


def named_scratch(heads, tokens, vocab_rows):
    dma = pltpu.SemaphoreType.DMA
    rows = NX * NY * SLOTS
    stat = (8, rows // 2)
    width = heads * HD
    tiles = tokens // WINDOW
    lanes = heads * WINDOW
    return {
        "policy": pltpu.VMEM((vocab_rows, D), bf16),
        "frozen": pltpu.VMEM((vocab_rows, D), bf16),
        "proj": pltpu.VMEM((D, width), bf16),
        "key_cols": pltpu.VMEM((tokens, 128), bf16),
        "value_cols": pltpu.VMEM((tokens, 128), bf16),
        "kv_own": pltpu.VMEM((tokens, 128), bf16),
        "kv_halo": pltpu.VMEM((WINDOW, 128), bf16),
        "doc_own": pltpu.VMEM((8, WINDOW), f32),
        "doc_halo": pltpu.VMEM((8, WINDOW), f32),
        "key_ext": pltpu.VMEM((tokens + WINDOW, HD), bf16),
        "value_ext": pltpu.VMEM((tokens + WINDOW, HD), bf16),
        "key_marks": pltpu.VMEM((tiles + 1, WINDOW, WINDOW), f32),
        "query_t": pltpu.VMEM((width, tokens), bf16),
        "upper_t": pltpu.VMEM((width, tokens), f32),
        "prob": pltpu.VMEM((tiles, WINDOW, lanes), f32),
        "prob_low": pltpu.VMEM((tiles, 2 * WINDOW, lanes), bf16),
        "share": pltpu.VMEM((tiles, 1, lanes), f32),
        "attended": pltpu.VMEM((tiles, HD, lanes), f32),
        "query_grad": pltpu.VMEM((width, tokens), f32),
        "key_grad": pltpu.VMEM((HD, tokens + WINDOW), f32),
        "value_grad": pltpu.VMEM((HD, tokens + WINDOW), f32),
        "kv_send": pltpu.VMEM((2, HD // 2, tokens), bf16),
        "kv_recv": pltpu.VMEM((2, HD // 2, tokens), bf16),
        "edge_send": pltpu.VMEM((2, 2, HD // 2, WINDOW), bf16),
        "edge_recv": pltpu.VMEM((2, 2, HD // 2, WINDOW), bf16),
        "sink_y": pltpu.VMEM((NY, 8, WINDOW), f32),
        "sink_x": pltpu.VMEM((NX, 8, WINDOW), f32),
        "wide": pltpu.VMEM((4, SLOTS, QUARTER), f32),
        "gathered": pltpu.VMEM((2, 2, NX, 2, PART, 2 * SLOTS, CHUNK), bf16),
        "rows": pltpu.VMEM((4, rows, QUARTER), bf16),
        "meta_y": pltpu.VMEM((NY,) + stat, f32),
        "meta_x": pltpu.VMEM((NX,) + stat, f32),
        "stat_xc": pltpu.VMEM((NX * NC,) + stat, f32),
        "stat_y": pltpu.VMEM((NY,) + stat, f32),
        "stat_z": pltpu.VMEM((NZ,) + stat, f32),
        "total": pltpu.VMEM((4, NX, NY * SLOTS, QUARTER), f32),
        "outgoing": pltpu.VMEM((2, NX, NY * SLOTS, QUARTER), bf16),
        "from_core": pltpu.VMEM((2, NX, NY * SLOTS, QUARTER), bf16),
        "send_x": pltpu.VMEM((2, NX, 2, PART * SLOTS, QUARTER), bf16),
        "relay": pltpu.VMEM((2, 2, PART * SLOTS, QUARTER), bf16),
        "from_x": pltpu.VMEM((2, 4, PART * SLOTS, QUARTER), bf16),
        "send_y": pltpu.VMEM((2, NY, 2 * SLOTS, CHUNK), bf16),
        "from_y": pltpu.VMEM((2, NY, 2 * SLOTS, CHUNK), bf16),
        "from_z": pltpu.VMEM((2, NZ, 2 * SLOTS, CHUNK), bf16),
        "final": pltpu.VMEM((4, 2 * SLOTS, CHUNK), f32),
        "queries": pltpu.VMEM((tokens, width), bf16),
        "upper": pltpu.VMEM((tokens, width), bf16),
        "slot_hot": pltpu.VMEM((tokens, WINDOW), f32),
        "slot_query": pltpu.VMEM((HD, WINDOW), bf16),
        "slot_upper": pltpu.VMEM((HD, WINDOW), f32),
        "slot_prob": pltpu.VMEM((tokens + WINDOW, WINDOW), f32),
        "slot_attended": pltpu.VMEM((HD, WINDOW), f32),
        "slot_share": pltpu.VMEM((1, WINDOW), f32),
        "sink_bulk": pltpu.VMEM((8, WINDOW), f32),
        "load_sem": dma((7,)),
        "gy": dma((2, 2 * NY)),
        "gx": dma((2, 12)),
        "gc": dma((2, 16)),
        "my": dma((2, NY)),
        "mx": dma((2, NX)),
        "sxc": dma((2, NX * NC)),
        "sy": dma((2, NY)),
        "sz": dma((2, NZ)),
        "rc": dma((2, 2 * NX)),
        "rx": dma((2, 12)),
        "ry": dma((2, 2 * NY)),
        "rz": dma((2, 2 * NZ)),
        "fc": dma((2, 2)),
        "halo": dma((2, 2)),
        "kv": dma((2, 3)),
        "ky": dma((2, NY)),
        "kx": dma((2, NX)),
    }


class Names:
    def __init__(self, names, refs):
        for name, ref in zip(names, refs):
            setattr(self, name, ref)


def kernel_of(names):
    def kernel(*refs):
        policy_step(Names(names, refs))

    return kernel


def policy_step(r):
    seq, vocab = lax.axis_index("seq"), lax.axis_index("vocab")
    x, y = lax.rem(seq, NX), lax.div(seq, NX)
    z, c = lax.div(vocab, NC), lax.rem(vocab, NC)
    n_seq = NX * NY
    vocab_rows = r.policy.shape[0]
    tokens = r.queries.shape[0]
    heads = r.queries.shape[1] // HD
    tiles = tokens // WINDOW
    scale = HD ** (-0.5)
    left, right, far = wrap(x - 1, NX), wrap(x + 1, NX), wrap(x + 2, NX)
    y_part, y_sub = lax.div(y, PART), lax.rem(y, PART)

    def load(src, dst, k):
        copy = pltpu.make_async_copy(src, dst, r.load_sem.at[k])
        copy.start()
        return copy

    column = pl.multiple_of(lax.div(z, 2) * 128, 128)
    load_keys = load(r.keys_hbm.at[:, pl.ds(column, 128)], r.key_cols, 0)
    load_values = load(r.values_hbm.at[:, pl.ds(column, 128)], r.value_cols, 1)
    load_policy = load(r.policy_hbm, r.policy, 2)
    load_frozen = load(r.frozen_hbm, r.frozen, 3)
    load_proj = load(r.proj_hbm, r.proj, 4)
    load_queries = load(r.queries_hbm, r.queries, 5)
    load_upper = load(r.upper_hbm, r.upper, 6)

    def along_x(d, other=0):
        return device(wrap(x + d, NX), y, z, 1 - c if other else c)

    def along_y(d):
        return device(x, wrap(y + d, NY), z, c)

    def along_z(d):
        return device(x, y, wrap(z + d, NZ), c)

    across = device(x, y, z, 1 - c)
    to_right, to_left = along_x(1), along_x(-1)
    xc_steps = [(d, o) for d in range(NX) for o in range(NC) if d or o]
    prev, after = wrap(seq - 1, n_seq), wrap(seq + 1, n_seq)

    def send(src, dst, sems, k, target):
        copy = pltpu.make_async_remote_copy(
            src_ref=src,
            dst_ref=dst,
            send_sem=sems.at[0, k],
            recv_sem=sems.at[1, k],
            device_id=target,
            device_id_type=MESH,
        )
        copy.start()
        return copy

    def wait_all(copies):
        for copy in copies:
            copy.wait()

    barrier = pltpu.get_barrier_semaphore()
    peers = [along_x(d, o) for d, o in xc_steps]
    peers += [along_y(d) for d in range(1, NY)] + [along_z(d) for d in range(1, NZ)]
    peers += [(owner, z * NC + o) for owner in (prev, after) for o in range(NC)]
    for peer in peers:
        pl.semaphore_signal(barrier, inc=1, device_id=peer, device_id_type=MESH)

    hidden = r.hidden[...].astype(f32)
    r.wide[3] = jnp.zeros((SLOTS, QUARTER), f32)
    for q in range(4):
        r.wide[q, :, : quarter_stop(q) - q * QUARTER] = hidden[:, q * QUARTER : quarter_stop(q)]
    packed = jnp.concatenate([r.wide[2 * c], r.wide[2 * c + 1]], axis=0).astype(bf16)
    for k in range(2):
        r.gathered[k, c, x, y_part, y_sub] = packed[:, k * CHUNK : (k + 1) * CHUNK]
    stat = r.meta_y.shape[1:]
    field = lax.broadcasted_iota(jnp.int32, stat, 0)
    lane = lax.broadcasted_iota(jnp.int32, stat, 1) + jnp.where(field < 3, 0, stat[1])
    field = jnp.where(field < 3, field, field - 3)
    meta = jnp.zeros(stat, f32)
    first_lane = (x * NY + y) * SLOTS
    for k in range(SLOTS):
        value = jnp.where(field == 1, r.sampled[k].astype(f32), r.live[k].astype(f32))
        meta = jnp.where(lane == first_lane + k, value, meta)
    advantages = jnp.concatenate([r.advantages[...].astype(f32)] * (stat[1] // SLOTS), axis=1)
    mine_here = (lane >= first_lane) & (lane < first_lane + SLOTS) & (field == 0)
    meta = jnp.where(mine_here, jnp.broadcast_to(advantages, stat), meta)
    r.meta_y[y] = meta
    pl.semaphore_wait(barrier, len(peers))

    copies_y = [[], []]
    for k in range(2):
        own_slot = r.gathered.at[k, c, x, y_part, y_sub]
        for d in far_first(NY):
            copies_y[k].append(send(own_slot, own_slot, r.gy, k * NY + d, along_y(d)))
    metas_y = [send(r.meta_y.at[y], r.meta_y.at[y], r.my, d, along_y(d)) for d in range(1, NY)]

    load_keys.wait()
    load_values.wait()

    def swapped(block):
        return jnp.concatenate([block[:, HD:], block[:, :HD]], axis=1)

    key_cols, value_cols = r.key_cols[...].astype(f32), r.value_cols[...].astype(f32)
    even = lax.rem(z, 2) == 0
    key_part = jnp.where(even, key_cols, swapped(key_cols))
    value_part = jnp.where(even, swapped(value_cols), value_cols)
    low_lanes = lax.broadcasted_iota(jnp.int32, key_cols.shape, 1) < HD
    r.kv_own[...] = jnp.where(low_lanes, key_part, value_part).astype(bf16)
    docs = r.docs[...].astype(f32)
    r.doc_own[...] = jnp.broadcast_to(docs[tiles - 1 :], r.doc_own.shape)
    after_me = (after, vocab)
    halos = [
        send(r.kv_own.at[pl.ds(tokens - WINDOW, WINDOW)], r.kv_halo, r.halo, 0, after_me),
        send(r.doc_own, r.doc_halo, r.halo, 1, after_me),
    ]
    load_queries.wait()
    load_upper.wait()
    r.query_t[...] = jnp.transpose(r.queries[...].astype(f32)).astype(bf16)
    r.upper_t[...] = jnp.transpose(r.upper[...].astype(f32))

    key_row = lax.broadcasted_iota(jnp.int32, (WINDOW, WINDOW), 0)
    query_col = lax.broadcasted_iota(jnp.int32, (WINDOW, WINDOW), 1)
    earlier = key_row > query_col
    query_row = lax.broadcasted_iota(jnp.int32, (1, WINDOW), 1)

    def per_head(block):
        return jnp.concatenate([block] * heads, axis=1)

    def by_head(ref, t):
        lanes = slice(t * WINDOW, (t + 1) * WINDOW)
        return jnp.concatenate([ref[h * HD : (h + 1) * HD, lanes] for h in range(heads)], axis=1)

    earlier_wide = per_head(earlier.astype(f32)) > 0.5
    sink_row = jnp.concatenate([jnp.full((1, WINDOW), r.sinks[h]) for h in range(heads)], axis=1)

    def both_blocks(block):
        return jnp.concatenate(
            [jnp.where(earlier_wide, block, 0.0), jnp.where(earlier_wide, 0.0, block)], axis=0
        ).astype(bf16)

    def one_block(strip):
        return jnp.where(earlier_wide, strip[:WINDOW], strip[WINDOW:])

    def attention_setup():
        wait_all(halos)
        kv_halo = r.kv_halo[...].astype(f32)
        kv_own = r.kv_own[...].astype(f32)
        r.key_ext[:WINDOW] = kv_halo[:, :HD].astype(bf16)
        r.key_ext[WINDOW:] = kv_own[:, :HD].astype(bf16)
        r.value_ext[:WINDOW] = kv_halo[:, HD:].astype(bf16)
        r.value_ext[WINDOW:] = kv_own[:, HD:].astype(bf16)
        halo_docs = jnp.where(seq == 0, -1.0, r.doc_halo[0:1])
        for t in range(tiles + 1):
            row = halo_docs if t == 0 else docs[t - 1 : t]
            r.key_marks[t] = jnp.transpose(jnp.broadcast_to(row, (WINDOW, WINDOW)))

    def attention_forward(t):
        strip = slice(t * WINDOW, (t + 2) * WINDOW)
        marks = jnp.where(earlier, r.key_marks[t], r.key_marks[t + 1])
        allowed = per_head((marks == docs[t : t + 1]).astype(f32)) > 0.5
        scores = one_block(
            jnp.dot(r.key_ext[strip], by_head(r.query_t, t), preferred_element_type=f32)
        )
        masked = jnp.where(allowed, scores * scale, masked_score)
        row_top = jnp.maximum(jnp.max(masked, axis=0, keepdims=True), sink_row)
        exp_terms = jnp.where(allowed, jnp.exp(masked - row_top), 0.0)
        sink_term = jnp.exp(sink_row - row_top)
        inverse = 1.0 / (jnp.sum(exp_terms, axis=0, keepdims=True) + sink_term)
        query_token = query_row + t * WINDOW
        keep = jnp.ones((1, WINDOW), f32)
        for k in range(SLOTS):
            keep = jnp.where(query_token == r.slot_pos[k], 0.0, keep)
        keep = per_head(keep)
        prob = exp_terms * (inverse * keep)
        low = both_blocks(prob)
        r.prob[t] = prob
        r.prob_low[t] = low
        r.share[t] = sink_term * inverse * keep
        r.attended[t] = lax.dot_general(
            r.value_ext[strip], low, contract_first, preferred_element_type=f32
        )

    def attention_backward(t):
        strip = slice(t * WINDOW, (t + 2) * WINDOW)
        grads_wide = by_head(r.upper_t, t)
        delta = jnp.sum(grads_wide * r.attended[t], axis=0, keepdims=True)
        sink_part = r.share[t] * delta
        for h in range(heads):
            r.sink_bulk[h : h + 1] -= sink_part[:, h * WINDOW : (h + 1) * WINDOW]
        grads = grads_wide.astype(bf16)
        dprob = one_block(jnp.dot(r.value_ext[strip], grads, preferred_element_type=f32))
        dscore = both_blocks(r.prob[t] * (dprob - delta))
        r.key_grad[:, strip] += lax.dot_general(
            by_head(r.query_t, t), dscore, contract_last, preferred_element_type=f32
        )
        r.value_grad[:, strip] += lax.dot_general(
            grads, r.prob_low[t], contract_last, preferred_element_type=f32
        )
        query_grad = scale * lax.dot_general(
            r.key_ext[strip], dscore, contract_first, preferred_element_type=f32
        )
        for h in range(heads):
            r.query_grad[h * HD : (h + 1) * HD, t * WINDOW : (t + 1) * WINDOW] = query_grad[
                :, h * WINDOW : (h + 1) * WINDOW
            ]

    lane_head = lax.div(query_row, SLOTS)

    def head_hot(h):
        return jnp.where(lane_head == h, r.slot_hot[...], 0.0).astype(bf16)

    def slot_setup():
        slot_of = lax.rem(query_row, SLOTS)
        pos_row = jnp.full((1, WINDOW), -1, jnp.int32)
        for k in range(SLOTS):
            pos_row = jnp.where(slot_of == k, r.slot_pos[k], pos_row)
        sink_slot = jnp.zeros((1, WINDOW), f32)
        for h in range(heads):
            sink_slot = jnp.where(lane_head == h, r.sinks[h], sink_slot)
        used = lane_head < heads
        token_row = lax.broadcasted_iota(jnp.int32, (tokens, WINDOW), 0)
        r.slot_hot[...] = jnp.where((token_row == pos_row) & used, 1.0, 0.0)
        doc_row = jnp.zeros((1, WINDOW), f32)
        for t in range(tiles):
            hot = r.slot_hot[t * WINDOW : (t + 1) * WINDOW]
            doc_row += jnp.sum(hot * r.key_marks[t + 1], axis=0, keepdims=True)
        query, upper = 0.0, 0.0
        for h in range(heads):
            hot, span = head_hot(h), slice(h * HD, (h + 1) * HD)
            query += jnp.dot(r.query_t[span], hot, preferred_element_type=f32)
            upper += jnp.dot(r.upper_t[span].astype(bf16), hot, preferred_element_type=f32)
        r.slot_query[...] = query.astype(bf16)
        r.slot_upper[...] = upper
        scores = jnp.dot(r.key_ext[...], r.slot_query[...], preferred_element_type=f32)
        key_at = lax.broadcasted_iota(jnp.int32, scores.shape, 0)
        behind = pos_row + WINDOW - key_at
        marks = r.key_marks[...].reshape(scores.shape)
        allowed = (behind >= 0) & (behind < WINDOW) & (marks == doc_row) & used
        masked = jnp.where(allowed, scores * scale, masked_score)
        row_top = jnp.maximum(jnp.max(masked, axis=0, keepdims=True), sink_slot)
        exp_terms = jnp.where(allowed, jnp.exp(masked - row_top), 0.0)
        sink_term = jnp.exp(sink_slot - row_top)
        inverse = 1.0 / (jnp.sum(exp_terms, axis=0, keepdims=True) + sink_term)
        prob = exp_terms * inverse
        r.slot_prob[...] = prob
        r.slot_share[...] = jnp.where(used, sink_term * inverse, 0.0)
        r.slot_attended[...] = lax.dot_general(
            r.value_ext[...], prob.astype(bf16), contract_first, preferred_element_type=f32
        )

    r.key_grad[...] = jnp.zeros(r.key_grad.shape, f32)
    r.value_grad[...] = jnp.zeros(r.value_grad.shape, f32)
    r.sink_bulk[...] = jnp.zeros(r.sink_bulk.shape, f32)
    sent_x, sent_c, order = [[], []], [[], []], [[], []]

    def along(k, group, part, target):
        block = r.gathered.at[k, c, group, part]
        sent_x[k].append(send(block, block, r.gx, 6 * k + len(sent_x[k]), target))

    def cross_send(k, group, part):
        block = r.gathered.at[k, c, group, part]
        sent_c[k].append(send(block, block, r.gc, 8 * k + len(sent_c[k]), across))
        order[k].append((group, part))

    def arrange(k, half, group, part):
        block = r.gathered[k, half, group, part].astype(f32).reshape(PART, 2, SLOTS, CHUNK)
        start = pl.multiple_of((group * 2 + part) * (PART * SLOTS), PART * SLOTS)
        for low in range(2):
            r.rows[
                2 * half + low, pl.ds(start, PART * SLOTS), k * CHUNK : (k + 1) * CHUNK
            ] = block[:, low].reshape(PART * SLOTS, CHUNK).astype(bf16)

    def spread(k):
        wait_all(copies_y[k])
        along(k, x, 0, to_right)
        along(k, x, 1, to_left)
        along(k, x, 1, to_right)
        along(k, x, 0, to_left)
        cross_send(k, x, 0)
        cross_send(k, x, 1)

    def relay_on(k):
        sent_x[k][0].wait_recv()
        along(k, left, 0, to_right)
        cross_send(k, left, 0)
        sent_x[k][1].wait_recv()
        along(k, right, 1, to_left)
        cross_send(k, right, 1)

    def direct_rest(k):
        sent_x[k][2].wait_recv()
        cross_send(k, left, 1)
        sent_x[k][3].wait_recv()
        cross_send(k, right, 0)

    def far_rest(k):
        sent_x[k][4].wait_recv()
        cross_send(k, far, 0)
        sent_x[k][5].wait_recv()
        cross_send(k, far, 1)

    def arrange_own(k):
        for group, part in order[k]:
            arrange(k, c, group, part)

    spread(0)
    wait_all(metas_y)
    meta = r.meta_y[0]
    for k in range(1, NY):
        meta += r.meta_y[k]
    r.meta_x[x] = meta
    metas_x = [send(r.meta_x.at[x], r.meta_x.at[x], r.mx, d, along_x(d)) for d in range(1, NX)]
    attention_setup()
    spread(1)
    relay_on(0)
    attention_forward(0)
    relay_on(1)
    direct_rest(0)
    attention_forward(1)
    direct_rest(1)
    far_rest(0)
    attention_forward(2)
    arrange_own(0)
    far_rest(1)
    for t in range(3, tiles):
        attention_forward(t)
    arrange_own(1)
    for k in range(2):
        for copy, (group, part) in zip(sent_c[k], order[k]):
            copy.wait_recv()
            arrange(k, 1 - c, group, part)
    for copy in sent_x[0] + sent_x[1] + sent_c[0] + sent_c[1]:
        copy.wait_send()
    wait_all(metas_x)
    meta = r.meta_x[0]
    for k in range(1, NX):
        meta += r.meta_x[k]

    load_policy.wait()
    load_frozen.wait()

    def logits_of(head):
        result = 0.0
        for q in range(4):
            stop = quarter_stop(q)
            result += lax.dot_general(
                head[:, q * QUARTER : stop],
                r.rows[q, :, : stop - q * QUARTER],
                contract_last,
                preferred_element_type=f32,
            )
        return result

    policy_logits = logits_of(r.policy)
    frozen_logits = logits_of(r.frozen)
    policy_peak = jnp.max(policy_logits, axis=0, keepdims=True)
    frozen_peak = jnp.max(frozen_logits, axis=0, keepdims=True)
    logit_diff = policy_logits - frozen_logits
    policy_terms = jnp.exp(policy_logits - policy_peak)
    mass = jnp.sum(policy_terms, axis=0, keepdims=True)
    mean = jnp.sum(policy_terms * logit_diff, axis=0, keepdims=True) / mass
    frozen_mass = jnp.sum(jnp.exp(frozen_logits - frozen_peak), axis=0, keepdims=True)
    stats = [policy_peak + jnp.log(mass), frozen_peak + jnp.log(frozen_mass), mean]

    r.stat_xc[0] = fold(stats)
    copies = [
        send(r.stat_xc.at[0], r.stat_xc.at[k + 1], r.sxc, k, along_x(d, o))
        for k, (d, o) in enumerate(xc_steps)
    ]
    attention_backward(0)
    wait_all(copies)
    r.stat_y[0] = fold(merged([r.stat_xc[k] for k in range(NX * NC)]))
    copies = [
        send(r.stat_y.at[0], r.stat_y.at[d], r.sy, d, along_y(d)) for d in far_first(NY)
    ]
    attention_backward(1)
    wait_all(copies)
    r.stat_z[0] = fold(merged([r.stat_y[k] for k in range(NY)]))
    copies = [
        send(r.stat_z.at[0], r.stat_z.at[d], r.sz, d, along_z(d)) for d in far_first(NZ)
    ]
    attention_backward(2)
    wait_all(copies)
    policy_lognorm, frozen_lognorm, cross_total = merged([r.stat_z[k] for k in range(NZ)])

    divergence = cross_total - policy_lognorm + frozen_lognorm
    policy_prob = jnp.exp(policy_logits - policy_lognorm)
    first_id = (seq * (NZ * NC) + vocab) * vocab_rows
    ids_here = (first_id + lax.broadcasted_iota(jnp.int32, policy_logits.shape, 0)).astype(f32)
    picked = (ids_here == unfold(meta, 1)).astype(f32)
    weight = loss_scale * unfold(meta, 2)
    log_ratio = policy_logits - policy_lognorm - (frozen_logits - frozen_lognorm) - divergence
    logit_grad = (
        weight * (-unfold(meta, 0) * (picked - policy_prob) + kl_weight * policy_prob * log_ratio)
    ).astype(bf16)

    group_rows = NY * SLOTS
    r.total[3] = jnp.zeros((NX, group_rows, QUARTER), f32)
    for q in range(4):
        width = quarter_stop(q) - q * QUARTER
        r.total[q, :, :, :width] = lax.dot_general(
            logit_grad,
            r.policy[:, q * QUARTER : quarter_stop(q)],
            contract_first,
            preferred_element_type=f32,
        ).reshape(NX, group_rows, width)
    part_rows = PART * SLOTS
    low_part, high_part = slice(0, part_rows), slice(part_rows, 2 * part_rows)
    cores, reduced, copies_y, copies_z = [[], []], [[], []], [[], []], [[], []]
    for k in range(2):
        for i, group in enumerate([far, right, left, x]):
            r.outgoing[k, group] = r.total[2 * (1 - c) + k, group].astype(bf16)
            cores[k].append(
                send(r.outgoing.at[k, group], r.from_core.at[k, group], r.rc, NX * k + i, across)
            )

    for t in range(3, tiles):
        attention_backward(t)

    def pass_on(k, src, dst, target):
        reduced[k].append(send(src, dst, r.rx, 6 * k + len(reduced[k]), target))

    def chip_sum(k, i, group):
        cores[k][i].wait_recv()
        return r.total[2 * c + k, group] + r.from_core[k, group].astype(f32)

    def start_far(k):
        both = chip_sum(k, 0, far)
        r.send_x[k, far, 0] = both[low_part].astype(bf16)
        r.send_x[k, far, 1] = both[high_part].astype(bf16)
        pass_on(k, r.send_x.at[k, far, 0], r.relay.at[k, 0], to_right)
        pass_on(k, r.send_x.at[k, far, 1], r.relay.at[k, 1], to_left)

    def start_direct(k):
        for_right = chip_sum(k, 1, right)
        r.send_x[k, right, 1] = for_right[high_part].astype(bf16)
        pass_on(k, r.send_x.at[k, right, 1], r.from_x.at[k, 0], to_right)
        r.total[2 * c + k, right, low_part] = for_right[low_part]
        for_left = chip_sum(k, 2, left)
        r.send_x[k, left, 0] = for_left[low_part].astype(bf16)
        pass_on(k, r.send_x.at[k, left, 0], r.from_x.at[k, 1], to_left)
        r.total[2 * c + k, left, high_part] = for_left[high_part]

    def start_summed(k):
        reduced[k][0].wait_recv()
        block = r.total[2 * c + k, right, low_part] + r.relay[k, 0].astype(f32)
        r.send_x[k, right, 0] = block.astype(bf16)
        pass_on(k, r.send_x.at[k, right, 0], r.from_x.at[k, 2], to_right)
        reduced[k][1].wait_recv()
        block = r.total[2 * c + k, left, high_part] + r.relay[k, 1].astype(f32)
        r.send_x[k, left, 1] = block.astype(bf16)
        pass_on(k, r.send_x.at[k, left, 1], r.from_x.at[k, 3], to_left)
        r.total[2 * c + k, x] = chip_sum(k, 3, x)

    def start_y(k):
        for copy in reduced[k][2:]:
            copy.wait_recv()
        for part, (rows, first, second) in enumerate([(low_part, 1, 2), (high_part, 0, 3)]):
            mine = r.total[2 * c + k, x, rows] + r.from_x[k, first].astype(f32)
            mine = (mine + r.from_x[k, second].astype(f32)).reshape(PART, SLOTS, QUARTER)
            packed = jnp.concatenate([mine[:, :, :CHUNK], mine[:, :, CHUNK:]], axis=1)
            r.send_y[k, part * PART : (part + 1) * PART] = packed.astype(bf16)
        for d in far_first(NY):
            copies_y[k].append(
                send(
                    r.send_y.at[k, wrap(y + d, NY)],
                    r.from_y.at[k, d],
                    r.ry,
                    NY * k + d,
                    along_y(d),
                )
            )

    def start_z(k):
        wait_all(copies_y[k])
        summed = r.send_y[k, y].astype(f32)
        for d in range(1, NY):
            summed += r.from_y[k, d].astype(f32)
        r.from_z[k, z] = summed.astype(bf16)
        block = r.from_z.at[k, z]
        for d in far_first(NZ):
            copies_z[k].append(send(block, block, r.rz, NZ * k + d, along_z(d)))

    def start_core(k):
        wait_all(copies_z[k])
        summed = r.from_z[k, 0].astype(f32)
        for d in range(1, NZ):
            summed += r.from_z[k, d].astype(f32)
        r.final[2 * c + k] = summed
        block = r.final.at[2 * c + k]
        return send(block, block, r.fc, k, across)

    start_far(0)
    start_direct(0)
    start_far(1)
    start_summed(0)
    start_direct(1)
    start_summed(1)
    start_y(0)
    start_y(1)
    slot_setup()
    start_z(0)
    start_z(1)
    load_proj.wait()
    finals = [start_core(0), start_core(1)]
    slot_grad = 0.0
    for k in range(2):
        finals[k].wait()
        for q in (k, 2 + k):
            stop = quarter_stop(q)
            part = jnp.concatenate([r.final[q, :SLOTS, :], r.final[q, SLOTS:, :]], axis=1)
            part = part[:, : stop - q * QUARTER]
            r.hidden_grad[:, q * QUARTER : stop] = part
            slot_grad += jnp.dot(
                part.astype(bf16), r.proj[q * QUARTER : stop, :], preferred_element_type=f32
            )
    for copy in cores[0] + cores[1] + reduced[0] + reduced[1]:
        copy.wait_send()
    slot_at = lax.broadcasted_iota(jnp.int32, (SLOTS, WINDOW), 0)
    spread_out = lax.rem(lax.broadcasted_iota(jnp.int32, (SLOTS, WINDOW), 1), SLOTS) == slot_at
    wide_grad = lax.dot_general(
        slot_grad,
        spread_out.astype(f32),
        contract_first,
        precision=lax.Precision.HIGHEST,
        preferred_element_type=f32,
    )
    slot_out = r.slot_upper[...]
    for h in range(heads):
        slot_out += jnp.where(lane_head == h, wide_grad[h * HD : (h + 1) * HD], 0.0)
    slot_low = slot_out.astype(bf16)
    slot_delta = jnp.sum(slot_low.astype(f32) * r.slot_attended[...], axis=0, keepdims=True)
    slot_sink = r.slot_share[...] * slot_delta
    sink_heads = lax.broadcasted_iota(jnp.int32, (8, WINDOW), 0) == lane_head
    r.sink_y[y] = r.sink_bulk[...] - jnp.where(sink_heads, slot_sink, 0.0)
    sinks_y = [
        send(r.sink_y.at[y], r.sink_y.at[y], r.ky, d, along_y(d)) for d in far_first(NY)
    ]
    slot_dprob = jnp.dot(r.value_ext[...], slot_low, preferred_element_type=f32)
    slot_dscore = (r.slot_prob[...] * (slot_dprob - slot_delta)).astype(bf16)
    r.key_grad[...] += lax.dot_general(
        r.slot_query[...], slot_dscore, contract_last, preferred_element_type=f32
    )
    r.value_grad[...] += lax.dot_general(
        slot_low, r.slot_prob[...].astype(bf16), contract_last, preferred_element_type=f32
    )
    half_width = HD // 2
    mine_rows = pl.ds(pl.multiple_of(c * half_width, half_width), half_width)
    other_rows = pl.ds(pl.multiple_of((1 - c) * half_width, half_width), half_width)
    both_grads = [(r.key_grad, scale), (r.value_grad, 1.0)]
    for k, (grad, factor) in enumerate(both_grads):
        r.kv_send[k] = (grad[other_rows, WINDOW:] * factor).astype(bf16)
        r.edge_send[0, k] = (grad[mine_rows, :WINDOW] * factor).astype(bf16)
        r.edge_send[1, k] = (grad[other_rows, :WINDOW] * factor).astype(bf16)
    kv_copies = [
        send(r.edge_send.at[0], r.edge_recv.at[0], r.kv, 0, (prev, vocab)),
        send(r.edge_send.at[1], r.edge_recv.at[1], r.kv, 1, (prev, z * NC + 1 - c)),
        send(r.kv_send, r.kv_recv, r.kv, 2, across),
    ]
    slot_query_grad = scale * lax.dot_general(
        r.key_ext[...], slot_dscore, contract_first, preferred_element_type=f32
    )
    slot_query_low = slot_query_grad.astype(bf16)
    for h in range(heads):
        r.query_grad[h * HD : (h + 1) * HD] += lax.dot_general(
            slot_query_low, head_hot(h), contract_last, preferred_element_type=f32
        )
    wait_all(sinks_y)
    sink_sum = r.sink_y[0]
    for k in range(1, NY):
        sink_sum += r.sink_y[k]
    r.sink_x[x] = sink_sum
    sinks_x = [send(r.sink_x.at[x], r.sink_x.at[x], r.kx, d, along_x(d)) for d in range(1, NX)]
    r.grad_queries[...] = jnp.transpose(r.query_grad[...]).astype(bf16)
    wait_all(kv_copies)
    for k, (grad, factor) in enumerate(both_grads):
        own = grad[mine_rows, WINDOW:] * factor + r.kv_recv[k].astype(f32)
        edge = r.edge_recv[0, k].astype(f32) + r.edge_recv[1, k].astype(f32)
        r.grad_kv[k] = jnp.concatenate(
            [own[:, : tokens - WINDOW], own[:, tokens - WINDOW :] + edge], axis=1
        ).astype(bf16)
    wait_all(sinks_x)
    sink_sum = r.sink_x[0]
    for k in range(1, NX):
        sink_sum += r.sink_x[k]
    for h in range(heads):
        r.grad_sinks[h] = jnp.sum(sink_sum[h : h + 1])


def hand_over(*refs):
    count = len(refs) // 2
    for source, result in zip(refs[: count - 1], refs[count:]):
        result[...] = source[...]
    for h in range(refs[-1].shape[0]):
        refs[-1][h] = refs[count - 1][h]


def shards(
    queries,
    keys,
    values,
    sinks,
    doc_ids,
    upper_grad,
    out_proj,
    final_hidden,
    advantages,
    slot_pos,
    slot_live,
    sampled_ids,
    policy_head,
    reference_head,
):
    vmem = pl.BlockSpec(memory_space=pltpu.VMEM)
    smem = pl.BlockSpec(memory_space=pltpu.SMEM)
    hbm = pl.BlockSpec(memory_space=pl.ANY)
    heads = sinks.shape[0]
    tokens = queries.shape[0]
    operands = [
        ("hidden", final_hidden, vmem),
        ("advantages", advantages.reshape(1, SLOTS), vmem),
        ("sampled", sampled_ids, smem),
        ("live", slot_live, smem),
        ("slot_pos", slot_pos, smem),
        ("sinks", sinks, smem),
        ("queries_hbm", queries, hbm),
        ("upper_hbm", upper_grad, hbm),
        ("docs", doc_ids.reshape(tokens // WINDOW, WINDOW), vmem),
        ("keys_hbm", keys, hbm),
        ("values_hbm", values, hbm),
        ("proj_hbm", out_proj.T, hbm),
        ("policy_hbm", policy_head, hbm),
        ("frozen_hbm", reference_head, hbm),
    ]
    results = [
        ("grad_queries", jax.ShapeDtypeStruct(queries.shape, bf16), vmem),
        ("grad_kv", jax.ShapeDtypeStruct((2, HD // 2, tokens), bf16), vmem),
        ("hidden_grad", jax.ShapeDtypeStruct(final_hidden.shape, f32), vmem),
        ("grad_sinks", jax.ShapeDtypeStruct((heads,), f32), smem),
    ]
    scratch = named_scratch(heads, tokens, policy_head.shape[0])
    names = [name for name, _, _ in operands + results] + list(scratch)
    shapes = [shape for _, shape, _ in results]
    made = pl.pallas_call(
        kernel_of(names),
        out_shape=shapes,
        in_specs=[spec for _, _, spec in operands],
        out_specs=[spec for _, _, spec in results],
        scratch_shapes=list(scratch.values()),
        compiler_params=pltpu.CompilerParams(
            collective_id=0, has_side_effects=True, vmem_limit_bytes=56 * 2**20
        ),
    )(*[value for _, value, _ in operands])
    grad_queries, grad_kv, hidden_grad, grad_sinks = pl.pallas_call(
        hand_over,
        out_shape=shapes,
        in_specs=[spec for _, _, spec in results],
        out_specs=[spec for _, _, spec in results],
        compiler_params=pltpu.CompilerParams(vmem_limit_bytes=60 * 2**20),
    )(*made)
    return (grad_queries, grad_kv, grad_sinks, hidden_grad)


def solution(mesh):
    in_specs = (
        P("seq", "vocab"),
        P("seq", None),
        P("seq", None),
        P("vocab"),
        P("seq"),
        P("seq", "vocab"),
        P("vocab", None),
        P("seq", None),
        P("seq"),
        P("seq"),
        P("seq"),
        P("seq"),
        P(("seq", "vocab"), None),
        P(("seq", "vocab"), None),
    )
    out_specs = (P("seq", "vocab"), P(None, "vocab", "seq"), P("vocab"), P("seq", None))
    return jax.shard_map(shards, mesh=mesh, in_specs=in_specs, out_specs=out_specs, check_vma=False)
```

```python
import jax
import jax.numpy as jnp
from jax import lax
from jax.experimental import pallas as pl
from jax.experimental.pallas import tpu as pltpu
from jax.sharding import PartitionSpec as P

HD = 64
WINDOW = 128
NX, NY, NZ, NC = 4, 8, 8, 2
D = 2880
QUARTER = 768
HALF = 2 * QUARTER
SLOTS = 8
PART = NY // 2
CHUNK = QUARTER // 2

loss_scale = 64.0
kl_weight = 1.0
masked_score = -1e30
contract_last = (((1,), (1,)), ((), ()))
contract_first = (((0,), (0,)), ((), ()))
MESH = pl.DeviceIdType.MESH
f32 = jnp.float32
bf16 = jnp.bfloat16


def wrap(value, size):
    return lax.rem(value + size, size)


def device(x, y, z, c):
    return (y * NX + x, z * NC + c)


def unfold(block, row):
    return jnp.concatenate([block[row : row + 1], block[row + 3 : row + 4]], axis=1)


def fold(rows):
    half = rows[0].shape[1] // 2
    parts = [row[:, :half] for row in rows] + [row[:, half:] for row in rows]
    return jnp.concatenate(parts + [jnp.zeros((2, half), f32)], axis=0)


def merged(blocks):
    rows = [[unfold(block, k) for block in blocks] for k in range(3)]
    tops = [rows[0][0], rows[1][0]]
    for k in range(2):
        for row in rows[k][1:]:
            tops[k] = jnp.maximum(tops[k], row)
    mass, cross, frozen = 0.0, 0.0, 0.0
    for policy, other, mean in zip(*rows):
        share = jnp.exp(policy - tops[0])
        mass += share
        cross += share * mean
        frozen += jnp.exp(other - tops[1])
    return [tops[0] + jnp.log(mass), tops[1] + jnp.log(frozen), cross / mass]


def far_first(size):
    return sorted(range(1, size), key=lambda d: (-min(d, size - d), d))


def quarter_stop(q):
    return min(D, (q + 1) * QUARTER)


def named_scratch(heads, tokens, vocab_rows):
    dma = pltpu.SemaphoreType.DMA
    rows = NX * NY * SLOTS
    stat = (8, rows // 2)
    width = heads * HD
    tiles = tokens // WINDOW
    lanes = heads * WINDOW
    return {
        "policy": pltpu.VMEM((vocab_rows, D), bf16),
        "frozen": pltpu.VMEM((vocab_rows, D), bf16),
        "proj": pltpu.VMEM((D, width), bf16),
        "key_cols": pltpu.VMEM((tokens, 128), bf16),
        "value_cols": pltpu.VMEM((tokens, 128), bf16),
        "kv_own": pltpu.VMEM((tokens, 128), bf16),
        "kv_halo": pltpu.VMEM((WINDOW, 128), bf16),
        "doc_own": pltpu.VMEM((8, WINDOW), f32),
        "doc_halo": pltpu.VMEM((8, WINDOW), f32),
        "key_ext": pltpu.VMEM((tokens + WINDOW, HD), bf16),
        "value_ext": pltpu.VMEM((tokens + WINDOW, HD), bf16),
        "key_marks": pltpu.VMEM((tiles + 1, WINDOW, WINDOW), f32),
        "query_t": pltpu.VMEM((width, tokens), bf16),
        "upper_t": pltpu.VMEM((width, tokens), f32),
        "prob": pltpu.VMEM((tiles, WINDOW, lanes), f32),
        "prob_low": pltpu.VMEM((tiles, 2 * WINDOW, lanes), bf16),
        "share": pltpu.VMEM((tiles, 1, lanes), f32),
        "attended": pltpu.VMEM((tiles, HD, lanes), f32),
        "query_grad": pltpu.VMEM((width, tokens), f32),
        "key_grad": pltpu.VMEM((HD, tokens + WINDOW), f32),
        "value_grad": pltpu.VMEM((HD, tokens + WINDOW), f32),
        "kv_send": pltpu.VMEM((2, HD // 2, tokens), bf16),
        "kv_recv": pltpu.VMEM((2, HD // 2, tokens), bf16),
        "edge_send": pltpu.VMEM((2, 2, HD // 2, WINDOW), bf16),
        "edge_recv": pltpu.VMEM((2, 2, HD // 2, WINDOW), bf16),
        "sink_y": pltpu.VMEM((NY, 1, WINDOW), f32),
        "sink_x": pltpu.VMEM((NX, 1, WINDOW), f32),
        "wide": pltpu.VMEM((4, SLOTS, QUARTER), f32),
        "gathered": pltpu.VMEM((2, 2, NX, 2, PART, 2 * SLOTS, CHUNK), bf16),
        "rows": pltpu.VMEM((4, rows, QUARTER), bf16),
        "meta_y": pltpu.VMEM((NY,) + stat, f32),
        "meta_x": pltpu.VMEM((NX,) + stat, f32),
        "stat_xc": pltpu.VMEM((NX * NC,) + stat, f32),
        "stat_y": pltpu.VMEM((NY,) + stat, f32),
        "stat_z": pltpu.VMEM((NZ,) + stat, f32),
        "total": pltpu.VMEM((4, NX, NY * SLOTS, QUARTER), f32),
        "outgoing": pltpu.VMEM((2, NX, NY * SLOTS, QUARTER), bf16),
        "from_core": pltpu.VMEM((2, NX, NY * SLOTS, QUARTER), bf16),
        "send_x": pltpu.VMEM((2, NX, 2, PART * SLOTS, QUARTER), bf16),
        "relay": pltpu.VMEM((2, 2, PART * SLOTS, QUARTER), bf16),
        "from_x": pltpu.VMEM((2, 4, PART * SLOTS, QUARTER), bf16),
        "send_y": pltpu.VMEM((2, NY, 2 * SLOTS, CHUNK), bf16),
        "from_y": pltpu.VMEM((2, NY, 2 * SLOTS, CHUNK), bf16),
        "from_z": pltpu.VMEM((2, NZ, 2 * SLOTS, CHUNK), bf16),
        "final": pltpu.VMEM((4, 2 * SLOTS, CHUNK), f32),
        "queries": pltpu.VMEM((tokens, width), bf16),
        "upper": pltpu.VMEM((tokens, width), bf16),
        "slot_hot": pltpu.VMEM((tokens, WINDOW), f32),
        "slot_query": pltpu.VMEM((HD, WINDOW), bf16),
        "slot_upper": pltpu.VMEM((HD, WINDOW), f32),
        "slot_prob": pltpu.VMEM((tokens + WINDOW, WINDOW), f32),
        "slot_attended": pltpu.VMEM((HD, WINDOW), f32),
        "slot_share": pltpu.VMEM((1, WINDOW), f32),
        "sink_bulk": pltpu.VMEM((8, WINDOW), f32),
        "hidden": pltpu.VMEM((SLOTS, D), bf16),
        "advantages": pltpu.VMEM((1, SLOTS), bf16),
        "docs": pltpu.VMEM((tiles, WINDOW), jnp.int32),
        "sampled": pltpu.SMEM((SLOTS,), jnp.int32),
        "live": pltpu.SMEM((SLOTS,), jnp.int32),
        "slot_pos": pltpu.SMEM((SLOTS,), jnp.int32),
        "sinks": pltpu.SMEM((heads,), f32),
        "grad_queries": pltpu.VMEM((tokens, width), bf16),
        "grad_kv": pltpu.VMEM((2, HD // 2, tokens), bf16),
        "hidden_grad": pltpu.VMEM((SLOTS, D), f32),
        "logits": pltpu.VMEM((2, vocab_rows, rows), f32),
        "load_sem": dma((14,)),
        "store_sem": dma((3,)),
        "gy": dma((2, 2 * NY)),
        "gx": dma((2, 12)),
        "gc": dma((2, 16)),
        "my": dma((2, NY)),
        "mx": dma((2, NX)),
        "sxc": dma((2, NX * NC)),
        "sy": dma((2, NY)),
        "sz": dma((2, NZ)),
        "rc": dma((2, 2 * NX)),
        "rx": dma((2, 12)),
        "ry": dma((2, 2 * NY)),
        "rz": dma((2, 2 * NZ)),
        "fc": dma((2, 2)),
        "halo": dma((2, 2)),
        "kv": dma((2, 3)),
        "ky": dma((2, NY)),
        "kx": dma((2, NX)),
    }


class Names:
    def __init__(self, names, refs):
        for name, ref in zip(names, refs):
            setattr(self, name, ref)


def kernel_of(names):
    def kernel(*refs):
        policy_step(Names(names, refs))

    return kernel


def policy_step(r):
    seq, vocab = lax.axis_index("seq"), lax.axis_index("vocab")
    x, y = lax.rem(seq, NX), lax.div(seq, NX)
    z, c = lax.div(vocab, NC), lax.rem(vocab, NC)
    n_seq = NX * NY
    vocab_rows = r.policy.shape[0]
    tokens = r.queries.shape[0]
    heads = r.queries.shape[1] // HD
    tiles = tokens // WINDOW
    scale = HD ** (-0.5)
    left, right, far = wrap(x - 1, NX), wrap(x + 1, NX), wrap(x + 2, NX)
    y_part, y_sub = lax.div(y, PART), lax.rem(y, PART)

    def along_x(d, other=0):
        return device(wrap(x + d, NX), y, z, 1 - c if other else c)

    def along_y(d):
        return device(x, wrap(y + d, NY), z, c)

    def along_z(d):
        return device(x, y, wrap(z + d, NZ), c)

    across = device(x, y, z, 1 - c)
    to_right, to_left = along_x(1), along_x(-1)
    xc_steps = [(d, o) for d in range(NX) for o in range(NC) if d or o]
    prev, after = wrap(seq - 1, n_seq), wrap(seq + 1, n_seq)

    def send(src, dst, sems, k, target):
        copy = pltpu.make_async_remote_copy(
            src_ref=src,
            dst_ref=dst,
            send_sem=sems.at[0, k],
            recv_sem=sems.at[1, k],
            device_id=target,
            device_id_type=MESH,
        )
        copy.start()
        return copy

    def wait_all(copies):
        for copy in copies:
            copy.wait()

    barrier = pltpu.get_barrier_semaphore()
    peers = [along_x(d, o) for d, o in xc_steps]
    peers += [along_y(d) for d in range(1, NY)] + [along_z(d) for d in range(1, NZ)]
    peers += [(owner, z * NC + o) for owner in (prev, after) for o in range(NC)]
    for peer in peers:
        pl.semaphore_signal(barrier, inc=1, device_id=peer, device_id_type=MESH)

    def load(src, dst, k):
        copy = pltpu.make_async_copy(src, dst, r.load_sem.at[k])
        copy.start()
        return copy

    load_hidden = load(r.hidden_hbm, r.hidden, 0)
    small = [
        load(r.advantages_hbm, r.advantages, 1),
        load(r.sampled_hbm, r.sampled, 2),
        load(r.live_hbm, r.live, 3),
        load(r.slot_pos_hbm, r.slot_pos, 4),
        load(r.sinks_hbm, r.sinks, 5),
        load(r.docs_hbm, r.docs, 6),
    ]
    column = pl.multiple_of(lax.div(z, 2) * 128, 128)
    load_keys = load(r.keys_hbm.at[:, pl.ds(column, 128)], r.key_cols, 7)
    load_values = load(r.values_hbm.at[:, pl.ds(column, 128)], r.value_cols, 8)
    load_queries = load(r.queries_hbm, r.queries, 9)
    load_upper = load(r.upper_hbm, r.upper, 10)
    load_policy = load(r.policy_hbm, r.policy, 11)
    load_frozen = load(r.frozen_hbm, r.frozen, 12)
    load_proj = load(r.proj_hbm, r.proj, 13)

    load_hidden.wait()
    hidden = r.hidden[...].astype(f32)
    r.wide[3] = jnp.zeros((SLOTS, QUARTER), f32)
    for q in range(4):
        r.wide[q, :, : quarter_stop(q) - q * QUARTER] = hidden[:, q * QUARTER : quarter_stop(q)]
    packed = jnp.concatenate([r.wide[2 * c], r.wide[2 * c + 1]], axis=0).astype(bf16)
    for k in range(2):
        r.gathered[k, c, x, y_part, y_sub] = packed[:, k * CHUNK : (k + 1) * CHUNK]
    wait_all(small)
    stat = r.meta_y.shape[1:]
    field = lax.broadcasted_iota(jnp.int32, stat, 0)
    lane = lax.broadcasted_iota(jnp.int32, stat, 1) + jnp.where(field < 3, 0, stat[1])
    field = jnp.where(field < 3, field, field - 3)
    meta = jnp.zeros(stat, f32)
    first_lane = (x * NY + y) * SLOTS
    for k in range(SLOTS):
        value = jnp.where(field == 1, r.sampled[k].astype(f32), r.live[k].astype(f32))
        meta = jnp.where(lane == first_lane + k, value, meta)
    advantages = jnp.concatenate([r.advantages[...].astype(f32)] * (stat[1] // SLOTS), axis=1)
    mine_here = (lane >= first_lane) & (lane < first_lane + SLOTS) & (field == 0)
    meta = jnp.where(mine_here, jnp.broadcast_to(advantages, stat), meta)
    r.meta_y[y] = meta
    pl.semaphore_wait(barrier, len(peers))

    copies_y = [[], []]
    for k in range(2):
        own_slot = r.gathered.at[k, c, x, y_part, y_sub]
        for d in far_first(NY):
            copies_y[k].append(send(own_slot, own_slot, r.gy, k * NY + d, along_y(d)))
    metas_y = [send(r.meta_y.at[y], r.meta_y.at[y], r.my, d, along_y(d)) for d in range(1, NY)]

    load_keys.wait()
    load_values.wait()

    def swapped(block):
        return jnp.concatenate([block[:, HD:], block[:, :HD]], axis=1)

    key_cols, value_cols = r.key_cols[...].astype(f32), r.value_cols[...].astype(f32)
    even = lax.rem(z, 2) == 0
    key_part = jnp.where(even, key_cols, swapped(key_cols))
    value_part = jnp.where(even, swapped(value_cols), value_cols)
    low_lanes = lax.broadcasted_iota(jnp.int32, key_cols.shape, 1) < HD
    r.kv_own[...] = jnp.where(low_lanes, key_part, value_part).astype(bf16)
    docs = r.docs[...].astype(f32)
    r.doc_own[...] = jnp.broadcast_to(docs[tiles - 1 :], r.doc_own.shape)
    after_me = (after, vocab)
    halos = [
        send(r.kv_own.at[pl.ds(tokens - WINDOW, WINDOW)], r.kv_halo, r.halo, 0, after_me),
        send(r.doc_own, r.doc_halo, r.halo, 1, after_me),
    ]
    load_queries.wait()
    load_upper.wait()
    r.query_t[...] = jnp.transpose(r.queries[...].astype(f32)).astype(bf16)
    r.upper_t[...] = jnp.transpose(r.upper[...].astype(f32))

    key_row = lax.broadcasted_iota(jnp.int32, (WINDOW, WINDOW), 0)
    query_col = lax.broadcasted_iota(jnp.int32, (WINDOW, WINDOW), 1)
    earlier = key_row > query_col
    query_row = lax.broadcasted_iota(jnp.int32, (1, WINDOW), 1)

    def per_head(block):
        return jnp.concatenate([block] * heads, axis=1)

    def by_head(ref, t):
        lanes = slice(t * WINDOW, (t + 1) * WINDOW)
        return jnp.concatenate([ref[h * HD : (h + 1) * HD, lanes] for h in range(heads)], axis=1)

    earlier_wide = per_head(earlier.astype(f32)) > 0.5
    sink_row = jnp.concatenate([jnp.full((1, WINDOW), r.sinks[h]) for h in range(heads)], axis=1)

    def both_blocks(block):
        return jnp.concatenate(
            [jnp.where(earlier_wide, block, 0.0), jnp.where(earlier_wide, 0.0, block)], axis=0
        ).astype(bf16)

    def one_block(strip):
        return jnp.where(earlier_wide, strip[:WINDOW], strip[WINDOW:])

    def attention_setup():
        wait_all(halos)
        kv_halo = r.kv_halo[...].astype(f32)
        kv_own = r.kv_own[...].astype(f32)
        r.key_ext[:WINDOW] = kv_halo[:, :HD].astype(bf16)
        r.key_ext[WINDOW:] = kv_own[:, :HD].astype(bf16)
        r.value_ext[:WINDOW] = kv_halo[:, HD:].astype(bf16)
        r.value_ext[WINDOW:] = kv_own[:, HD:].astype(bf16)
        halo_docs = jnp.where(seq == 0, -1.0, r.doc_halo[0:1])
        for t in range(tiles + 1):
            row = halo_docs if t == 0 else docs[t - 1 : t]
            r.key_marks[t] = jnp.transpose(jnp.broadcast_to(row, (WINDOW, WINDOW)))

    def attention_forward(t):
        strip = slice(t * WINDOW, (t + 2) * WINDOW)
        marks = jnp.where(earlier, r.key_marks[t], r.key_marks[t + 1])
        allowed = per_head((marks == docs[t : t + 1]).astype(f32)) > 0.5
        scores = one_block(
            jnp.dot(r.key_ext[strip], by_head(r.query_t, t), preferred_element_type=f32)
        )
        masked = jnp.where(allowed, scores * scale, masked_score)
        row_top = jnp.maximum(jnp.max(masked, axis=0, keepdims=True), sink_row)
        exp_terms = jnp.where(allowed, jnp.exp(masked - row_top), 0.0)
        sink_term = jnp.exp(sink_row - row_top)
        inverse = 1.0 / (jnp.sum(exp_terms, axis=0, keepdims=True) + sink_term)
        query_token = query_row + t * WINDOW
        keep = jnp.ones((1, WINDOW), f32)
        for k in range(SLOTS):
            keep = jnp.where(query_token == r.slot_pos[k], 0.0, keep)
        keep = per_head(keep)
        prob = exp_terms * (inverse * keep)
        low = both_blocks(prob)
        r.prob[t] = prob
        r.prob_low[t] = low
        r.share[t] = sink_term * inverse * keep
        r.attended[t] = lax.dot_general(
            r.value_ext[strip], low, contract_first, preferred_element_type=f32
        )

    def attention_backward(t):
        strip = slice(t * WINDOW, (t + 2) * WINDOW)
        grads_wide = by_head(r.upper_t, t)
        delta = jnp.sum(grads_wide * r.attended[t], axis=0, keepdims=True)
        sink_part = r.share[t] * delta
        for h in range(heads):
            r.sink_bulk[h : h + 1] -= sink_part[:, h * WINDOW : (h + 1) * WINDOW]
        grads = grads_wide.astype(bf16)
        dprob = one_block(jnp.dot(r.value_ext[strip], grads, preferred_element_type=f32))
        dscore = both_blocks(r.prob[t] * (dprob - delta))
        r.key_grad[:, strip] += lax.dot_general(
            by_head(r.query_t, t), dscore, contract_last, preferred_element_type=f32
        )
        r.value_grad[:, strip] += lax.dot_general(
            grads, r.prob_low[t], contract_last, preferred_element_type=f32
        )
        query_grad = scale * lax.dot_general(
            r.key_ext[strip], dscore, contract_first, preferred_element_type=f32
        )
        for h in range(heads):
            r.query_grad[h * HD : (h + 1) * HD, t * WINDOW : (t + 1) * WINDOW] = query_grad[
                :, h * WINDOW : (h + 1) * WINDOW
            ]

    lane_head = lax.div(query_row, SLOTS)

    def head_hot(h):
        return jnp.where(lane_head == h, r.slot_hot[...], 0.0).astype(bf16)

    def slot_setup():
        slot_of = lax.rem(query_row, SLOTS)
        pos_row = jnp.full((1, WINDOW), -1, jnp.int32)
        for k in range(SLOTS):
            pos_row = jnp.where(slot_of == k, r.slot_pos[k], pos_row)
        sink_slot = jnp.zeros((1, WINDOW), f32)
        for h in range(heads):
            sink_slot = jnp.where(lane_head == h, r.sinks[h], sink_slot)
        used = lane_head < heads
        token_row = lax.broadcasted_iota(jnp.int32, (tokens, WINDOW), 0)
        r.slot_hot[...] = jnp.where((token_row == pos_row) & used, 1.0, 0.0)
        doc_row = jnp.zeros((1, WINDOW), f32)
        for t in range(tiles):
            hot = r.slot_hot[t * WINDOW : (t + 1) * WINDOW]
            doc_row += jnp.sum(hot * r.key_marks[t + 1], axis=0, keepdims=True)
        query, upper = 0.0, 0.0
        for h in range(heads):
            hot, span = head_hot(h), slice(h * HD, (h + 1) * HD)
            query += jnp.dot(r.query_t[span], hot, preferred_element_type=f32)
            upper += jnp.dot(r.upper_t[span].astype(bf16), hot, preferred_element_type=f32)
        r.slot_query[...] = query.astype(bf16)
        r.slot_upper[...] = upper
        scores = jnp.dot(r.key_ext[...], r.slot_query[...], preferred_element_type=f32)
        key_at = lax.broadcasted_iota(jnp.int32, scores.shape, 0)
        behind = pos_row + WINDOW - key_at
        marks = r.key_marks[...].reshape(scores.shape)
        allowed = (behind >= 0) & (behind < WINDOW) & (marks == doc_row) & used
        masked = jnp.where(allowed, scores * scale, masked_score)
        row_top = jnp.maximum(jnp.max(masked, axis=0, keepdims=True), sink_slot)
        exp_terms = jnp.where(allowed, jnp.exp(masked - row_top), 0.0)
        sink_term = jnp.exp(sink_slot - row_top)
        inverse = 1.0 / (jnp.sum(exp_terms, axis=0, keepdims=True) + sink_term)
        prob = exp_terms * inverse
        r.slot_prob[...] = prob
        r.slot_share[...] = jnp.where(used, sink_term * inverse, 0.0)
        r.slot_attended[...] = lax.dot_general(
            r.value_ext[...], prob.astype(bf16), contract_first, preferred_element_type=f32
        )

    r.key_grad[...] = jnp.zeros(r.key_grad.shape, f32)
    r.value_grad[...] = jnp.zeros(r.value_grad.shape, f32)
    r.sink_bulk[...] = jnp.zeros(r.sink_bulk.shape, f32)
    sent_x, sent_c, order = [[], []], [[], []], [[], []]

    def along(k, group, part, target):
        block = r.gathered.at[k, c, group, part]
        sent_x[k].append(send(block, block, r.gx, 6 * k + len(sent_x[k]), target))

    def cross_send(k, group, part):
        block = r.gathered.at[k, c, group, part]
        sent_c[k].append(send(block, block, r.gc, 8 * k + len(sent_c[k]), across))
        order[k].append((group, part))

    def arrange(k, half, group, part):
        block = r.gathered[k, half, group, part].astype(f32).reshape(PART, 2, SLOTS, CHUNK)
        start = pl.multiple_of((group * 2 + part) * (PART * SLOTS), PART * SLOTS)
        for low in range(2):
            r.rows[
                2 * half + low, pl.ds(start, PART * SLOTS), k * CHUNK : (k + 1) * CHUNK
            ] = block[:, low].reshape(PART * SLOTS, CHUNK).astype(bf16)

    def spread(k):
        wait_all(copies_y[k])
        along(k, x, 0, to_right)
        along(k, x, 1, to_left)
        along(k, x, 1, to_right)
        along(k, x, 0, to_left)
        cross_send(k, x, 0)
        cross_send(k, x, 1)

    def relay_on(k):
        sent_x[k][0].wait_recv()
        along(k, left, 0, to_right)
        cross_send(k, left, 0)
        sent_x[k][1].wait_recv()
        along(k, right, 1, to_left)
        cross_send(k, right, 1)

    def direct_rest(k):
        sent_x[k][2].wait_recv()
        cross_send(k, left, 1)
        sent_x[k][3].wait_recv()
        cross_send(k, right, 0)

    def far_rest(k):
        sent_x[k][4].wait_recv()
        cross_send(k, far, 0)
        sent_x[k][5].wait_recv()
        cross_send(k, far, 1)

    def arrange_own(k):
        for group, part in order[k]:
            arrange(k, c, group, part)

    spread(0)
    wait_all(metas_y)
    meta = r.meta_y[0]
    for k in range(1, NY):
        meta += r.meta_y[k]
    r.meta_x[x] = meta
    metas_x = [send(r.meta_x.at[x], r.meta_x.at[x], r.mx, d, along_x(d)) for d in range(1, NX)]
    attention_setup()
    spread(1)
    relay_on(0)
    attention_forward(0)
    relay_on(1)
    direct_rest(0)
    attention_forward(1)
    direct_rest(1)
    far_rest(0)
    attention_forward(2)
    arrange_own(0)
    far_rest(1)
    for t in range(3, tiles):
        attention_forward(t)
    arrange_own(1)
    load_policy.wait()
    load_frozen.wait()

    def add_logits(half, first):
        for i, head in enumerate([r.policy, r.frozen]):
            result = 0.0
            for q in (2 * half, 2 * half + 1):
                width = quarter_stop(q) - q * QUARTER
                result += lax.dot_general(
                    head[:, q * QUARTER : quarter_stop(q)],
                    r.rows[q, :, :width],
                    contract_last,
                    preferred_element_type=f32,
                )
            r.logits[i] = result if first else r.logits[i] + result

    for half in range(2):
        pl.when(c == half)(lambda half=half: add_logits(half, True))
    for k in range(2):
        for copy, (group, part) in zip(sent_c[k], order[k]):
            copy.wait_recv()
            arrange(k, 1 - c, group, part)
    for half in range(2):
        pl.when(c != half)(lambda half=half: add_logits(half, False))
    for copy in sent_x[0] + sent_x[1] + sent_c[0] + sent_c[1]:
        copy.wait_send()
    wait_all(metas_x)
    meta = r.meta_x[0]
    for k in range(1, NX):
        meta += r.meta_x[k]

    policy_logits, frozen_logits = r.logits[0], r.logits[1]
    policy_peak = jnp.max(policy_logits, axis=0, keepdims=True)
    frozen_peak = jnp.max(frozen_logits, axis=0, keepdims=True)
    logit_diff = policy_logits - frozen_logits
    policy_terms = jnp.exp(policy_logits - policy_peak)
    mass = jnp.sum(policy_terms, axis=0, keepdims=True)
    mean = jnp.sum(policy_terms * logit_diff, axis=0, keepdims=True) / mass
    frozen_mass = jnp.sum(jnp.exp(frozen_logits - frozen_peak), axis=0, keepdims=True)
    stats = [policy_peak + jnp.log(mass), frozen_peak + jnp.log(frozen_mass), mean]

    r.stat_xc[0] = fold(stats)
    copies = [
        send(r.stat_xc.at[0], r.stat_xc.at[k + 1], r.sxc, k, along_x(d, o))
        for k, (d, o) in enumerate(xc_steps)
    ]
    attention_backward(0)
    wait_all(copies)
    r.stat_y[0] = fold(merged([r.stat_xc[k] for k in range(NX * NC)]))
    copies = [
        send(r.stat_y.at[0], r.stat_y.at[d], r.sy, d, along_y(d)) for d in far_first(NY)
    ]
    attention_backward(1)
    wait_all(copies)
    r.stat_z[0] = fold(merged([r.stat_y[k] for k in range(NY)]))
    copies = [
        send(r.stat_z.at[0], r.stat_z.at[d], r.sz, d, along_z(d)) for d in far_first(NZ)
    ]
    attention_backward(2)
    wait_all(copies)
    policy_lognorm, frozen_lognorm, cross_total = merged([r.stat_z[k] for k in range(NZ)])

    divergence = cross_total - policy_lognorm + frozen_lognorm
    policy_prob = jnp.exp(policy_logits - policy_lognorm)
    first_id = (seq * (NZ * NC) + vocab) * vocab_rows
    ids_here = (first_id + lax.broadcasted_iota(jnp.int32, policy_logits.shape, 0)).astype(f32)
    picked = (ids_here == unfold(meta, 1)).astype(f32)
    weight = loss_scale * unfold(meta, 2)
    log_ratio = policy_logits - policy_lognorm - (frozen_logits - frozen_lognorm) - divergence
    logit_grad = (
        weight * (-unfold(meta, 0) * (picked - policy_prob) + kl_weight * policy_prob * log_ratio)
    ).astype(bf16)

    group_rows = NY * SLOTS
    r.total[3, :, :, D - 3 * QUARTER - 64 :] = jnp.zeros(
        (NX, group_rows, 4 * QUARTER - D + 64), f32
    )

    def product(half):
        stop = quarter_stop(2 * half + 1)
        whole = lax.dot_general(
            logit_grad,
            r.policy[:, half * HALF : stop],
            contract_first,
            preferred_element_type=f32,
        )
        for q in (2 * half, 2 * half + 1):
            width = quarter_stop(q) - q * QUARTER
            low = (q - 2 * half) * QUARTER
            r.total[q, :, :, :width] = whole[:, low : low + width].reshape(NX, group_rows, width)

    for half in range(2):
        pl.when(c != half)(lambda half=half: product(half))
    part_rows = PART * SLOTS
    low_part, high_part = slice(0, part_rows), slice(part_rows, 2 * part_rows)
    cores, reduced, copies_y, copies_z = [[], []], [[], []], [[], []], [[], []]
    for k in range(2):
        for i, group in enumerate([far, right, left, x]):
            r.outgoing[k, group] = r.total[2 * (1 - c) + k, group].astype(bf16)
            cores[k].append(
                send(r.outgoing.at[k, group], r.from_core.at[k, group], r.rc, NX * k + i, across)
            )

    for half in range(2):
        pl.when(c == half)(lambda half=half: product(half))
    for t in range(3, tiles):
        attention_backward(t)

    def pass_on(k, src, dst, target):
        reduced[k].append(send(src, dst, r.rx, 6 * k + len(reduced[k]), target))

    def chip_sum(k, i, group):
        cores[k][i].wait_recv()
        return r.total[2 * c + k, group] + r.from_core[k, group].astype(f32)

    def start_far(k):
        both = chip_sum(k, 0, far)
        r.send_x[k, far, 0] = both[low_part].astype(bf16)
        r.send_x[k, far, 1] = both[high_part].astype(bf16)
        pass_on(k, r.send_x.at[k, far, 0], r.relay.at[k, 0], to_right)
        pass_on(k, r.send_x.at[k, far, 1], r.relay.at[k, 1], to_left)

    def start_direct(k):
        for_right = chip_sum(k, 1, right)
        r.send_x[k, right, 1] = for_right[high_part].astype(bf16)
        pass_on(k, r.send_x.at[k, right, 1], r.from_x.at[k, 0], to_right)
        r.total[2 * c + k, right, low_part] = for_right[low_part]
        for_left = chip_sum(k, 2, left)
        r.send_x[k, left, 0] = for_left[low_part].astype(bf16)
        pass_on(k, r.send_x.at[k, left, 0], r.from_x.at[k, 1], to_left)
        r.total[2 * c + k, left, high_part] = for_left[high_part]

    def start_summed(k):
        reduced[k][0].wait_recv()
        block = r.total[2 * c + k, right, low_part] + r.relay[k, 0].astype(f32)
        r.send_x[k, right, 0] = block.astype(bf16)
        pass_on(k, r.send_x.at[k, right, 0], r.from_x.at[k, 2], to_right)
        reduced[k][1].wait_recv()
        block = r.total[2 * c + k, left, high_part] + r.relay[k, 1].astype(f32)
        r.send_x[k, left, 1] = block.astype(bf16)
        pass_on(k, r.send_x.at[k, left, 1], r.from_x.at[k, 3], to_left)
        r.total[2 * c + k, x] = chip_sum(k, 3, x)

    def start_y(k):
        for copy in reduced[k][2:]:
            copy.wait_recv()
        for part, (rows, first, second) in enumerate([(low_part, 1, 2), (high_part, 0, 3)]):
            mine = r.total[2 * c + k, x, rows] + r.from_x[k, first].astype(f32)
            mine = (mine + r.from_x[k, second].astype(f32)).reshape(PART, SLOTS, QUARTER)
            packed = jnp.concatenate([mine[:, :, :CHUNK], mine[:, :, CHUNK:]], axis=1)
            r.send_y[k, part * PART : (part + 1) * PART] = packed.astype(bf16)
        for d in far_first(NY):
            copies_y[k].append(
                send(
                    r.send_y.at[k, wrap(y + d, NY)],
                    r.from_y.at[k, d],
                    r.ry,
                    NY * k + d,
                    along_y(d),
                )
            )

    def start_z(k):
        wait_all(copies_y[k])
        summed = r.send_y[k, y].astype(f32)
        for d in range(1, NY):
            summed += r.from_y[k, d].astype(f32)
        r.from_z[k, z] = summed.astype(bf16)
        block = r.from_z.at[k, z]
        for d in far_first(NZ):
            copies_z[k].append(send(block, block, r.rz, NZ * k + d, along_z(d)))

    def start_core(k):
        wait_all(copies_z[k])
        summed = r.from_z[k, 0].astype(f32)
        for d in range(1, NZ):
            summed += r.from_z[k, d].astype(f32)
        r.final[2 * c + k] = summed
        block = r.final.at[2 * c + k]
        return send(block, block, r.fc, k, across)

    start_far(0)
    start_direct(0)
    start_far(1)
    start_summed(0)
    start_direct(1)
    start_summed(1)
    start_y(0)
    start_y(1)
    slot_setup()
    start_z(0)
    start_z(1)
    load_proj.wait()
    finals = [start_core(0), start_core(1)]
    slot_grad = 0.0
    for k in range(2):
        finals[k].wait()
        for q in (k, 2 + k):
            stop = quarter_stop(q)
            part = jnp.concatenate([r.final[q, :SLOTS, :], r.final[q, SLOTS:, :]], axis=1)
            part = part[:, : stop - q * QUARTER]
            r.hidden_grad[:, q * QUARTER : stop] = part
            slot_grad += jnp.dot(
                part.astype(bf16), r.proj[q * QUARTER : stop, :], preferred_element_type=f32
            )
    for copy in cores[0] + cores[1] + reduced[0] + reduced[1]:
        copy.wait_send()
    stores = []

    def store(src, dst):
        copy = pltpu.make_async_copy(src, dst, r.store_sem.at[len(stores)])
        copy.start()
        stores.append(copy)

    store(r.hidden_grad, r.hidden_grad_hbm)
    slot_at = lax.broadcasted_iota(jnp.int32, (SLOTS, WINDOW), 0)
    spread_out = lax.rem(lax.broadcasted_iota(jnp.int32, (SLOTS, WINDOW), 1), SLOTS) == slot_at
    wide_grad = lax.dot_general(
        slot_grad,
        spread_out.astype(f32),
        contract_first,
        precision=lax.Precision.HIGHEST,
        preferred_element_type=f32,
    )
    slot_out = r.slot_upper[...]
    for h in range(heads):
        slot_out += jnp.where(lane_head == h, wide_grad[h * HD : (h + 1) * HD], 0.0)
    slot_low = slot_out.astype(bf16)
    slot_delta = jnp.sum(slot_low.astype(f32) * r.slot_attended[...], axis=0, keepdims=True)
    slot_sink = r.slot_share[...] * slot_delta
    sink_heads = lax.broadcasted_iota(jnp.int32, (8, WINDOW), 0)
    sink_block = r.sink_bulk[...] - jnp.where(sink_heads == lane_head, slot_sink, 0.0)
    sink_sums = jnp.sum(sink_block, axis=1, keepdims=True)
    r.sink_y[y] = jnp.sum(jnp.where(sink_heads == query_row, sink_sums, 0.0), axis=0, keepdims=True)
    sinks_y = [
        send(r.sink_y.at[y], r.sink_y.at[y], r.ky, d, along_y(d)) for d in far_first(NY)
    ]
    slot_dprob = jnp.dot(r.value_ext[...], slot_low, preferred_element_type=f32)
    slot_dscore = (r.slot_prob[...] * (slot_dprob - slot_delta)).astype(bf16)
    r.key_grad[...] += lax.dot_general(
        r.slot_query[...], slot_dscore, contract_last, preferred_element_type=f32
    )
    r.value_grad[...] += lax.dot_general(
        slot_low, r.slot_prob[...].astype(bf16), contract_last, preferred_element_type=f32
    )
    half_width = HD // 2
    mine_rows = pl.ds(pl.multiple_of(c * half_width, half_width), half_width)
    other_rows = pl.ds(pl.multiple_of((1 - c) * half_width, half_width), half_width)
    both_grads = [(r.key_grad, scale), (r.value_grad, 1.0)]
    for k, (grad, factor) in enumerate(both_grads):
        r.kv_send[k] = (grad[other_rows, WINDOW:] * factor).astype(bf16)
        r.edge_send[0, k] = (grad[mine_rows, :WINDOW] * factor).astype(bf16)
        r.edge_send[1, k] = (grad[other_rows, :WINDOW] * factor).astype(bf16)
    kv_copies = [
        send(r.edge_send.at[0], r.edge_recv.at[0], r.kv, 0, (prev, vocab)),
        send(r.edge_send.at[1], r.edge_recv.at[1], r.kv, 1, (prev, z * NC + 1 - c)),
        send(r.kv_send, r.kv_recv, r.kv, 2, across),
    ]
    slot_query_grad = scale * lax.dot_general(
        r.key_ext[...], slot_dscore, contract_first, preferred_element_type=f32
    )
    slot_query_low = slot_query_grad.astype(bf16)
    for h in range(heads):
        r.query_grad[h * HD : (h + 1) * HD] += lax.dot_general(
            slot_query_low, head_hot(h), contract_last, preferred_element_type=f32
        )
    wait_all(sinks_y)
    sink_sum = r.sink_y[0]
    for k in range(1, NY):
        sink_sum += r.sink_y[k]
    r.sink_x[x] = sink_sum
    sinks_x = [send(r.sink_x.at[x], r.sink_x.at[x], r.kx, d, along_x(d)) for d in range(1, NX)]
    r.grad_queries[...] = jnp.transpose(r.query_grad[...]).astype(bf16)
    store(r.grad_queries, r.grad_queries_hbm)
    wait_all(kv_copies)
    for k, (grad, factor) in enumerate(both_grads):
        own = grad[mine_rows, WINDOW:] * factor + r.kv_recv[k].astype(f32)
        edge = r.edge_recv[0, k].astype(f32) + r.edge_recv[1, k].astype(f32)
        r.grad_kv[k] = jnp.concatenate(
            [own[:, : tokens - WINDOW], own[:, tokens - WINDOW :] + edge], axis=1
        ).astype(bf16)
    store(r.grad_kv, r.grad_kv_hbm)
    wait_all(sinks_x)
    sink_sum = r.sink_x[0]
    for k in range(1, NX):
        sink_sum += r.sink_x[k]
    for h in range(heads):
        r.grad_sinks[h] = jnp.sum(jnp.where(query_row == h, sink_sum, 0.0))
    wait_all(stores)


def hand_over(*refs):
    count = len(refs) // 2
    for source, result in zip(refs[: count - 1], refs[count:]):
        result[...] = source[...]
    for h in range(refs[-1].shape[0]):
        refs[-1][h] = refs[count - 1][h]


def shards(
    queries,
    keys,
    values,
    sinks,
    doc_ids,
    upper_grad,
    out_proj,
    final_hidden,
    advantages,
    slot_pos,
    slot_live,
    sampled_ids,
    policy_head,
    reference_head,
):
    vmem = pl.BlockSpec(memory_space=pltpu.VMEM)
    smem = pl.BlockSpec(memory_space=pltpu.SMEM)
    hbm = pl.BlockSpec(memory_space=pl.ANY)
    heads = sinks.shape[0]
    tokens = queries.shape[0]
    operands = [
        ("hidden_hbm", final_hidden),
        ("advantages_hbm", advantages.reshape(1, SLOTS)),
        ("sampled_hbm", sampled_ids),
        ("live_hbm", slot_live),
        ("slot_pos_hbm", slot_pos),
        ("sinks_hbm", sinks),
        ("docs_hbm", doc_ids.reshape(tokens // WINDOW, WINDOW)),
        ("queries_hbm", queries),
        ("upper_hbm", upper_grad),
        ("keys_hbm", keys),
        ("values_hbm", values),
        ("proj_hbm", out_proj.T),
        ("policy_hbm", policy_head),
        ("frozen_hbm", reference_head),
    ]
    results = [
        ("grad_queries_hbm", jax.ShapeDtypeStruct(queries.shape, bf16), vmem),
        ("grad_kv_hbm", jax.ShapeDtypeStruct((2, HD // 2, tokens), bf16), vmem),
        ("hidden_grad_hbm", jax.ShapeDtypeStruct(final_hidden.shape, f32), vmem),
        ("grad_sinks", jax.ShapeDtypeStruct((heads,), f32), smem),
    ]
    scratch = named_scratch(heads, tokens, policy_head.shape[0])
    names = [entry[0] for entry in operands + results] + list(scratch)
    shapes = [shape for _, shape, _ in results]
    made = pl.pallas_call(
        kernel_of(names),
        out_shape=shapes,
        in_specs=[hbm] * len(operands),
        out_specs=[hbm] * 3 + [smem],
        scratch_shapes=list(scratch.values()),
        compiler_params=pltpu.CompilerParams(
            collective_id=0, has_side_effects=True, vmem_limit_bytes=56 * 2**20
        ),
    )(*[value for _, value in operands])
    grad_queries, grad_kv, hidden_grad, grad_sinks = pl.pallas_call(
        hand_over,
        out_shape=shapes,
        in_specs=[spec for _, _, spec in results],
        out_specs=[spec for _, _, spec in results],
        compiler_params=pltpu.CompilerParams(vmem_limit_bytes=60 * 2**20),
    )(*made)
    return (grad_queries, grad_kv, grad_sinks, hidden_grad)


def solution(mesh):
    in_specs = (
        P("seq", "vocab"),
        P("seq", None),
        P("seq", None),
        P("vocab"),
        P("seq"),
        P("seq", "vocab"),
        P("vocab", None),
        P("seq", None),
        P("seq"),
        P("seq"),
        P("seq"),
        P("seq"),
        P(("seq", "vocab"), None),
        P(("seq", "vocab"), None),
    )
    out_specs = (P("seq", "vocab"), P(None, "vocab", "seq"), P("vocab"), P("seq", None))
    return jax.shard_map(shards, mesh=mesh, in_specs=in_specs, out_specs=out_specs, check_vma=False)
```

```python
import jax
import jax.numpy as jnp
from jax import lax
from jax.experimental import pallas as pl
from jax.experimental.pallas import tpu as pltpu
from jax.sharding import PartitionSpec as P

HD = 64
WINDOW = 128
NX, NY, NZ, NC = 4, 8, 8, 2
D = 2880
QUARTER = 768
HALF = 2 * QUARTER
SLOTS = 8
PART = NY // 2
CHUNK = QUARTER // 2
TILES = CHUNK // 128

loss_scale = 64.0
kl_weight = 1.0
masked_score = -1e30
contract_last = (((1,), (1,)), ((), ()))
contract_first = (((0,), (0,)), ((), ()))
MESH = pl.DeviceIdType.MESH
f32 = jnp.float32
bf16 = jnp.bfloat16


def wrap(value, size):
    return lax.rem(value + size, size)


def device(x, y, z, c):
    return (y * NX + x, z * NC + c)


def unfold(block, row):
    return jnp.concatenate([block[row : row + 1], block[row + 3 : row + 4]], axis=1)


def fold(rows):
    half = rows[0].shape[1] // 2
    parts = [row[:, :half] for row in rows] + [row[:, half:] for row in rows]
    return jnp.concatenate(parts + [jnp.zeros((2, half), f32)], axis=0)


def merged(blocks):
    top = blocks[0]
    for block in blocks[1:]:
        top = jnp.maximum(top, block)
    mass, cross = 0.0, 0.0
    for block in blocks:
        share = jnp.exp(block - top)
        mass += share
        cross += pltpu.roll(share, 2, axis=0) * block
    row = lax.broadcasted_iota(jnp.int32, top.shape, 0)
    return jnp.where(
        (row == 2) | (row == 5), cross / pltpu.roll(mass, 2, axis=0), top + jnp.log(mass)
    )


def far_first(size):
    return sorted(range(1, size), key=lambda d: (-min(d, size - d), d))


def quarter_stop(q):
    return min(D, (q + 1) * QUARTER)


def named_scratch(heads, tokens, vocab_rows):
    dma = pltpu.SemaphoreType.DMA
    rows = NX * NY * SLOTS
    stat = (8, rows // 2)
    width = heads * HD
    tiles = tokens // WINDOW
    lanes = heads * WINDOW
    return {
        "policy": pltpu.VMEM((vocab_rows, D), bf16),
        "frozen": pltpu.VMEM((vocab_rows, D), bf16),
        "proj": pltpu.VMEM((D, width), bf16),
        "key_cols": pltpu.VMEM((tokens, 128), bf16),
        "value_cols": pltpu.VMEM((tokens, 128), bf16),
        "kv_own": pltpu.VMEM((tokens, 128), bf16),
        "kv_halo": pltpu.VMEM((WINDOW, 128), bf16),
        "doc_own": pltpu.VMEM((8, WINDOW), f32),
        "doc_halo": pltpu.VMEM((8, WINDOW), f32),
        "key_ext": pltpu.VMEM((tokens + WINDOW, HD), bf16),
        "value_ext": pltpu.VMEM((tokens + WINDOW, HD), bf16),
        "key_marks": pltpu.VMEM((tiles + 1, WINDOW, WINDOW), f32),
        "query_t": pltpu.VMEM((width, tokens), bf16),
        "upper_t": pltpu.VMEM((width, tokens), f32),
        "prob": pltpu.VMEM((tiles, WINDOW, lanes), f32),
        "prob_low": pltpu.VMEM((tiles, 2 * WINDOW, lanes), bf16),
        "share": pltpu.VMEM((tiles, 1, lanes), f32),
        "attended": pltpu.VMEM((tiles, HD, lanes), f32),
        "query_grad": pltpu.VMEM((width, tokens), f32),
        "key_grad": pltpu.VMEM((HD, tokens + WINDOW), f32),
        "value_grad": pltpu.VMEM((HD, tokens + WINDOW), f32),
        "kv_send": pltpu.VMEM((2, HD // 2, tokens), bf16),
        "kv_recv": pltpu.VMEM((2, HD // 2, tokens), bf16),
        "edge_send": pltpu.VMEM((2, 2, HD // 2, WINDOW), bf16),
        "edge_recv": pltpu.VMEM((2, 2, HD // 2, WINDOW), bf16),
        "sink_y": pltpu.VMEM((NY, 1, WINDOW), f32),
        "sink_x": pltpu.VMEM((NX, 1, WINDOW), f32),
        "wide": pltpu.VMEM((4, SLOTS, QUARTER), f32),
        "gathered": pltpu.VMEM((2, 2, NX, 2, PART, 2 * SLOTS, CHUNK), bf16),
        "rows": pltpu.VMEM((4, rows, QUARTER), bf16),
        "meta_y": pltpu.VMEM((NY,) + stat, f32),
        "meta_x": pltpu.VMEM((NX,) + stat, f32),
        "stat_xc": pltpu.VMEM((NX * NC,) + stat, f32),
        "stat_y": pltpu.VMEM((NY,) + stat, f32),
        "stat_z": pltpu.VMEM((NZ,) + stat, f32),
        "total": pltpu.VMEM((4, NX, NY * SLOTS, QUARTER), f32),
        "outgoing": pltpu.VMEM((2, NX, NY * SLOTS, QUARTER), bf16),
        "from_core": pltpu.VMEM((2, NX, NY * SLOTS, QUARTER), bf16),
        "send_x": pltpu.VMEM((2, NX, 2, PART * SLOTS, QUARTER), bf16),
        "relay": pltpu.VMEM((2, 2, PART * SLOTS, QUARTER), bf16),
        "from_x": pltpu.VMEM((2, 4, PART * SLOTS, QUARTER), bf16),
        "send_y": pltpu.VMEM((2, NY, 2 * SLOTS, CHUNK), bf16),
        "from_y": pltpu.VMEM((2, NY, 2 * SLOTS, CHUNK), bf16),
        "send_z": pltpu.VMEM((2 * TILES, 2 * SLOTS, 128), bf16),
        "from_z": pltpu.VMEM((NZ, 2 * SLOTS, 128), bf16),
        "final": pltpu.VMEM((NC, 2 * TILES, 2 * SLOTS, 128), bf16),
        "queries": pltpu.VMEM((tokens, width), bf16),
        "upper": pltpu.VMEM((tokens, width), bf16),
        "slot_hot": pltpu.VMEM((tokens, WINDOW), f32),
        "slot_query": pltpu.VMEM((HD, WINDOW), bf16),
        "slot_upper": pltpu.VMEM((HD, WINDOW), f32),
        "slot_prob": pltpu.VMEM((tokens + WINDOW, WINDOW), f32),
        "slot_attended": pltpu.VMEM((HD, WINDOW), f32),
        "slot_share": pltpu.VMEM((1, WINDOW), f32),
        "sink_bulk": pltpu.VMEM((8, WINDOW), f32),
        "hidden": pltpu.VMEM((SLOTS, D), bf16),
        "advantages": pltpu.VMEM((1, SLOTS), bf16),
        "docs": pltpu.VMEM((tiles, WINDOW), jnp.int32),
        "sampled": pltpu.SMEM((SLOTS,), jnp.int32),
        "live": pltpu.SMEM((SLOTS,), jnp.int32),
        "slot_pos": pltpu.SMEM((SLOTS,), jnp.int32),
        "sinks": pltpu.SMEM((heads,), f32),
        "grad_queries": pltpu.VMEM((tokens, width), bf16),
        "grad_kv": pltpu.VMEM((2, HD // 2, tokens), bf16),
        "hidden_grad": pltpu.VMEM((SLOTS, D), f32),
        "logits": pltpu.VMEM((2, vocab_rows, rows), f32),
        "load_sem": dma((14,)),
        "store_sem": dma((3,)),
        "gy": dma((2, 2 * NY)),
        "gx": dma((2, 12)),
        "gc": dma((2, 16)),
        "my": dma((2, NY)),
        "mx": dma((2, NX)),
        "sxc": dma((2, NX * NC)),
        "sy": dma((2, NY)),
        "sz": dma((2, NZ)),
        "rc": dma((2, 2 * NX)),
        "rx": dma((2, 12)),
        "ry": dma((2, 2 * NY)),
        "rz": dma((2, NZ)),
        "fc": dma((2, NC * NZ)),
        "halo": dma((2, 2)),
        "kv": dma((2, 3)),
        "ky": dma((2, NY)),
        "kx": dma((2, NX)),
    }


class Names:
    def __init__(self, names, refs):
        for name, ref in zip(names, refs):
            setattr(self, name, ref)


def kernel_of(names):
    def kernel(*refs):
        policy_step(Names(names, refs))

    return kernel


def policy_step(r):
    seq, vocab = lax.axis_index("seq"), lax.axis_index("vocab")
    x, y = lax.rem(seq, NX), lax.div(seq, NX)
    z, c = lax.div(vocab, NC), lax.rem(vocab, NC)
    n_seq = NX * NY
    vocab_rows = r.policy.shape[0]
    tokens = r.queries.shape[0]
    heads = r.queries.shape[1] // HD
    tiles = tokens // WINDOW
    scale = HD ** (-0.5)
    left, right, far = wrap(x - 1, NX), wrap(x + 1, NX), wrap(x + 2, NX)
    y_part, y_sub = lax.div(y, PART), lax.rem(y, PART)

    def along_x(d, other=0):
        return device(wrap(x + d, NX), y, z, 1 - c if other else c)

    def along_y(d):
        return device(x, wrap(y + d, NY), z, c)

    def along_z(d):
        return device(x, y, wrap(z + d, NZ), c)

    across = device(x, y, z, 1 - c)
    to_right, to_left = along_x(1), along_x(-1)
    xc_steps = [(d, o) for d in range(NX) for o in range(NC) if d or o]
    prev, after = wrap(seq - 1, n_seq), wrap(seq + 1, n_seq)

    def send(src, dst, sems, k, target):
        copy = pltpu.make_async_remote_copy(
            src_ref=src,
            dst_ref=dst,
            send_sem=sems.at[0, k],
            recv_sem=sems.at[1, k],
            device_id=target,
            device_id_type=MESH,
        )
        copy.start()
        return copy

    def wait_all(copies):
        for copy in copies:
            copy.wait()

    barrier = pltpu.get_barrier_semaphore()
    peers = [along_y(d) for d in far_first(NY)] + [along_x(d, o) for d, o in xc_steps]
    peers += [device(x, y, wrap(z + d, NZ), o) for d in far_first(NZ) for o in range(NC)]
    peers += [(owner, z * NC + o) for owner in (prev, after) for o in range(NC)]
    for peer in peers:
        pl.semaphore_signal(barrier, inc=1, device_id=peer, device_id_type=MESH)

    def load(src, dst, k):
        copy = pltpu.make_async_copy(src, dst, r.load_sem.at[k])
        copy.start()
        return copy

    load_hidden = load(r.hidden_hbm, r.hidden, 0)
    small = [
        load(r.advantages_hbm, r.advantages, 1),
        load(r.sampled_hbm, r.sampled, 2),
        load(r.live_hbm, r.live, 3),
        load(r.slot_pos_hbm, r.slot_pos, 4),
        load(r.sinks_hbm, r.sinks, 5),
        load(r.docs_hbm, r.docs, 6),
    ]
    column = pl.multiple_of(lax.div(z, 2) * 128, 128)
    load_keys = load(r.keys_hbm.at[:, pl.ds(column, 128)], r.key_cols, 7)
    load_values = load(r.values_hbm.at[:, pl.ds(column, 128)], r.value_cols, 8)
    load_queries = load(r.queries_hbm, r.queries, 9)
    load_upper = load(r.upper_hbm, r.upper, 10)
    load_policy = load(r.policy_hbm, r.policy, 11)
    load_frozen = load(r.frozen_hbm, r.frozen, 12)
    load_proj = load(r.proj_hbm, r.proj, 13)

    load_hidden.wait()
    hidden = r.hidden[...].astype(f32)
    r.wide[3] = jnp.zeros((SLOTS, QUARTER), f32)
    for q in range(4):
        r.wide[q, :, : quarter_stop(q) - q * QUARTER] = hidden[:, q * QUARTER : quarter_stop(q)]
    packed = jnp.concatenate([r.wide[2 * c], r.wide[2 * c + 1]], axis=0).astype(bf16)
    for k in range(2):
        r.gathered[k, c, x, y_part, y_sub] = packed[:, k * CHUNK : (k + 1) * CHUNK]
    wait_all(small)
    stat = r.meta_y.shape[1:]
    field = lax.broadcasted_iota(jnp.int32, stat, 0)
    lane = lax.broadcasted_iota(jnp.int32, stat, 1) + jnp.where(field < 3, 0, stat[1])
    field = jnp.where(field < 3, field, field - 3)
    meta = jnp.zeros(stat, f32)
    first_lane = (x * NY + y) * SLOTS
    for k in range(SLOTS):
        value = jnp.where(field == 1, r.sampled[k].astype(f32), r.live[k].astype(f32))
        meta = jnp.where(lane == first_lane + k, value, meta)
    advantages = jnp.concatenate([r.advantages[...].astype(f32)] * (stat[1] // SLOTS), axis=1)
    mine_here = (lane >= first_lane) & (lane < first_lane + SLOTS) & (field == 0)
    meta = jnp.where(mine_here, jnp.broadcast_to(advantages, stat), meta)
    r.meta_y[y] = meta
    pl.semaphore_wait(barrier, len(peers))

    copies_y = [[], []]
    for k in range(2):
        own_slot = r.gathered.at[k, c, x, y_part, y_sub]
        for d in far_first(NY):
            copies_y[k].append(send(own_slot, own_slot, r.gy, k * NY + d, along_y(d)))
    metas_y = [send(r.meta_y.at[y], r.meta_y.at[y], r.my, d, along_y(d)) for d in range(1, NY)]

    load_keys.wait()
    load_values.wait()

    def swapped(block):
        return jnp.concatenate([block[:, HD:], block[:, :HD]], axis=1)

    key_cols, value_cols = r.key_cols[...].astype(f32), r.value_cols[...].astype(f32)
    even = lax.rem(z, 2) == 0
    key_part = jnp.where(even, key_cols, swapped(key_cols))
    value_part = jnp.where(even, swapped(value_cols), value_cols)
    low_lanes = lax.broadcasted_iota(jnp.int32, key_cols.shape, 1) < HD
    r.kv_own[...] = jnp.where(low_lanes, key_part, value_part).astype(bf16)
    docs = r.docs[...].astype(f32)
    r.doc_own[...] = jnp.broadcast_to(docs[tiles - 1 :], r.doc_own.shape)
    after_me = (after, vocab)
    halos = [
        send(r.kv_own.at[pl.ds(tokens - WINDOW, WINDOW)], r.kv_halo, r.halo, 0, after_me),
        send(r.doc_own, r.doc_halo, r.halo, 1, after_me),
    ]
    load_queries.wait()
    load_upper.wait()
    r.query_t[...] = jnp.transpose(r.queries[...].astype(f32)).astype(bf16)
    r.upper_t[...] = jnp.transpose(r.upper[...].astype(f32))

    key_row = lax.broadcasted_iota(jnp.int32, (WINDOW, WINDOW), 0)
    query_col = lax.broadcasted_iota(jnp.int32, (WINDOW, WINDOW), 1)
    earlier = key_row > query_col
    query_row = lax.broadcasted_iota(jnp.int32, (1, WINDOW), 1)

    def per_head(block):
        return jnp.concatenate([block] * heads, axis=1)

    def by_head(ref, t):
        lanes = slice(t * WINDOW, (t + 1) * WINDOW)
        return jnp.concatenate([ref[h * HD : (h + 1) * HD, lanes] for h in range(heads)], axis=1)

    earlier_wide = per_head(earlier.astype(f32)) > 0.5
    sink_row = jnp.concatenate([jnp.full((1, WINDOW), r.sinks[h]) for h in range(heads)], axis=1)

    def both_blocks(block):
        return jnp.concatenate(
            [jnp.where(earlier_wide, block, 0.0), jnp.where(earlier_wide, 0.0, block)], axis=0
        ).astype(bf16)

    def one_block(strip):
        return jnp.where(earlier_wide, strip[:WINDOW], strip[WINDOW:])

    def attention_setup():
        wait_all(halos)
        kv_halo = r.kv_halo[...].astype(f32)
        kv_own = r.kv_own[...].astype(f32)
        r.key_ext[:WINDOW] = kv_halo[:, :HD].astype(bf16)
        r.key_ext[WINDOW:] = kv_own[:, :HD].astype(bf16)
        r.value_ext[:WINDOW] = kv_halo[:, HD:].astype(bf16)
        r.value_ext[WINDOW:] = kv_own[:, HD:].astype(bf16)
        halo_docs = jnp.where(seq == 0, -1.0, r.doc_halo[0:1])
        for t in range(tiles + 1):
            row = halo_docs if t == 0 else docs[t - 1 : t]
            r.key_marks[t] = jnp.transpose(jnp.broadcast_to(row, (WINDOW, WINDOW)))

    def attention_forward(t):
        strip = slice(t * WINDOW, (t + 2) * WINDOW)
        marks = jnp.where(earlier, r.key_marks[t], r.key_marks[t + 1])
        allowed = per_head((marks == docs[t : t + 1]).astype(f32)) > 0.5
        scores = one_block(
            jnp.dot(r.key_ext[strip], by_head(r.query_t, t), preferred_element_type=f32)
        )
        masked = jnp.where(allowed, scores * scale, masked_score)
        row_top = jnp.maximum(jnp.max(masked, axis=0, keepdims=True), sink_row)
        exp_terms = jnp.where(allowed, jnp.exp(masked - row_top), 0.0)
        sink_term = jnp.exp(sink_row - row_top)
        inverse = 1.0 / (jnp.sum(exp_terms, axis=0, keepdims=True) + sink_term)
        query_token = query_row + t * WINDOW
        keep = jnp.ones((1, WINDOW), f32)
        for k in range(SLOTS):
            keep = jnp.where(query_token == r.slot_pos[k], 0.0, keep)
        keep = per_head(keep)
        prob = exp_terms * (inverse * keep)
        low = both_blocks(prob)
        r.prob[t] = prob
        r.prob_low[t] = low
        r.share[t] = sink_term * inverse * keep
        r.attended[t] = lax.dot_general(
            r.value_ext[strip], low, contract_first, preferred_element_type=f32
        )

    def attention_backward(t):
        strip = slice(t * WINDOW, (t + 2) * WINDOW)
        grads_wide = by_head(r.upper_t, t)
        delta = jnp.sum(grads_wide * r.attended[t], axis=0, keepdims=True)
        sink_part = r.share[t] * delta
        for h in range(heads):
            r.sink_bulk[h : h + 1] -= sink_part[:, h * WINDOW : (h + 1) * WINDOW]
        grads = grads_wide.astype(bf16)
        dprob = one_block(jnp.dot(r.value_ext[strip], grads, preferred_element_type=f32))
        dscore = both_blocks(r.prob[t] * (dprob - delta))
        r.key_grad[:, strip] += lax.dot_general(
            by_head(r.query_t, t), dscore, contract_last, preferred_element_type=f32
        )
        r.value_grad[:, strip] += lax.dot_general(
            grads, r.prob_low[t], contract_last, preferred_element_type=f32
        )
        query_grad = scale * lax.dot_general(
            r.key_ext[strip], dscore, contract_first, preferred_element_type=f32
        )
        for h in range(heads):
            r.query_grad[h * HD : (h + 1) * HD, t * WINDOW : (t + 1) * WINDOW] = query_grad[
                :, h * WINDOW : (h + 1) * WINDOW
            ]

    lane_head = lax.div(query_row, SLOTS)

    def head_hot(h):
        return jnp.where(lane_head == h, r.slot_hot[...], 0.0).astype(bf16)

    def slot_setup():
        slot_of = lax.rem(query_row, SLOTS)
        pos_row = jnp.full((1, WINDOW), -1, jnp.int32)
        for k in range(SLOTS):
            pos_row = jnp.where(slot_of == k, r.slot_pos[k], pos_row)
        sink_slot = jnp.zeros((1, WINDOW), f32)
        for h in range(heads):
            sink_slot = jnp.where(lane_head == h, r.sinks[h], sink_slot)
        used = lane_head < heads
        token_row = lax.broadcasted_iota(jnp.int32, (tokens, WINDOW), 0)
        r.slot_hot[...] = jnp.where((token_row == pos_row) & used, 1.0, 0.0)
        doc_row = jnp.zeros((1, WINDOW), f32)
        for t in range(tiles):
            hot = r.slot_hot[t * WINDOW : (t + 1) * WINDOW]
            doc_row += jnp.sum(hot * r.key_marks[t + 1], axis=0, keepdims=True)
        query, upper = 0.0, 0.0
        for h in range(heads):
            hot, span = head_hot(h), slice(h * HD, (h + 1) * HD)
            query += jnp.dot(r.query_t[span], hot, preferred_element_type=f32)
            upper += jnp.dot(r.upper_t[span].astype(bf16), hot, preferred_element_type=f32)
        r.slot_query[...] = query.astype(bf16)
        r.slot_upper[...] = upper
        scores = jnp.dot(r.key_ext[...], r.slot_query[...], preferred_element_type=f32)
        key_at = lax.broadcasted_iota(jnp.int32, scores.shape, 0)
        behind = pos_row + WINDOW - key_at
        marks = r.key_marks[...].reshape(scores.shape)
        allowed = (behind >= 0) & (behind < WINDOW) & (marks == doc_row) & used
        masked = jnp.where(allowed, scores * scale, masked_score)
        row_top = jnp.maximum(jnp.max(masked, axis=0, keepdims=True), sink_slot)
        exp_terms = jnp.where(allowed, jnp.exp(masked - row_top), 0.0)
        sink_term = jnp.exp(sink_slot - row_top)
        inverse = 1.0 / (jnp.sum(exp_terms, axis=0, keepdims=True) + sink_term)
        prob = exp_terms * inverse
        r.slot_prob[...] = prob
        r.slot_share[...] = jnp.where(used, sink_term * inverse, 0.0)
        r.slot_attended[...] = lax.dot_general(
            r.value_ext[...], prob.astype(bf16), contract_first, preferred_element_type=f32
        )

    r.key_grad[...] = jnp.zeros(r.key_grad.shape, f32)
    r.value_grad[...] = jnp.zeros(r.value_grad.shape, f32)
    r.sink_bulk[...] = jnp.zeros(r.sink_bulk.shape, f32)
    sent_x, sent_c, order = [[], []], [[], []], [[], []]

    def along(k, group, part, target):
        block = r.gathered.at[k, c, group, part]
        sent_x[k].append(send(block, block, r.gx, 6 * k + len(sent_x[k]), target))

    def cross_send(k, group, part):
        block = r.gathered.at[k, c, group, part]
        sent_c[k].append(send(block, block, r.gc, 8 * k + len(sent_c[k]), across))
        order[k].append((group, part))

    def arrange(k, half, group, part):
        block = r.gathered[k, half, group, part].astype(f32).reshape(PART, 2, SLOTS, CHUNK)
        start = pl.multiple_of((group * 2 + part) * (PART * SLOTS), PART * SLOTS)
        for low in range(2):
            r.rows[
                2 * half + low, pl.ds(start, PART * SLOTS), k * CHUNK : (k + 1) * CHUNK
            ] = block[:, low].reshape(PART * SLOTS, CHUNK).astype(bf16)

    def spread(k):
        wait_all(copies_y[k])
        along(k, x, 0, to_right)
        along(k, x, 1, to_left)
        along(k, x, 1, to_right)
        along(k, x, 0, to_left)
        cross_send(k, x, 0)
        cross_send(k, x, 1)

    def relay_on(k):
        sent_x[k][0].wait_recv()
        along(k, left, 0, to_right)
        cross_send(k, left, 0)
        sent_x[k][1].wait_recv()
        along(k, right, 1, to_left)
        cross_send(k, right, 1)

    def direct_rest(k):
        sent_x[k][2].wait_recv()
        cross_send(k, left, 1)
        sent_x[k][3].wait_recv()
        cross_send(k, right, 0)

    def far_rest(k):
        sent_x[k][4].wait_recv()
        cross_send(k, far, 0)
        sent_x[k][5].wait_recv()
        cross_send(k, far, 1)

    def arrange_own(k):
        for group, part in order[k]:
            arrange(k, c, group, part)

    spread(0)
    wait_all(metas_y)
    meta = r.meta_y[0]
    for k in range(1, NY):
        meta += r.meta_y[k]
    r.meta_x[x] = meta
    metas_x = [send(r.meta_x.at[x], r.meta_x.at[x], r.mx, d, along_x(d)) for d in range(1, NX)]
    attention_setup()
    spread(1)
    relay_on(0)
    attention_forward(0)
    relay_on(1)
    direct_rest(0)
    attention_forward(1)
    direct_rest(1)
    far_rest(0)
    attention_forward(2)
    arrange_own(0)
    far_rest(1)
    for t in range(3, tiles):
        attention_forward(t)
    arrange_own(1)
    load_policy.wait()
    load_frozen.wait()

    def add_logits(half, first):
        for i, head in enumerate([r.policy, r.frozen]):
            result = 0.0
            for q in (2 * half, 2 * half + 1):
                width = quarter_stop(q) - q * QUARTER
                result += lax.dot_general(
                    head[:, q * QUARTER : quarter_stop(q)],
                    r.rows[q, :, :width],
                    contract_last,
                    preferred_element_type=f32,
                )
            r.logits[i] = result if first else r.logits[i] + result

    for half in range(2):
        pl.when(c == half)(lambda half=half: add_logits(half, True))
    for k in range(2):
        for copy, (group, part) in zip(sent_c[k], order[k]):
            copy.wait_recv()
            arrange(k, 1 - c, group, part)
    for half in range(2):
        pl.when(c != half)(lambda half=half: add_logits(half, False))
    for copy in sent_x[0] + sent_x[1] + sent_c[0] + sent_c[1]:
        copy.wait_send()
    wait_all(metas_x)
    meta = r.meta_x[0]
    for k in range(1, NX):
        meta += r.meta_x[k]

    policy_logits, frozen_logits = r.logits[0], r.logits[1]
    policy_peak = jnp.max(policy_logits, axis=0, keepdims=True)
    frozen_peak = jnp.max(frozen_logits, axis=0, keepdims=True)
    logit_diff = policy_logits - frozen_logits
    policy_terms = jnp.exp(policy_logits - policy_peak)
    mass = jnp.sum(policy_terms, axis=0, keepdims=True)
    mean = jnp.sum(policy_terms * logit_diff, axis=0, keepdims=True) / mass
    frozen_mass = jnp.sum(jnp.exp(frozen_logits - frozen_peak), axis=0, keepdims=True)
    stats = [policy_peak + jnp.log(mass), frozen_peak + jnp.log(frozen_mass), mean]

    r.stat_xc[0] = fold(stats)
    copies = [
        send(r.stat_xc.at[0], r.stat_xc.at[k + 1], r.sxc, k, along_x(d, o))
        for k, (d, o) in enumerate(xc_steps)
    ]
    attention_backward(0)
    wait_all(copies)
    r.stat_y[0] = merged([r.stat_xc[k] for k in range(NX * NC)])
    copies = [
        send(r.stat_y.at[0], r.stat_y.at[d], r.sy, d, along_y(d)) for d in far_first(NY)
    ]
    attention_backward(1)
    wait_all(copies)
    r.stat_z[0] = merged([r.stat_y[k] for k in range(NY)])
    copies = [
        send(r.stat_z.at[0], r.stat_z.at[d], r.sz, d, along_z(d)) for d in far_first(NZ)
    ]
    attention_backward(2)
    wait_all(copies)
    stats = merged([r.stat_z[k] for k in range(NZ)])
    policy_lognorm, frozen_lognorm, cross_total = [unfold(stats, k) for k in range(3)]

    divergence = cross_total - policy_lognorm + frozen_lognorm
    policy_prob = jnp.exp(policy_logits - policy_lognorm)
    first_id = (seq * (NZ * NC) + vocab) * vocab_rows
    ids_here = (first_id + lax.broadcasted_iota(jnp.int32, policy_logits.shape, 0)).astype(f32)
    picked = (ids_here == unfold(meta, 1)).astype(f32)
    weight = loss_scale * unfold(meta, 2)
    log_ratio = policy_logits - policy_lognorm - (frozen_logits - frozen_lognorm) - divergence
    logit_grad = (
        weight * (-unfold(meta, 0) * (picked - policy_prob) + kl_weight * policy_prob * log_ratio)
    ).astype(bf16)

    group_rows = NY * SLOTS
    r.total[3, :, :, D - 3 * QUARTER - 64 :] = jnp.zeros(
        (NX, group_rows, 4 * QUARTER - D + 64), f32
    )

    def product(half):
        stop = quarter_stop(2 * half + 1)
        whole = lax.dot_general(
            logit_grad,
            r.policy[:, half * HALF : stop],
            contract_first,
            preferred_element_type=f32,
        )
        for q in (2 * half, 2 * half + 1):
            width = quarter_stop(q) - q * QUARTER
            low = (q - 2 * half) * QUARTER
            r.total[q, :, :, :width] = whole[:, low : low + width].reshape(NX, group_rows, width)

    for half in range(2):
        pl.when(c != half)(lambda half=half: product(half))
    part_rows = PART * SLOTS
    low_part, high_part = slice(0, part_rows), slice(part_rows, 2 * part_rows)
    cores, reduced, copies_y = [[], []], [[], []], [[], []]
    for k in range(2):
        for i, group in enumerate([far, right, left, x]):
            r.outgoing[k, group] = r.total[2 * (1 - c) + k, group].astype(bf16)
            cores[k].append(
                send(r.outgoing.at[k, group], r.from_core.at[k, group], r.rc, NX * k + i, across)
            )

    for half in range(2):
        pl.when(c == half)(lambda half=half: product(half))
    for t in range(3, tiles):
        attention_backward(t)

    def pass_on(k, src, dst, target):
        reduced[k].append(send(src, dst, r.rx, 6 * k + len(reduced[k]), target))

    def chip_sum(k, i, group):
        cores[k][i].wait_recv()
        return r.total[2 * c + k, group] + r.from_core[k, group].astype(f32)

    def start_far(k):
        both = chip_sum(k, 0, far)
        r.send_x[k, far, 0] = both[low_part].astype(bf16)
        r.send_x[k, far, 1] = both[high_part].astype(bf16)
        pass_on(k, r.send_x.at[k, far, 0], r.relay.at[k, 0], to_right)
        pass_on(k, r.send_x.at[k, far, 1], r.relay.at[k, 1], to_left)

    def start_direct(k):
        for_right = chip_sum(k, 1, right)
        r.send_x[k, right, 1] = for_right[high_part].astype(bf16)
        pass_on(k, r.send_x.at[k, right, 1], r.from_x.at[k, 0], to_right)
        r.total[2 * c + k, right, low_part] = for_right[low_part]
        for_left = chip_sum(k, 2, left)
        r.send_x[k, left, 0] = for_left[low_part].astype(bf16)
        pass_on(k, r.send_x.at[k, left, 0], r.from_x.at[k, 1], to_left)
        r.total[2 * c + k, left, high_part] = for_left[high_part]

    def start_summed(k):
        reduced[k][0].wait_recv()
        block = r.total[2 * c + k, right, low_part] + r.relay[k, 0].astype(f32)
        r.send_x[k, right, 0] = block.astype(bf16)
        pass_on(k, r.send_x.at[k, right, 0], r.from_x.at[k, 2], to_right)
        reduced[k][1].wait_recv()
        block = r.total[2 * c + k, left, high_part] + r.relay[k, 1].astype(f32)
        r.send_x[k, left, 1] = block.astype(bf16)
        pass_on(k, r.send_x.at[k, left, 1], r.from_x.at[k, 3], to_left)
        r.total[2 * c + k, x] = chip_sum(k, 3, x)

    def start_y(k):
        for copy in reduced[k][2:]:
            copy.wait_recv()
        for part, (rows, first, second) in enumerate([(low_part, 1, 2), (high_part, 0, 3)]):
            mine = r.total[2 * c + k, x, rows] + r.from_x[k, first].astype(f32)
            mine = (mine + r.from_x[k, second].astype(f32)).reshape(PART, SLOTS, QUARTER)
            packed = jnp.concatenate([mine[:, :, :CHUNK], mine[:, :, CHUNK:]], axis=1)
            r.send_y[k, part * PART : (part + 1) * PART] = packed.astype(bf16)
        for d in far_first(NY):
            copies_y[k].append(
                send(
                    r.send_y.at[k, wrap(y + d, NY)],
                    r.from_y.at[k, d],
                    r.ry,
                    NY * k + d,
                    along_y(d),
                )
            )

    def start_z(k):
        wait_all(copies_y[k])
        summed = r.send_y[k, y].astype(f32)
        for d in range(1, NY):
            summed += r.from_y[k, d].astype(f32)
        for j in range(TILES):
            owner = TILES * k + j
            r.send_z[owner] = summed[:, j * 128 : (j + 1) * 128].astype(bf16)
            pl.when(z != owner)(lambda owner=owner: to_owner(owner).start())
            pl.when(z == owner)(lambda owner=owner: keep_own(owner))

    def to_owner(owner):
        return pltpu.make_async_remote_copy(
            src_ref=r.send_z.at[owner],
            dst_ref=r.from_z.at[z],
            send_sem=r.rz.at[0, owner],
            recv_sem=r.rz.at[1, z],
            device_id=device(x, y, owner, c),
            device_id_type=MESH,
        )

    def keep_own(owner):
        r.from_z[owner] = r.send_z[owner]

    def arrival(block, sem):
        return pltpu.make_async_remote_copy(
            src_ref=block,
            dst_ref=block,
            send_sem=r.fc.at[0, 0],
            recv_sem=sem,
            device_id=across,
            device_id_type=MESH,
        )

    column_peers = [(d, o) for d in far_first(NZ) for o in range(NC)] + [(0, 1)]

    def to_column(k):
        d, o = column_peers[k]
        block = r.final.at[c, z]
        return pltpu.make_async_remote_copy(
            src_ref=block,
            dst_ref=block,
            send_sem=r.fc.at[0, k],
            recv_sem=r.fc.at[1, c * NZ + z],
            device_id=device(x, y, wrap(z + d, NZ), 1 - c if o else c),
            device_id_type=MESH,
        )

    def sum_column():
        for d in range(1, NZ):
            source = wrap(z + d, NZ)
            arrival(r.from_z.at[source], r.rz.at[1, source]).wait_recv()
        summed = r.from_z[0].astype(f32)
        for k in range(1, NZ):
            summed += r.from_z[k].astype(f32)
        r.final[c, z] = summed.astype(bf16)
        for k in range(len(column_peers)):
            to_column(k).start()

    def end_column():
        for k in range(len(column_peers)):
            to_column(k).wait_send()

    start_far(0)
    start_direct(0)
    start_far(1)
    start_summed(0)
    start_direct(1)
    start_summed(1)
    start_y(0)
    start_y(1)
    slot_setup()
    start_z(0)
    start_z(1)
    load_proj.wait()
    pl.when(z < 2 * TILES)(sum_column)
    for core in range(NC):
        for owner in range(2 * TILES):
            block, sem = r.final.at[core, owner], r.fc.at[1, core * NZ + owner]
            pl.when((c != core) | (z != owner))(
                lambda block=block, sem=sem: arrival(block, sem).wait_recv()
            )
    slot_grad = 0.0
    for q in range(4):
        stop = quarter_stop(q)
        tiles_of = [r.final[q // 2, TILES * (q % 2) + j].astype(f32) for j in range(TILES)]
        pieces = [tile[:SLOTS] for tile in tiles_of] + [tile[SLOTS:] for tile in tiles_of]
        part = jnp.concatenate(pieces, axis=1)[:, : stop - q * QUARTER]
        r.hidden_grad[:, q * QUARTER : stop] = part
        slot_grad += jnp.dot(
            part.astype(bf16), r.proj[q * QUARTER : stop, :], preferred_element_type=f32
        )
    pl.when(z < 2 * TILES)(end_column)
    for owner in range(2 * TILES):
        pl.when(z != owner)(lambda owner=owner: to_owner(owner).wait_send())
    for copy in cores[0] + cores[1] + reduced[0] + reduced[1]:
        copy.wait_send()
    stores = []

    def store(src, dst):
        copy = pltpu.make_async_copy(src, dst, r.store_sem.at[len(stores)])
        copy.start()
        stores.append(copy)

    store(r.hidden_grad, r.hidden_grad_hbm)
    slot_at = lax.broadcasted_iota(jnp.int32, (SLOTS, WINDOW), 0)
    spread_out = lax.rem(lax.broadcasted_iota(jnp.int32, (SLOTS, WINDOW), 1), SLOTS) == slot_at
    wide_grad = lax.dot_general(
        slot_grad,
        spread_out.astype(f32),
        contract_first,
        precision=lax.Precision.HIGHEST,
        preferred_element_type=f32,
    )
    slot_out = r.slot_upper[...]
    for h in range(heads):
        slot_out += jnp.where(lane_head == h, wide_grad[h * HD : (h + 1) * HD], 0.0)
    slot_low = slot_out.astype(bf16)
    slot_delta = jnp.sum(slot_low.astype(f32) * r.slot_attended[...], axis=0, keepdims=True)
    slot_sink = r.slot_share[...] * slot_delta
    sink_heads = lax.broadcasted_iota(jnp.int32, (8, WINDOW), 0)
    sink_block = r.sink_bulk[...] - jnp.where(sink_heads == lane_head, slot_sink, 0.0)
    sink_sums = jnp.sum(sink_block, axis=1, keepdims=True)
    r.sink_y[y] = jnp.sum(jnp.where(sink_heads == query_row, sink_sums, 0.0), axis=0, keepdims=True)
    sinks_y = [
        send(r.sink_y.at[y], r.sink_y.at[y], r.ky, d, along_y(d)) for d in far_first(NY)
    ]
    slot_dprob = jnp.dot(r.value_ext[...], slot_low, preferred_element_type=f32)
    slot_dscore = (r.slot_prob[...] * (slot_dprob - slot_delta)).astype(bf16)
    r.key_grad[...] += lax.dot_general(
        r.slot_query[...], slot_dscore, contract_last, preferred_element_type=f32
    )
    r.value_grad[...] += lax.dot_general(
        slot_low, r.slot_prob[...].astype(bf16), contract_last, preferred_element_type=f32
    )
    half_width = HD // 2
    mine_rows = pl.ds(pl.multiple_of(c * half_width, half_width), half_width)
    other_rows = pl.ds(pl.multiple_of((1 - c) * half_width, half_width), half_width)
    both_grads = [(r.key_grad, scale), (r.value_grad, 1.0)]
    for k, (grad, factor) in enumerate(both_grads):
        r.kv_send[k] = (grad[other_rows, WINDOW:] * factor).astype(bf16)
        r.edge_send[0, k] = (grad[mine_rows, :WINDOW] * factor).astype(bf16)
        r.edge_send[1, k] = (grad[other_rows, :WINDOW] * factor).astype(bf16)
    kv_copies = [
        send(r.edge_send.at[0], r.edge_recv.at[0], r.kv, 0, (prev, vocab)),
        send(r.edge_send.at[1], r.edge_recv.at[1], r.kv, 1, (prev, z * NC + 1 - c)),
        send(r.kv_send, r.kv_recv, r.kv, 2, across),
    ]
    slot_query_grad = scale * lax.dot_general(
        r.key_ext[...], slot_dscore, contract_first, preferred_element_type=f32
    )
    slot_query_low = slot_query_grad.astype(bf16)
    for h in range(heads):
        r.query_grad[h * HD : (h + 1) * HD] += lax.dot_general(
            slot_query_low, head_hot(h), contract_last, preferred_element_type=f32
        )
    wait_all(sinks_y)
    sink_sum = r.sink_y[0]
    for k in range(1, NY):
        sink_sum += r.sink_y[k]
    r.sink_x[x] = sink_sum
    sinks_x = [send(r.sink_x.at[x], r.sink_x.at[x], r.kx, d, along_x(d)) for d in range(1, NX)]
    r.grad_queries[...] = jnp.transpose(r.query_grad[...]).astype(bf16)
    store(r.grad_queries, r.grad_queries_hbm)
    wait_all(kv_copies)
    for k, (grad, factor) in enumerate(both_grads):
        own = grad[mine_rows, WINDOW:] * factor + r.kv_recv[k].astype(f32)
        edge = r.edge_recv[0, k].astype(f32) + r.edge_recv[1, k].astype(f32)
        r.grad_kv[k] = jnp.concatenate(
            [own[:, : tokens - WINDOW], own[:, tokens - WINDOW :] + edge], axis=1
        ).astype(bf16)
    store(r.grad_kv, r.grad_kv_hbm)
    wait_all(sinks_x)
    sink_sum = r.sink_x[0]
    for k in range(1, NX):
        sink_sum += r.sink_x[k]
    for h in range(heads):
        r.grad_sinks[h] = jnp.sum(jnp.where(query_row == h, sink_sum, 0.0))
    wait_all(stores)


def hand_over(*refs):
    count = len(refs) // 2
    for source, result in zip(refs[: count - 1], refs[count:]):
        result[...] = source[...]
    for h in range(refs[-1].shape[0]):
        refs[-1][h] = refs[count - 1][h]


def shards(
    queries,
    keys,
    values,
    sinks,
    doc_ids,
    upper_grad,
    out_proj,
    final_hidden,
    advantages,
    slot_pos,
    slot_live,
    sampled_ids,
    policy_head,
    reference_head,
):
    vmem = pl.BlockSpec(memory_space=pltpu.VMEM)
    smem = pl.BlockSpec(memory_space=pltpu.SMEM)
    hbm = pl.BlockSpec(memory_space=pl.ANY)
    heads = sinks.shape[0]
    tokens = queries.shape[0]
    operands = [
        ("hidden_hbm", final_hidden),
        ("advantages_hbm", advantages.reshape(1, SLOTS)),
        ("sampled_hbm", sampled_ids),
        ("live_hbm", slot_live),
        ("slot_pos_hbm", slot_pos),
        ("sinks_hbm", sinks),
        ("docs_hbm", doc_ids.reshape(tokens // WINDOW, WINDOW)),
        ("queries_hbm", queries),
        ("upper_hbm", upper_grad),
        ("keys_hbm", keys),
        ("values_hbm", values),
        ("proj_hbm", out_proj.T),
        ("policy_hbm", policy_head),
        ("frozen_hbm", reference_head),
    ]
    results = [
        ("grad_queries_hbm", jax.ShapeDtypeStruct(queries.shape, bf16), vmem),
        ("grad_kv_hbm", jax.ShapeDtypeStruct((2, HD // 2, tokens), bf16), vmem),
        ("hidden_grad_hbm", jax.ShapeDtypeStruct(final_hidden.shape, f32), vmem),
        ("grad_sinks", jax.ShapeDtypeStruct((heads,), f32), smem),
    ]
    scratch = named_scratch(heads, tokens, policy_head.shape[0])
    names = [entry[0] for entry in operands + results] + list(scratch)
    shapes = [shape for _, shape, _ in results]
    made = pl.pallas_call(
        kernel_of(names),
        out_shape=shapes,
        in_specs=[hbm] * len(operands),
        out_specs=[hbm] * 3 + [smem],
        scratch_shapes=list(scratch.values()),
        compiler_params=pltpu.CompilerParams(
            collective_id=0, has_side_effects=True, vmem_limit_bytes=56 * 2**20
        ),
    )(*[value for _, value in operands])
    grad_queries, grad_kv, hidden_grad, grad_sinks = pl.pallas_call(
        hand_over,
        out_shape=shapes,
        in_specs=[spec for _, _, spec in results],
        out_specs=[spec for _, _, spec in results],
        compiler_params=pltpu.CompilerParams(vmem_limit_bytes=60 * 2**20),
    )(*made)
    return (grad_queries, grad_kv, grad_sinks, hidden_grad)


def solution(mesh):
    in_specs = (
        P("seq", "vocab"),
        P("seq", None),
        P("seq", None),
        P("vocab"),
        P("seq"),
        P("seq", "vocab"),
        P("vocab", None),
        P("seq", None),
        P("seq"),
        P("seq"),
        P("seq"),
        P("seq"),
        P(("seq", "vocab"), None),
        P(("seq", "vocab"), None),
    )
    out_specs = (P("seq", "vocab"), P(None, "vocab", "seq"), P("vocab"), P("seq", None))
    return jax.shard_map(shards, mesh=mesh, in_specs=in_specs, out_specs=out_specs, check_vma=False)
```

```python
import jax
import jax.numpy as jnp
from jax import lax
from jax.experimental import pallas as pl
from jax.experimental.pallas import tpu as pltpu
from jax.sharding import PartitionSpec as P

HD = 64
WINDOW = 128
NX, NY, NZ, NC = 4, 8, 8, 2
D = 2880
QUARTER = 768
HALF = 2 * QUARTER
SLOTS = 8
PART = NY // 2
CHUNK = QUARTER // 2

loss_scale = 64.0
kl_weight = 1.0
masked_score = -1e30
contract_last = (((1,), (1,)), ((), ()))
contract_first = (((0,), (0,)), ((), ()))
MESH = pl.DeviceIdType.MESH
f32 = jnp.float32
bf16 = jnp.bfloat16


def wrap(value, size):
    return lax.rem(value + size, size)


def device(x, y, z, c):
    return (y * NX + x, z * NC + c)


def unfold(block, row):
    return jnp.concatenate([block[row : row + 1], block[row + 3 : row + 4]], axis=1)


def fold(rows):
    half = rows[0].shape[1] // 2
    parts = [row[:, :half] for row in rows] + [row[:, half:] for row in rows]
    return jnp.concatenate(parts + [jnp.zeros((2, half), f32)], axis=0)


def merged(blocks):
    top = blocks[0]
    for block in blocks[1:]:
        top = jnp.maximum(top, block)
    mass, cross = 0.0, 0.0
    for block in blocks:
        share = jnp.exp(block - top)
        mass += share
        cross += pltpu.roll(share, 2, axis=0) * block
    row = lax.broadcasted_iota(jnp.int32, top.shape, 0)
    return jnp.where(
        (row == 2) | (row == 5), cross / pltpu.roll(mass, 2, axis=0), top + jnp.log(mass)
    )


def far_first(size):
    return sorted(range(1, size), key=lambda d: (-min(d, size - d), d))


def quarter_stop(q):
    return min(D, (q + 1) * QUARTER)


def named_scratch(heads, tokens, vocab_rows):
    dma = pltpu.SemaphoreType.DMA
    rows = NX * NY * SLOTS
    stat = (8, rows // 2)
    width = heads * HD
    tiles = tokens // WINDOW
    lanes = heads * WINDOW
    return {
        "policy": pltpu.VMEM((vocab_rows, D), bf16),
        "frozen": pltpu.VMEM((vocab_rows, D), bf16),
        "proj": pltpu.VMEM((D, width), bf16),
        "key_cols": pltpu.VMEM((tokens, 128), bf16),
        "value_cols": pltpu.VMEM((tokens, 128), bf16),
        "kv_own": pltpu.VMEM((tokens, 128), bf16),
        "kv_halo": pltpu.VMEM((WINDOW, 128), bf16),
        "doc_own": pltpu.VMEM((8, WINDOW), f32),
        "doc_halo": pltpu.VMEM((8, WINDOW), f32),
        "key_ext": pltpu.VMEM((tokens + WINDOW, HD), bf16),
        "value_ext": pltpu.VMEM((tokens + WINDOW, HD), bf16),
        "key_marks": pltpu.VMEM((tiles + 1, WINDOW, WINDOW), f32),
        "query_t": pltpu.VMEM((width, tokens), bf16),
        "upper_t": pltpu.VMEM((width, tokens), f32),
        "prob": pltpu.VMEM((tiles, WINDOW, lanes), f32),
        "prob_low": pltpu.VMEM((tiles, 2 * WINDOW, lanes), bf16),
        "share": pltpu.VMEM((tiles, 1, lanes), f32),
        "attended": pltpu.VMEM((tiles, HD, lanes), f32),
        "query_grad": pltpu.VMEM((width, tokens), f32),
        "key_grad": pltpu.VMEM((HD, tokens + WINDOW), f32),
        "value_grad": pltpu.VMEM((HD, tokens + WINDOW), f32),
        "kv_send": pltpu.VMEM((2, HD // 2, tokens), bf16),
        "kv_recv": pltpu.VMEM((2, HD // 2, tokens), bf16),
        "edge_send": pltpu.VMEM((2, 2, HD // 2, WINDOW), bf16),
        "edge_recv": pltpu.VMEM((2, 2, HD // 2, WINDOW), bf16),
        "sink_y": pltpu.VMEM((NY, 1, WINDOW), f32),
        "sink_x": pltpu.VMEM((NX, 1, WINDOW), f32),
        "wide": pltpu.VMEM((4, SLOTS, QUARTER), f32),
        "gathered": pltpu.VMEM((2, 2, NX, 2, PART, 2 * SLOTS, CHUNK), bf16),
        "rows": pltpu.VMEM((4, rows, QUARTER), bf16),
        "meta_y": pltpu.VMEM((NY,) + stat, f32),
        "meta_x": pltpu.VMEM((NX,) + stat, f32),
        "stat_xc": pltpu.VMEM((NX * NC,) + stat, f32),
        "stat_y": pltpu.VMEM((NY,) + stat, f32),
        "stat_z": pltpu.VMEM((NZ,) + stat, f32),
        "total": pltpu.VMEM((4, NX, NY * SLOTS, QUARTER), f32),
        "outgoing": pltpu.VMEM((2, NX, NY * SLOTS, QUARTER), bf16),
        "from_core": pltpu.VMEM((2, NX, NY * SLOTS, QUARTER), bf16),
        "send_x": pltpu.VMEM((2, NX, 2, PART * SLOTS, QUARTER), bf16),
        "relay": pltpu.VMEM((2, 2, PART * SLOTS, QUARTER), bf16),
        "from_x": pltpu.VMEM((2, 4, PART * SLOTS, QUARTER), bf16),
        "send_y": pltpu.VMEM((2, NY, 2 * SLOTS, CHUNK), bf16),
        "from_y": pltpu.VMEM((2, NY, 2 * SLOTS, CHUNK), bf16),
        "from_z": pltpu.VMEM((2, NZ, 2 * SLOTS, CHUNK), bf16),
        "final": pltpu.VMEM((4, 2 * SLOTS, CHUNK), f32),
        "queries": pltpu.VMEM((tokens, width), bf16),
        "upper": pltpu.VMEM((tokens, width), bf16),
        "slot_hot": pltpu.VMEM((tokens, WINDOW), f32),
        "slot_query": pltpu.VMEM((HD, WINDOW), bf16),
        "slot_upper": pltpu.VMEM((HD, WINDOW), f32),
        "slot_prob": pltpu.VMEM((tokens + WINDOW, WINDOW), f32),
        "slot_attended": pltpu.VMEM((HD, WINDOW), f32),
        "slot_share": pltpu.VMEM((1, WINDOW), f32),
        "sink_bulk": pltpu.VMEM((8, WINDOW), f32),
        "hidden": pltpu.VMEM((SLOTS, D), bf16),
        "advantages": pltpu.VMEM((1, SLOTS), bf16),
        "docs": pltpu.VMEM((tiles, WINDOW), jnp.int32),
        "sampled": pltpu.SMEM((SLOTS,), jnp.int32),
        "live": pltpu.SMEM((SLOTS,), jnp.int32),
        "slot_pos": pltpu.SMEM((SLOTS,), jnp.int32),
        "sinks": pltpu.SMEM((heads,), f32),
        "grad_queries": pltpu.VMEM((tokens, width), bf16),
        "grad_kv": pltpu.VMEM((2, HD // 2, tokens), bf16),
        "hidden_grad": pltpu.VMEM((SLOTS, D), f32),
        "logits": pltpu.VMEM((2, vocab_rows, rows), f32),
        "load_sem": dma((14,)),
        "store_sem": dma((3,)),
        "gy": dma((2, 2 * NY)),
        "gx": dma((2, 12)),
        "gc": dma((2, 16)),
        "my": dma((2, NY)),
        "mx": dma((2, NX)),
        "sxc": dma((2, NX * NC)),
        "sy": dma((2, NY)),
        "sz": dma((2, NZ)),
        "rc": dma((2, 2 * NX)),
        "rx": dma((2, 12)),
        "ry": dma((2, 2 * NY)),
        "rz": dma((2, 2 * NZ)),
        "fc": dma((2, 2)),
        "halo": dma((2, 2)),
        "kv": dma((2, 3)),
        "ky": dma((2, NY)),
        "kx": dma((2, NX)),
    }


class Names:
    def __init__(self, names, refs):
        for name, ref in zip(names, refs):
            setattr(self, name, ref)


def kernel_of(names):
    def kernel(*refs):
        policy_step(Names(names, refs))

    return kernel


def policy_step(r):
    seq, vocab = lax.axis_index("seq"), lax.axis_index("vocab")
    x, y = lax.rem(seq, NX), lax.div(seq, NX)
    z, c = lax.div(vocab, NC), lax.rem(vocab, NC)
    n_seq = NX * NY
    vocab_rows = r.policy.shape[0]
    tokens = r.queries.shape[0]
    heads = r.queries.shape[1] // HD
    tiles = tokens // WINDOW
    scale = HD ** (-0.5)
    left, right, far = wrap(x - 1, NX), wrap(x + 1, NX), wrap(x + 2, NX)
    y_part, y_sub = lax.div(y, PART), lax.rem(y, PART)

    def along_x(d, other=0):
        return device(wrap(x + d, NX), y, z, 1 - c if other else c)

    def along_y(d):
        return device(x, wrap(y + d, NY), z, c)

    def along_z(d):
        return device(x, y, wrap(z + d, NZ), c)

    across = device(x, y, z, 1 - c)
    to_right, to_left = along_x(1), along_x(-1)
    xc_steps = [(d, o) for d in range(NX) for o in range(NC) if d or o]
    prev, after = wrap(seq - 1, n_seq), wrap(seq + 1, n_seq)

    def send(src, dst, sems, k, target):
        copy = pltpu.make_async_remote_copy(
            src_ref=src,
            dst_ref=dst,
            send_sem=sems.at[0, k],
            recv_sem=sems.at[1, k],
            device_id=target,
            device_id_type=MESH,
        )
        copy.start()
        return copy

    def wait_all(copies):
        for copy in copies:
            copy.wait()

    barrier = pltpu.get_barrier_semaphore()
    peers = [along_y(d) for d in far_first(NY)] + [along_x(d, o) for d, o in xc_steps]
    peers += [along_z(d) for d in far_first(NZ)]
    peers += [(owner, z * NC + o) for owner in (prev, after) for o in range(NC)]
    for peer in peers:
        pl.semaphore_signal(barrier, inc=1, device_id=peer, device_id_type=MESH)

    def load(src, dst, k):
        copy = pltpu.make_async_copy(src, dst, r.load_sem.at[k])
        copy.start()
        return copy

    load_hidden = load(r.hidden_hbm, r.hidden, 0)
    small = [
        load(r.advantages_hbm, r.advantages, 1),
        load(r.sampled_hbm, r.sampled, 2),
        load(r.live_hbm, r.live, 3),
        load(r.slot_pos_hbm, r.slot_pos, 4),
        load(r.sinks_hbm, r.sinks, 5),
        load(r.docs_hbm, r.docs, 6),
    ]
    column = pl.multiple_of(lax.div(z, 2) * 128, 128)
    load_keys = load(r.keys_hbm.at[:, pl.ds(column, 128)], r.key_cols, 7)
    load_values = load(r.values_hbm.at[:, pl.ds(column, 128)], r.value_cols, 8)
    load_queries = load(r.queries_hbm, r.queries, 9)
    load_upper = load(r.upper_hbm, r.upper, 10)
    load_policy = load(r.policy_hbm, r.policy, 11)
    load_frozen = load(r.frozen_hbm, r.frozen, 12)
    load_proj = load(r.proj_hbm, r.proj, 13)

    load_hidden.wait()
    hidden = r.hidden[...].astype(f32)
    r.wide[3] = jnp.zeros((SLOTS, QUARTER), f32)
    for q in range(4):
        r.wide[q, :, : quarter_stop(q) - q * QUARTER] = hidden[:, q * QUARTER : quarter_stop(q)]
    packed = jnp.concatenate([r.wide[2 * c], r.wide[2 * c + 1]], axis=0).astype(bf16)
    for k in range(2):
        r.gathered[k, c, x, y_part, y_sub] = packed[:, k * CHUNK : (k + 1) * CHUNK]
    wait_all(small)
    stat = r.meta_y.shape[1:]
    field = lax.broadcasted_iota(jnp.int32, stat, 0)
    lane = lax.broadcasted_iota(jnp.int32, stat, 1) + jnp.where(field < 3, 0, stat[1])
    field = jnp.where(field < 3, field, field - 3)
    meta = jnp.zeros(stat, f32)
    first_lane = (x * NY + y) * SLOTS
    for k in range(SLOTS):
        value = jnp.where(field == 1, r.sampled[k].astype(f32), r.live[k].astype(f32))
        meta = jnp.where(lane == first_lane + k, value, meta)
    advantages = jnp.concatenate([r.advantages[...].astype(f32)] * (stat[1] // SLOTS), axis=1)
    mine_here = (lane >= first_lane) & (lane < first_lane + SLOTS) & (field == 0)
    meta = jnp.where(mine_here, jnp.broadcast_to(advantages, stat), meta)
    r.meta_y[y] = meta
    pl.semaphore_wait(barrier, len(peers))

    copies_y = [[], []]
    for k in range(2):
        own_slot = r.gathered.at[k, c, x, y_part, y_sub]
        for d in far_first(NY):
            copies_y[k].append(send(own_slot, own_slot, r.gy, k * NY + d, along_y(d)))
    metas_y = [send(r.meta_y.at[y], r.meta_y.at[y], r.my, d, along_y(d)) for d in range(1, NY)]

    load_keys.wait()
    load_values.wait()

    def swapped(block):
        return jnp.concatenate([block[:, HD:], block[:, :HD]], axis=1)

    key_cols, value_cols = r.key_cols[...].astype(f32), r.value_cols[...].astype(f32)
    even = lax.rem(z, 2) == 0
    key_part = jnp.where(even, key_cols, swapped(key_cols))
    value_part = jnp.where(even, swapped(value_cols), value_cols)
    low_lanes = lax.broadcasted_iota(jnp.int32, key_cols.shape, 1) < HD
    r.kv_own[...] = jnp.where(low_lanes, key_part, value_part).astype(bf16)
    docs = r.docs[...].astype(f32)
    r.doc_own[...] = jnp.broadcast_to(docs[tiles - 1 :], r.doc_own.shape)
    after_me = (after, vocab)
    halos = [
        send(r.kv_own.at[pl.ds(tokens - WINDOW, WINDOW)], r.kv_halo, r.halo, 0, after_me),
        send(r.doc_own, r.doc_halo, r.halo, 1, after_me),
    ]
    load_queries.wait()
    load_upper.wait()
    r.query_t[...] = jnp.transpose(r.queries[...].astype(f32)).astype(bf16)
    r.upper_t[...] = jnp.transpose(r.upper[...].astype(f32))

    key_row = lax.broadcasted_iota(jnp.int32, (WINDOW, WINDOW), 0)
    query_col = lax.broadcasted_iota(jnp.int32, (WINDOW, WINDOW), 1)
    earlier = key_row > query_col
    query_row = lax.broadcasted_iota(jnp.int32, (1, WINDOW), 1)

    def per_head(block):
        return jnp.concatenate([block] * heads, axis=1)

    def by_head(ref, t):
        lanes = slice(t * WINDOW, (t + 1) * WINDOW)
        return jnp.concatenate([ref[h * HD : (h + 1) * HD, lanes] for h in range(heads)], axis=1)

    earlier_wide = per_head(earlier.astype(f32)) > 0.5
    sink_row = jnp.concatenate([jnp.full((1, WINDOW), r.sinks[h]) for h in range(heads)], axis=1)

    def both_blocks(block):
        return jnp.concatenate(
            [jnp.where(earlier_wide, block, 0.0), jnp.where(earlier_wide, 0.0, block)], axis=0
        ).astype(bf16)

    def one_block(strip):
        return jnp.where(earlier_wide, strip[:WINDOW], strip[WINDOW:])

    def attention_setup():
        wait_all(halos)
        kv_halo = r.kv_halo[...].astype(f32)
        kv_own = r.kv_own[...].astype(f32)
        r.key_ext[:WINDOW] = kv_halo[:, :HD].astype(bf16)
        r.key_ext[WINDOW:] = kv_own[:, :HD].astype(bf16)
        r.value_ext[:WINDOW] = kv_halo[:, HD:].astype(bf16)
        r.value_ext[WINDOW:] = kv_own[:, HD:].astype(bf16)
        halo_docs = jnp.where(seq == 0, -1.0, r.doc_halo[0:1])
        for t in range(tiles + 1):
            row = halo_docs if t == 0 else docs[t - 1 : t]
            r.key_marks[t] = jnp.transpose(jnp.broadcast_to(row, (WINDOW, WINDOW)))

    def attention_forward(t):
        strip = slice(t * WINDOW, (t + 2) * WINDOW)
        marks = jnp.where(earlier, r.key_marks[t], r.key_marks[t + 1])
        allowed = per_head((marks == docs[t : t + 1]).astype(f32)) > 0.5
        scores = one_block(
            jnp.dot(r.key_ext[strip], by_head(r.query_t, t), preferred_element_type=f32)
        )
        masked = jnp.where(allowed, scores * scale, masked_score)
        row_top = jnp.maximum(jnp.max(masked, axis=0, keepdims=True), sink_row)
        exp_terms = jnp.where(allowed, jnp.exp(masked - row_top), 0.0)
        sink_term = jnp.exp(sink_row - row_top)
        inverse = 1.0 / (jnp.sum(exp_terms, axis=0, keepdims=True) + sink_term)
        query_token = query_row + t * WINDOW
        keep = jnp.ones((1, WINDOW), f32)
        for k in range(SLOTS):
            keep = jnp.where(query_token == r.slot_pos[k], 0.0, keep)
        keep = per_head(keep)
        prob = exp_terms * (inverse * keep)
        low = both_blocks(prob)
        r.prob[t] = prob
        r.prob_low[t] = low
        r.share[t] = sink_term * inverse * keep
        r.attended[t] = lax.dot_general(
            r.value_ext[strip], low, contract_first, preferred_element_type=f32
        )

    def attention_backward(t):
        strip = slice(t * WINDOW, (t + 2) * WINDOW)
        grads_wide = by_head(r.upper_t, t)
        delta = jnp.sum(grads_wide * r.attended[t], axis=0, keepdims=True)
        sink_part = r.share[t] * delta
        for h in range(heads):
            r.sink_bulk[h : h + 1] -= sink_part[:, h * WINDOW : (h + 1) * WINDOW]
        grads = grads_wide.astype(bf16)
        dprob = one_block(jnp.dot(r.value_ext[strip], grads, preferred_element_type=f32))
        dscore = both_blocks(r.prob[t] * (dprob - delta))
        r.key_grad[:, strip] += lax.dot_general(
            by_head(r.query_t, t), dscore, contract_last, preferred_element_type=f32
        )
        r.value_grad[:, strip] += lax.dot_general(
            grads, r.prob_low[t], contract_last, preferred_element_type=f32
        )
        query_grad = scale * lax.dot_general(
            r.key_ext[strip], dscore, contract_first, preferred_element_type=f32
        )
        for h in range(heads):
            r.query_grad[h * HD : (h + 1) * HD, t * WINDOW : (t + 1) * WINDOW] = query_grad[
                :, h * WINDOW : (h + 1) * WINDOW
            ]

    lane_head = lax.div(query_row, SLOTS)

    def head_hot(h):
        return jnp.where(lane_head == h, r.slot_hot[...], 0.0).astype(bf16)

    def slot_setup():
        slot_of = lax.rem(query_row, SLOTS)
        pos_row = jnp.full((1, WINDOW), -1, jnp.int32)
        for k in range(SLOTS):
            pos_row = jnp.where(slot_of == k, r.slot_pos[k], pos_row)
        sink_slot = jnp.zeros((1, WINDOW), f32)
        for h in range(heads):
            sink_slot = jnp.where(lane_head == h, r.sinks[h], sink_slot)
        used = lane_head < heads
        token_row = lax.broadcasted_iota(jnp.int32, (tokens, WINDOW), 0)
        r.slot_hot[...] = jnp.where((token_row == pos_row) & used, 1.0, 0.0)
        doc_row = jnp.zeros((1, WINDOW), f32)
        for t in range(tiles):
            hot = r.slot_hot[t * WINDOW : (t + 1) * WINDOW]
            doc_row += jnp.sum(hot * r.key_marks[t + 1], axis=0, keepdims=True)
        query, upper = 0.0, 0.0
        for h in range(heads):
            hot, span = head_hot(h), slice(h * HD, (h + 1) * HD)
            query += jnp.dot(r.query_t[span], hot, preferred_element_type=f32)
            upper += jnp.dot(r.upper_t[span].astype(bf16), hot, preferred_element_type=f32)
        r.slot_query[...] = query.astype(bf16)
        r.slot_upper[...] = upper
        scores = jnp.dot(r.key_ext[...], r.slot_query[...], preferred_element_type=f32)
        key_at = lax.broadcasted_iota(jnp.int32, scores.shape, 0)
        behind = pos_row + WINDOW - key_at
        marks = r.key_marks[...].reshape(scores.shape)
        allowed = (behind >= 0) & (behind < WINDOW) & (marks == doc_row) & used
        masked = jnp.where(allowed, scores * scale, masked_score)
        row_top = jnp.maximum(jnp.max(masked, axis=0, keepdims=True), sink_slot)
        exp_terms = jnp.where(allowed, jnp.exp(masked - row_top), 0.0)
        sink_term = jnp.exp(sink_slot - row_top)
        inverse = 1.0 / (jnp.sum(exp_terms, axis=0, keepdims=True) + sink_term)
        prob = exp_terms * inverse
        r.slot_prob[...] = prob
        r.slot_share[...] = jnp.where(used, sink_term * inverse, 0.0)
        r.slot_attended[...] = lax.dot_general(
            r.value_ext[...], prob.astype(bf16), contract_first, preferred_element_type=f32
        )

    r.key_grad[...] = jnp.zeros(r.key_grad.shape, f32)
    r.value_grad[...] = jnp.zeros(r.value_grad.shape, f32)
    r.sink_bulk[...] = jnp.zeros(r.sink_bulk.shape, f32)
    sent_x, sent_c, order = [[], []], [[], []], [[], []]

    def along(k, group, part, target):
        block = r.gathered.at[k, c, group, part]
        sent_x[k].append(send(block, block, r.gx, 6 * k + len(sent_x[k]), target))

    def cross_send(k, group, part):
        block = r.gathered.at[k, c, group, part]
        sent_c[k].append(send(block, block, r.gc, 8 * k + len(sent_c[k]), across))
        order[k].append((group, part))

    def arrange(k, half, group, part):
        block = r.gathered[k, half, group, part].astype(f32).reshape(PART, 2, SLOTS, CHUNK)
        start = pl.multiple_of((group * 2 + part) * (PART * SLOTS), PART * SLOTS)
        for low in range(2):
            r.rows[
                2 * half + low, pl.ds(start, PART * SLOTS), k * CHUNK : (k + 1) * CHUNK
            ] = block[:, low].reshape(PART * SLOTS, CHUNK).astype(bf16)

    def spread(k):
        wait_all(copies_y[k])
        along(k, x, 0, to_right)
        along(k, x, 1, to_left)
        along(k, x, 1, to_right)
        along(k, x, 0, to_left)
        cross_send(k, x, 0)
        cross_send(k, x, 1)

    def relay_on(k):
        sent_x[k][0].wait_recv()
        along(k, left, 0, to_right)
        cross_send(k, left, 0)
        sent_x[k][1].wait_recv()
        along(k, right, 1, to_left)
        cross_send(k, right, 1)

    def direct_rest(k):
        sent_x[k][2].wait_recv()
        cross_send(k, left, 1)
        sent_x[k][3].wait_recv()
        cross_send(k, right, 0)

    def far_rest(k):
        sent_x[k][4].wait_recv()
        cross_send(k, far, 0)
        sent_x[k][5].wait_recv()
        cross_send(k, far, 1)

    def arrange_own(k):
        for group, part in order[k]:
            arrange(k, c, group, part)

    spread(0)
    wait_all(metas_y)
    meta = r.meta_y[0]
    for k in range(1, NY):
        meta += r.meta_y[k]
    r.meta_x[x] = meta
    metas_x = [send(r.meta_x.at[x], r.meta_x.at[x], r.mx, d, along_x(d)) for d in range(1, NX)]
    attention_setup()
    spread(1)
    relay_on(0)
    attention_forward(0)
    relay_on(1)
    direct_rest(0)
    attention_forward(1)
    direct_rest(1)
    far_rest(0)
    attention_forward(2)
    arrange_own(0)
    far_rest(1)
    for t in range(3, tiles):
        attention_forward(t)
    arrange_own(1)
    load_policy.wait()
    load_frozen.wait()

    def add_logits(half, first):
        for i, head in enumerate([r.policy, r.frozen]):
            result = 0.0
            for q in (2 * half, 2 * half + 1):
                width = quarter_stop(q) - q * QUARTER
                result += lax.dot_general(
                    head[:, q * QUARTER : quarter_stop(q)],
                    r.rows[q, :, :width],
                    contract_last,
                    preferred_element_type=f32,
                )
            r.logits[i] = result if first else r.logits[i] + result

    for half in range(2):
        pl.when(c == half)(lambda half=half: add_logits(half, True))
    for k in range(2):
        for copy, (group, part) in zip(sent_c[k], order[k]):
            copy.wait_recv()
            arrange(k, 1 - c, group, part)
    for half in range(2):
        pl.when(c != half)(lambda half=half: add_logits(half, False))
    for copy in sent_x[0] + sent_x[1] + sent_c[0] + sent_c[1]:
        copy.wait_send()
    wait_all(metas_x)
    meta = r.meta_x[0]
    for k in range(1, NX):
        meta += r.meta_x[k]

    policy_logits, frozen_logits = r.logits[0], r.logits[1]
    policy_peak = jnp.max(policy_logits, axis=0, keepdims=True)
    frozen_peak = jnp.max(frozen_logits, axis=0, keepdims=True)
    logit_diff = policy_logits - frozen_logits
    policy_terms = jnp.exp(policy_logits - policy_peak)
    mass = jnp.sum(policy_terms, axis=0, keepdims=True)
    mean = jnp.sum(policy_terms * logit_diff, axis=0, keepdims=True) / mass
    frozen_mass = jnp.sum(jnp.exp(frozen_logits - frozen_peak), axis=0, keepdims=True)
    stats = [policy_peak + jnp.log(mass), frozen_peak + jnp.log(frozen_mass), mean]

    r.stat_xc[0] = fold(stats)
    copies = [
        send(r.stat_xc.at[0], r.stat_xc.at[k + 1], r.sxc, k, along_x(d, o))
        for k, (d, o) in enumerate(xc_steps)
    ]
    wait_all(copies)
    r.stat_y[0] = merged([r.stat_xc[k] for k in range(NX * NC)])
    copies = [
        send(r.stat_y.at[0], r.stat_y.at[d], r.sy, d, along_y(d)) for d in far_first(NY)
    ]
    wait_all(copies)
    r.stat_z[0] = merged([r.stat_y[k] for k in range(NY)])
    copies = [
        send(r.stat_z.at[0], r.stat_z.at[d], r.sz, d, along_z(d)) for d in far_first(NZ)
    ]
    wait_all(copies)
    stats = merged([r.stat_z[k] for k in range(NZ)])
    policy_lognorm, frozen_lognorm, cross_total = [unfold(stats, k) for k in range(3)]

    divergence = cross_total - policy_lognorm + frozen_lognorm
    policy_prob = jnp.exp(policy_logits - policy_lognorm)
    first_id = (seq * (NZ * NC) + vocab) * vocab_rows
    ids_here = (first_id + lax.broadcasted_iota(jnp.int32, policy_logits.shape, 0)).astype(f32)
    picked = (ids_here == unfold(meta, 1)).astype(f32)
    weight = loss_scale * unfold(meta, 2)
    log_ratio = policy_logits - policy_lognorm - (frozen_logits - frozen_lognorm) - divergence
    logit_grad = (
        weight * (-unfold(meta, 0) * (picked - policy_prob) + kl_weight * policy_prob * log_ratio)
    ).astype(bf16)

    group_rows = NY * SLOTS
    r.total[3, :, :, D - 3 * QUARTER - 64 :] = jnp.zeros(
        (NX, group_rows, 4 * QUARTER - D + 64), f32
    )

    def product(half):
        stop = quarter_stop(2 * half + 1)
        whole = lax.dot_general(
            logit_grad,
            r.policy[:, half * HALF : stop],
            contract_first,
            preferred_element_type=f32,
        )
        for q in (2 * half, 2 * half + 1):
            width = quarter_stop(q) - q * QUARTER
            low = (q - 2 * half) * QUARTER
            r.total[q, :, :, :width] = whole[:, low : low + width].reshape(NX, group_rows, width)

    for half in range(2):
        pl.when(c != half)(lambda half=half: product(half))
    part_rows = PART * SLOTS
    low_part, high_part = slice(0, part_rows), slice(part_rows, 2 * part_rows)
    cores, reduced, copies_y, copies_z = [[], []], [[], []], [[], []], [[], []]
    for k in range(2):
        for i, group in enumerate([far, right, left, x]):
            r.outgoing[k, group] = r.total[2 * (1 - c) + k, group].astype(bf16)
            cores[k].append(
                send(r.outgoing.at[k, group], r.from_core.at[k, group], r.rc, NX * k + i, across)
            )

    for half in range(2):
        pl.when(c == half)(lambda half=half: product(half))

    def pass_on(k, src, dst, target):
        reduced[k].append(send(src, dst, r.rx, 6 * k + len(reduced[k]), target))

    def chip_sum(k, i, group):
        cores[k][i].wait_recv()
        return r.total[2 * c + k, group] + r.from_core[k, group].astype(f32)

    def start_far(k):
        both = chip_sum(k, 0, far)
        r.send_x[k, far, 0] = both[low_part].astype(bf16)
        r.send_x[k, far, 1] = both[high_part].astype(bf16)
        pass_on(k, r.send_x.at[k, far, 0], r.relay.at[k, 0], to_right)
        pass_on(k, r.send_x.at[k, far, 1], r.relay.at[k, 1], to_left)

    def start_direct(k):
        for_right = chip_sum(k, 1, right)
        r.send_x[k, right, 1] = for_right[high_part].astype(bf16)
        pass_on(k, r.send_x.at[k, right, 1], r.from_x.at[k, 0], to_right)
        r.total[2 * c + k, right, low_part] = for_right[low_part]
        for_left = chip_sum(k, 2, left)
        r.send_x[k, left, 0] = for_left[low_part].astype(bf16)
        pass_on(k, r.send_x.at[k, left, 0], r.from_x.at[k, 1], to_left)
        r.total[2 * c + k, left, high_part] = for_left[high_part]

    def start_summed(k):
        reduced[k][0].wait_recv()
        block = r.total[2 * c + k, right, low_part] + r.relay[k, 0].astype(f32)
        r.send_x[k, right, 0] = block.astype(bf16)
        pass_on(k, r.send_x.at[k, right, 0], r.from_x.at[k, 2], to_right)
        reduced[k][1].wait_recv()
        block = r.total[2 * c + k, left, high_part] + r.relay[k, 1].astype(f32)
        r.send_x[k, left, 1] = block.astype(bf16)
        pass_on(k, r.send_x.at[k, left, 1], r.from_x.at[k, 3], to_left)
        r.total[2 * c + k, x] = chip_sum(k, 3, x)

    def start_y(k):
        for copy in reduced[k][2:]:
            copy.wait_recv()
        for part, (rows, first, second) in enumerate([(low_part, 1, 2), (high_part, 0, 3)]):
            mine = r.total[2 * c + k, x, rows] + r.from_x[k, first].astype(f32)
            mine = (mine + r.from_x[k, second].astype(f32)).reshape(PART, SLOTS, QUARTER)
            packed = jnp.concatenate([mine[:, :, :CHUNK], mine[:, :, CHUNK:]], axis=1)
            r.send_y[k, part * PART : (part + 1) * PART] = packed.astype(bf16)
        for d in far_first(NY):
            copies_y[k].append(
                send(
                    r.send_y.at[k, wrap(y + d, NY)],
                    r.from_y.at[k, d],
                    r.ry,
                    NY * k + d,
                    along_y(d),
                )
            )

    def start_z(k):
        wait_all(copies_y[k])
        summed = r.send_y[k, y].astype(f32)
        for d in range(1, NY):
            summed += r.from_y[k, d].astype(f32)
        r.from_z[k, z] = summed.astype(bf16)
        block = r.from_z.at[k, z]
        for d in far_first(NZ):
            copies_z[k].append(send(block, block, r.rz, NZ * k + d, along_z(d)))

    def start_core(k):
        wait_all(copies_z[k])
        summed = r.from_z[k, 0].astype(f32)
        for d in range(1, NZ):
            summed += r.from_z[k, d].astype(f32)
        r.final[2 * c + k] = summed
        block = r.final.at[2 * c + k]
        return send(block, block, r.fc, k, across)

    start_far(0)
    start_direct(0)
    start_far(1)
    attention_backward(0)
    start_summed(0)
    start_direct(1)
    attention_backward(1)
    start_summed(1)
    attention_backward(2)
    start_y(0)
    for t in range(3, tiles):
        attention_backward(t)
    start_y(1)
    slot_setup()
    start_z(0)
    start_z(1)
    load_proj.wait()
    finals = [start_core(0), start_core(1)]
    slot_grad = 0.0
    for k in range(2):
        finals[k].wait()
        for q in (k, 2 + k):
            stop = quarter_stop(q)
            part = jnp.concatenate([r.final[q, :SLOTS, :], r.final[q, SLOTS:, :]], axis=1)
            part = part[:, : stop - q * QUARTER]
            r.hidden_grad[:, q * QUARTER : stop] = part
            slot_grad += jnp.dot(
                part.astype(bf16), r.proj[q * QUARTER : stop, :], preferred_element_type=f32
            )
    for copy in cores[0] + cores[1] + reduced[0] + reduced[1]:
        copy.wait_send()
    stores = []

    def store(src, dst):
        copy = pltpu.make_async_copy(src, dst, r.store_sem.at[len(stores)])
        copy.start()
        stores.append(copy)

    store(r.hidden_grad, r.hidden_grad_hbm)
    slot_at = lax.broadcasted_iota(jnp.int32, (SLOTS, WINDOW), 0)
    spread_out = lax.rem(lax.broadcasted_iota(jnp.int32, (SLOTS, WINDOW), 1), SLOTS) == slot_at
    wide_grad = lax.dot_general(
        slot_grad,
        spread_out.astype(f32),
        contract_first,
        precision=lax.Precision.HIGHEST,
        preferred_element_type=f32,
    )
    slot_out = r.slot_upper[...]
    for h in range(heads):
        slot_out += jnp.where(lane_head == h, wide_grad[h * HD : (h + 1) * HD], 0.0)
    slot_low = slot_out.astype(bf16)
    slot_delta = jnp.sum(slot_low.astype(f32) * r.slot_attended[...], axis=0, keepdims=True)
    slot_sink = r.slot_share[...] * slot_delta
    sink_heads = lax.broadcasted_iota(jnp.int32, (8, WINDOW), 0)
    sink_block = r.sink_bulk[...] - jnp.where(sink_heads == lane_head, slot_sink, 0.0)
    sink_sums = jnp.sum(sink_block, axis=1, keepdims=True)
    r.sink_y[y] = jnp.sum(jnp.where(sink_heads == query_row, sink_sums, 0.0), axis=0, keepdims=True)
    sinks_y = [
        send(r.sink_y.at[y], r.sink_y.at[y], r.ky, d, along_y(d)) for d in far_first(NY)
    ]
    slot_dprob = jnp.dot(r.value_ext[...], slot_low, preferred_element_type=f32)
    slot_dscore = (r.slot_prob[...] * (slot_dprob - slot_delta)).astype(bf16)
    r.key_grad[...] += lax.dot_general(
        r.slot_query[...], slot_dscore, contract_last, preferred_element_type=f32
    )
    r.value_grad[...] += lax.dot_general(
        slot_low, r.slot_prob[...].astype(bf16), contract_last, preferred_element_type=f32
    )
    half_width = HD // 2
    mine_rows = pl.ds(pl.multiple_of(c * half_width, half_width), half_width)
    other_rows = pl.ds(pl.multiple_of((1 - c) * half_width, half_width), half_width)
    both_grads = [(r.key_grad, scale), (r.value_grad, 1.0)]
    for k, (grad, factor) in enumerate(both_grads):
        r.kv_send[k] = (grad[other_rows, WINDOW:] * factor).astype(bf16)
        r.edge_send[0, k] = (grad[mine_rows, :WINDOW] * factor).astype(bf16)
        r.edge_send[1, k] = (grad[other_rows, :WINDOW] * factor).astype(bf16)
    kv_copies = [
        send(r.edge_send.at[0], r.edge_recv.at[0], r.kv, 0, (prev, vocab)),
        send(r.edge_send.at[1], r.edge_recv.at[1], r.kv, 1, (prev, z * NC + 1 - c)),
        send(r.kv_send, r.kv_recv, r.kv, 2, across),
    ]
    slot_query_grad = scale * lax.dot_general(
        r.key_ext[...], slot_dscore, contract_first, preferred_element_type=f32
    )
    slot_query_low = slot_query_grad.astype(bf16)
    for h in range(heads):
        r.query_grad[h * HD : (h + 1) * HD] += lax.dot_general(
            slot_query_low, head_hot(h), contract_last, preferred_element_type=f32
        )
    wait_all(sinks_y)
    sink_sum = r.sink_y[0]
    for k in range(1, NY):
        sink_sum += r.sink_y[k]
    r.sink_x[x] = sink_sum
    sinks_x = [send(r.sink_x.at[x], r.sink_x.at[x], r.kx, d, along_x(d)) for d in range(1, NX)]
    r.grad_queries[...] = jnp.transpose(r.query_grad[...]).astype(bf16)
    store(r.grad_queries, r.grad_queries_hbm)
    wait_all(kv_copies)
    for k, (grad, factor) in enumerate(both_grads):
        own = grad[mine_rows, WINDOW:] * factor + r.kv_recv[k].astype(f32)
        edge = r.edge_recv[0, k].astype(f32) + r.edge_recv[1, k].astype(f32)
        r.grad_kv[k] = jnp.concatenate(
            [own[:, : tokens - WINDOW], own[:, tokens - WINDOW :] + edge], axis=1
        ).astype(bf16)
    store(r.grad_kv, r.grad_kv_hbm)
    wait_all(sinks_x)
    sink_sum = r.sink_x[0]
    for k in range(1, NX):
        sink_sum += r.sink_x[k]
    for h in range(heads):
        r.grad_sinks[h] = jnp.sum(jnp.where(query_row == h, sink_sum, 0.0))
    wait_all(stores)


def hand_over(*refs):
    count = len(refs) // 2
    for source, result in zip(refs[: count - 1], refs[count:]):
        result[...] = source[...]
    for h in range(refs[-1].shape[0]):
        refs[-1][h] = refs[count - 1][h]


def shards(
    queries,
    keys,
    values,
    sinks,
    doc_ids,
    upper_grad,
    out_proj,
    final_hidden,
    advantages,
    slot_pos,
    slot_live,
    sampled_ids,
    policy_head,
    reference_head,
):
    vmem = pl.BlockSpec(memory_space=pltpu.VMEM)
    smem = pl.BlockSpec(memory_space=pltpu.SMEM)
    hbm = pl.BlockSpec(memory_space=pl.ANY)
    heads = sinks.shape[0]
    tokens = queries.shape[0]
    operands = [
        ("hidden_hbm", final_hidden),
        ("advantages_hbm", advantages.reshape(1, SLOTS)),
        ("sampled_hbm", sampled_ids),
        ("live_hbm", slot_live),
        ("slot_pos_hbm", slot_pos),
        ("sinks_hbm", sinks),
        ("docs_hbm", doc_ids.reshape(tokens // WINDOW, WINDOW)),
        ("queries_hbm", queries),
        ("upper_hbm", upper_grad),
        ("keys_hbm", keys),
        ("values_hbm", values),
        ("proj_hbm", out_proj.T),
        ("policy_hbm", policy_head),
        ("frozen_hbm", reference_head),
    ]
    results = [
        ("grad_queries_hbm", jax.ShapeDtypeStruct(queries.shape, bf16), vmem),
        ("grad_kv_hbm", jax.ShapeDtypeStruct((2, HD // 2, tokens), bf16), vmem),
        ("hidden_grad_hbm", jax.ShapeDtypeStruct(final_hidden.shape, f32), vmem),
        ("grad_sinks", jax.ShapeDtypeStruct((heads,), f32), smem),
    ]
    scratch = named_scratch(heads, tokens, policy_head.shape[0])
    names = [entry[0] for entry in operands + results] + list(scratch)
    shapes = [shape for _, shape, _ in results]
    made = pl.pallas_call(
        kernel_of(names),
        out_shape=shapes,
        in_specs=[hbm] * len(operands),
        out_specs=[hbm] * 3 + [smem],
        scratch_shapes=list(scratch.values()),
        compiler_params=pltpu.CompilerParams(
            collective_id=0, has_side_effects=True, vmem_limit_bytes=56 * 2**20
        ),
    )(*[value for _, value in operands])
    grad_queries, grad_kv, hidden_grad, grad_sinks = pl.pallas_call(
        hand_over,
        out_shape=shapes,
        in_specs=[spec for _, _, spec in results],
        out_specs=[spec for _, _, spec in results],
        compiler_params=pltpu.CompilerParams(vmem_limit_bytes=60 * 2**20),
    )(*made)
    return (grad_queries, grad_kv, grad_sinks, hidden_grad)


def solution(mesh):
    in_specs = (
        P("seq", "vocab"),
        P("seq", None),
        P("seq", None),
        P("vocab"),
        P("seq"),
        P("seq", "vocab"),
        P("vocab", None),
        P("seq", None),
        P("seq"),
        P("seq"),
        P("seq"),
        P("seq"),
        P(("seq", "vocab"), None),
        P(("seq", "vocab"), None),
    )
    out_specs = (P("seq", "vocab"), P(None, "vocab", "seq"), P("vocab"), P("seq", None))
    return jax.shard_map(shards, mesh=mesh, in_specs=in_specs, out_specs=out_specs, check_vma=False)
```

```python
import jax
import jax.numpy as jnp
from jax import lax
from jax.experimental import pallas as pl
from jax.experimental.pallas import tpu as pltpu
from jax.sharding import PartitionSpec as P

HD = 64
WINDOW = 128
NX, NY, NZ, NC = 4, 8, 8, 2
D = 2880
QUARTER = 768
HALF = 2 * QUARTER
SLOTS = 8
PART = NY // 2
CHUNK = QUARTER // 2

loss_scale = 64.0
kl_weight = 1.0
masked_score = -1e30
contract_last = (((1,), (1,)), ((), ()))
contract_first = (((0,), (0,)), ((), ()))
MESH = pl.DeviceIdType.MESH
f32 = jnp.float32
bf16 = jnp.bfloat16


def wrap(value, size):
    return lax.rem(value + size, size)


def device(x, y, z, c):
    return (y * NX + x, z * NC + c)


def unfold(block, row):
    return jnp.concatenate([block[row : row + 1], block[row + 3 : row + 4]], axis=1)


def fold(rows):
    half = rows[0].shape[1] // 2
    parts = [row[:, :half] for row in rows] + [row[:, half:] for row in rows]
    return jnp.concatenate(parts + [jnp.zeros((2, half), f32)], axis=0)


def merged(blocks):
    top = blocks[0]
    for block in blocks[1:]:
        top = jnp.maximum(top, block)
    mass, cross = 0.0, 0.0
    for block in blocks:
        share = jnp.exp(block - top)
        mass += share
        cross += pltpu.roll(share, 2, axis=0) * block
    row = lax.broadcasted_iota(jnp.int32, top.shape, 0)
    return jnp.where(
        (row == 2) | (row == 5), cross / pltpu.roll(mass, 2, axis=0), top + jnp.log(mass)
    )


def far_first(size):
    return sorted(range(1, size), key=lambda d: (-min(d, size - d), d))


def quarter_stop(q):
    return min(D, (q + 1) * QUARTER)


def named_scratch(heads, tokens, vocab_rows):
    dma = pltpu.SemaphoreType.DMA
    rows = NX * NY * SLOTS
    stat = (8, rows // 2)
    width = heads * HD
    tiles = tokens // WINDOW
    lanes = heads * WINDOW
    return {
        "policy": pltpu.VMEM((vocab_rows, D), bf16),
        "frozen": pltpu.VMEM((vocab_rows, D), bf16),
        "proj": pltpu.VMEM((D, width), bf16),
        "key_cols": pltpu.VMEM((tokens, 128), bf16),
        "value_cols": pltpu.VMEM((tokens, 128), bf16),
        "kv_own": pltpu.VMEM((tokens, 128), bf16),
        "kv_halo": pltpu.VMEM((WINDOW, 128), bf16),
        "doc_own": pltpu.VMEM((8, WINDOW), f32),
        "doc_halo": pltpu.VMEM((8, WINDOW), f32),
        "key_ext": pltpu.VMEM((tokens + WINDOW, HD), bf16),
        "value_ext": pltpu.VMEM((tokens + WINDOW, HD), bf16),
        "key_marks": pltpu.VMEM((tiles + 1, WINDOW, WINDOW), f32),
        "query_t": pltpu.VMEM((width, tokens), bf16),
        "upper_t": pltpu.VMEM((width, tokens), f32),
        "prob": pltpu.VMEM((tiles, WINDOW, lanes), f32),
        "prob_low": pltpu.VMEM((tiles, 2 * WINDOW, lanes), bf16),
        "share": pltpu.VMEM((tiles, 1, lanes), f32),
        "attended": pltpu.VMEM((tiles, HD, lanes), f32),
        "query_grad": pltpu.VMEM((width, tokens), f32),
        "key_grad": pltpu.VMEM((HD, tokens + WINDOW), f32),
        "value_grad": pltpu.VMEM((HD, tokens + WINDOW), f32),
        "kv_send": pltpu.VMEM((2, HD // 2, tokens), bf16),
        "kv_recv": pltpu.VMEM((2, HD // 2, tokens), bf16),
        "edge_send": pltpu.VMEM((2, 2, HD // 2, WINDOW), bf16),
        "edge_recv": pltpu.VMEM((2, 2, HD // 2, WINDOW), bf16),
        "sink_y": pltpu.VMEM((NY, 1, WINDOW), f32),
        "sink_x": pltpu.VMEM((NX, 1, WINDOW), f32),
        "wide": pltpu.VMEM((4, SLOTS, QUARTER), f32),
        "gathered": pltpu.VMEM((1, 2, NX, 2, PART, 2 * SLOTS, QUARTER), bf16),
        "rows": pltpu.VMEM((4, rows, QUARTER), bf16),
        "meta_y": pltpu.VMEM((NY,) + stat, f32),
        "meta_x": pltpu.VMEM((NX,) + stat, f32),
        "stat_xc": pltpu.VMEM((NX * NC,) + stat, f32),
        "stat_y": pltpu.VMEM((NY,) + stat, f32),
        "stat_z": pltpu.VMEM((NZ,) + stat, f32),
        "total": pltpu.VMEM((4, NX, NY * SLOTS, QUARTER), f32),
        "outgoing": pltpu.VMEM((2, NX, NY * SLOTS, QUARTER), bf16),
        "from_core": pltpu.VMEM((2, NX, NY * SLOTS, QUARTER), bf16),
        "send_x": pltpu.VMEM((2, NX, 2, PART * SLOTS, QUARTER), bf16),
        "relay": pltpu.VMEM((2, 2, PART * SLOTS, QUARTER), bf16),
        "from_x": pltpu.VMEM((2, 4, PART * SLOTS, QUARTER), bf16),
        "send_y": pltpu.VMEM((2, NY, 2 * SLOTS, CHUNK), bf16),
        "from_y": pltpu.VMEM((2, NY, 2 * SLOTS, CHUNK), bf16),
        "from_z": pltpu.VMEM((2, NZ, 2 * SLOTS, CHUNK), bf16),
        "final": pltpu.VMEM((4, 2 * SLOTS, CHUNK), f32),
        "queries": pltpu.VMEM((tokens, width), bf16),
        "upper": pltpu.VMEM((tokens, width), bf16),
        "slot_hot": pltpu.VMEM((tokens, WINDOW), f32),
        "slot_query": pltpu.VMEM((HD, WINDOW), bf16),
        "slot_upper": pltpu.VMEM((HD, WINDOW), f32),
        "slot_prob": pltpu.VMEM((tokens + WINDOW, WINDOW), f32),
        "slot_attended": pltpu.VMEM((HD, WINDOW), f32),
        "slot_share": pltpu.VMEM((1, WINDOW), f32),
        "sink_bulk": pltpu.VMEM((8, WINDOW), f32),
        "hidden": pltpu.VMEM((SLOTS, D), bf16),
        "advantages": pltpu.VMEM((1, SLOTS), bf16),
        "docs": pltpu.VMEM((tiles, WINDOW), jnp.int32),
        "sampled": pltpu.SMEM((SLOTS,), jnp.int32),
        "live": pltpu.SMEM((SLOTS,), jnp.int32),
        "slot_pos": pltpu.SMEM((SLOTS,), jnp.int32),
        "sinks": pltpu.SMEM((heads,), f32),
        "grad_queries": pltpu.VMEM((tokens, width), bf16),
        "grad_kv": pltpu.VMEM((2, HD // 2, tokens), bf16),
        "hidden_grad": pltpu.VMEM((SLOTS, D), f32),
        "logits": pltpu.VMEM((2, vocab_rows, rows), f32),
        "load_sem": dma((14,)),
        "store_sem": dma((3,)),
        "gy": dma((2, 2 * NY)),
        "gx": dma((2, 12)),
        "gc": dma((2, 16)),
        "my": dma((2, NY)),
        "mx": dma((2, NX)),
        "sxc": dma((2, NX * NC)),
        "sy": dma((2, NY)),
        "sz": dma((2, NZ)),
        "rc": dma((2, 2 * NX)),
        "rx": dma((2, 12)),
        "ry": dma((2, 2 * NY)),
        "rz": dma((2, 2 * NZ)),
        "fc": dma((2, 2)),
        "halo": dma((2, 2)),
        "kv": dma((2, 3)),
        "ky": dma((2, NY)),
        "kx": dma((2, NX)),
    }


class Names:
    def __init__(self, names, refs):
        for name, ref in zip(names, refs):
            setattr(self, name, ref)


def kernel_of(names):
    def kernel(*refs):
        policy_step(Names(names, refs))

    return kernel


def policy_step(r):
    seq, vocab = lax.axis_index("seq"), lax.axis_index("vocab")
    x, y = lax.rem(seq, NX), lax.div(seq, NX)
    z, c = lax.div(vocab, NC), lax.rem(vocab, NC)
    n_seq = NX * NY
    vocab_rows = r.policy.shape[0]
    tokens = r.queries.shape[0]
    heads = r.queries.shape[1] // HD
    tiles = tokens // WINDOW
    scale = HD ** (-0.5)
    left, right, far = wrap(x - 1, NX), wrap(x + 1, NX), wrap(x + 2, NX)
    y_part, y_sub = lax.div(y, PART), lax.rem(y, PART)

    def along_x(d, other=0):
        return device(wrap(x + d, NX), y, z, 1 - c if other else c)

    def along_y(d):
        return device(x, wrap(y + d, NY), z, c)

    def along_z(d):
        return device(x, y, wrap(z + d, NZ), c)

    across = device(x, y, z, 1 - c)
    to_right, to_left = along_x(1), along_x(-1)
    xc_steps = [(d, o) for d in range(NX) for o in range(NC) if d or o]
    prev, after = wrap(seq - 1, n_seq), wrap(seq + 1, n_seq)

    def send(src, dst, sems, k, target):
        copy = pltpu.make_async_remote_copy(
            src_ref=src,
            dst_ref=dst,
            send_sem=sems.at[0, k],
            recv_sem=sems.at[1, k],
            device_id=target,
            device_id_type=MESH,
        )
        copy.start()
        return copy

    def wait_all(copies):
        for copy in copies:
            copy.wait()

    barrier = pltpu.get_barrier_semaphore()
    peers = [along_y(d) for d in far_first(NY)] + [along_x(d, o) for d, o in xc_steps]
    peers += [along_z(d) for d in far_first(NZ)]
    peers += [(owner, z * NC + o) for owner in (prev, after) for o in range(NC)]
    for peer in peers:
        pl.semaphore_signal(barrier, inc=1, device_id=peer, device_id_type=MESH)

    def load(src, dst, k):
        copy = pltpu.make_async_copy(src, dst, r.load_sem.at[k])
        copy.start()
        return copy

    load_hidden = load(r.hidden_hbm, r.hidden, 0)
    small = [
        load(r.advantages_hbm, r.advantages, 1),
        load(r.sampled_hbm, r.sampled, 2),
        load(r.live_hbm, r.live, 3),
        load(r.slot_pos_hbm, r.slot_pos, 4),
        load(r.sinks_hbm, r.sinks, 5),
        load(r.docs_hbm, r.docs, 6),
    ]
    column = pl.multiple_of(lax.div(z, 2) * 128, 128)
    load_keys = load(r.keys_hbm.at[:, pl.ds(column, 128)], r.key_cols, 7)
    load_values = load(r.values_hbm.at[:, pl.ds(column, 128)], r.value_cols, 8)
    load_queries = load(r.queries_hbm, r.queries, 9)
    load_upper = load(r.upper_hbm, r.upper, 10)
    load_policy = load(r.policy_hbm, r.policy, 11)
    load_frozen = load(r.frozen_hbm, r.frozen, 12)
    load_proj = load(r.proj_hbm, r.proj, 13)

    load_hidden.wait()
    hidden = r.hidden[...].astype(f32)
    r.wide[3] = jnp.zeros((SLOTS, QUARTER), f32)
    for q in range(4):
        r.wide[q, :, : quarter_stop(q) - q * QUARTER] = hidden[:, q * QUARTER : quarter_stop(q)]
    packed = jnp.concatenate([r.wide[2 * c], r.wide[2 * c + 1]], axis=0).astype(bf16)
    r.gathered[0, c, x, y_part, y_sub] = packed
    wait_all(small)
    stat = r.meta_y.shape[1:]
    field = lax.broadcasted_iota(jnp.int32, stat, 0)
    lane = lax.broadcasted_iota(jnp.int32, stat, 1) + jnp.where(field < 3, 0, stat[1])
    field = jnp.where(field < 3, field, field - 3)
    meta = jnp.zeros(stat, f32)
    first_lane = (x * NY + y) * SLOTS
    for k in range(SLOTS):
        value = jnp.where(field == 1, r.sampled[k].astype(f32), r.live[k].astype(f32))
        meta = jnp.where(lane == first_lane + k, value, meta)
    advantages = jnp.concatenate([r.advantages[...].astype(f32)] * (stat[1] // SLOTS), axis=1)
    mine_here = (lane >= first_lane) & (lane < first_lane + SLOTS) & (field == 0)
    meta = jnp.where(mine_here, jnp.broadcast_to(advantages, stat), meta)
    r.meta_y[y] = meta
    pl.semaphore_wait(barrier, len(peers))

    copies_y = [[]]
    for k in range(1):
        own_slot = r.gathered.at[k, c, x, y_part, y_sub]
        for d in far_first(NY):
            copies_y[k].append(send(own_slot, own_slot, r.gy, k * NY + d, along_y(d)))
    metas_y = [send(r.meta_y.at[y], r.meta_y.at[y], r.my, d, along_y(d)) for d in range(1, NY)]

    load_keys.wait()
    load_values.wait()

    def swapped(block):
        return jnp.concatenate([block[:, HD:], block[:, :HD]], axis=1)

    key_cols, value_cols = r.key_cols[...].astype(f32), r.value_cols[...].astype(f32)
    even = lax.rem(z, 2) == 0
    key_part = jnp.where(even, key_cols, swapped(key_cols))
    value_part = jnp.where(even, swapped(value_cols), value_cols)
    low_lanes = lax.broadcasted_iota(jnp.int32, key_cols.shape, 1) < HD
    r.kv_own[...] = jnp.where(low_lanes, key_part, value_part).astype(bf16)
    docs = r.docs[...].astype(f32)
    r.doc_own[...] = jnp.broadcast_to(docs[tiles - 1 :], r.doc_own.shape)
    after_me = (after, vocab)
    halos = [
        send(r.kv_own.at[pl.ds(tokens - WINDOW, WINDOW)], r.kv_halo, r.halo, 0, after_me),
        send(r.doc_own, r.doc_halo, r.halo, 1, after_me),
    ]
    load_queries.wait()
    load_upper.wait()
    r.query_t[...] = jnp.transpose(r.queries[...].astype(f32)).astype(bf16)
    r.upper_t[...] = jnp.transpose(r.upper[...].astype(f32))

    key_row = lax.broadcasted_iota(jnp.int32, (WINDOW, WINDOW), 0)
    query_col = lax.broadcasted_iota(jnp.int32, (WINDOW, WINDOW), 1)
    earlier = key_row > query_col
    query_row = lax.broadcasted_iota(jnp.int32, (1, WINDOW), 1)

    def per_head(block):
        return jnp.concatenate([block] * heads, axis=1)

    def by_head(ref, t):
        lanes = slice(t * WINDOW, (t + 1) * WINDOW)
        return jnp.concatenate([ref[h * HD : (h + 1) * HD, lanes] for h in range(heads)], axis=1)

    earlier_wide = per_head(earlier.astype(f32)) > 0.5
    sink_row = jnp.concatenate([jnp.full((1, WINDOW), r.sinks[h]) for h in range(heads)], axis=1)

    def both_blocks(block):
        return jnp.concatenate(
            [jnp.where(earlier_wide, block, 0.0), jnp.where(earlier_wide, 0.0, block)], axis=0
        ).astype(bf16)

    def one_block(strip):
        return jnp.where(earlier_wide, strip[:WINDOW], strip[WINDOW:])

    def attention_setup():
        wait_all(halos)
        kv_halo = r.kv_halo[...].astype(f32)
        kv_own = r.kv_own[...].astype(f32)
        r.key_ext[:WINDOW] = kv_halo[:, :HD].astype(bf16)
        r.key_ext[WINDOW:] = kv_own[:, :HD].astype(bf16)
        r.value_ext[:WINDOW] = kv_halo[:, HD:].astype(bf16)
        r.value_ext[WINDOW:] = kv_own[:, HD:].astype(bf16)
        halo_docs = jnp.where(seq == 0, -1.0, r.doc_halo[0:1])
        for t in range(tiles + 1):
            row = halo_docs if t == 0 else docs[t - 1 : t]
            r.key_marks[t] = jnp.transpose(jnp.broadcast_to(row, (WINDOW, WINDOW)))

    def attention_forward(t):
        strip = slice(t * WINDOW, (t + 2) * WINDOW)
        marks = jnp.where(earlier, r.key_marks[t], r.key_marks[t + 1])
        allowed = per_head((marks == docs[t : t + 1]).astype(f32)) > 0.5
        scores = one_block(
            jnp.dot(r.key_ext[strip], by_head(r.query_t, t), preferred_element_type=f32)
        )
        masked = jnp.where(allowed, scores * scale, masked_score)
        row_top = jnp.maximum(jnp.max(masked, axis=0, keepdims=True), sink_row)
        exp_terms = jnp.where(allowed, jnp.exp(masked - row_top), 0.0)
        sink_term = jnp.exp(sink_row - row_top)
        inverse = 1.0 / (jnp.sum(exp_terms, axis=0, keepdims=True) + sink_term)
        query_token = query_row + t * WINDOW
        keep = jnp.ones((1, WINDOW), f32)
        for k in range(SLOTS):
            keep = jnp.where(query_token == r.slot_pos[k], 0.0, keep)
        keep = per_head(keep)
        prob = exp_terms * (inverse * keep)
        low = both_blocks(prob)
        r.prob[t] = prob
        r.prob_low[t] = low
        r.share[t] = sink_term * inverse * keep
        r.attended[t] = lax.dot_general(
            r.value_ext[strip], low, contract_first, preferred_element_type=f32
        )

    def attention_backward(t):
        strip = slice(t * WINDOW, (t + 2) * WINDOW)
        grads_wide = by_head(r.upper_t, t)
        delta = jnp.sum(grads_wide * r.attended[t], axis=0, keepdims=True)
        sink_part = r.share[t] * delta
        for h in range(heads):
            r.sink_bulk[h : h + 1] -= sink_part[:, h * WINDOW : (h + 1) * WINDOW]
        grads = grads_wide.astype(bf16)
        dprob = one_block(jnp.dot(r.value_ext[strip], grads, preferred_element_type=f32))
        dscore = both_blocks(r.prob[t] * (dprob - delta))
        r.key_grad[:, strip] += lax.dot_general(
            by_head(r.query_t, t), dscore, contract_last, preferred_element_type=f32
        )
        r.value_grad[:, strip] += lax.dot_general(
            grads, r.prob_low[t], contract_last, preferred_element_type=f32
        )
        query_grad = scale * lax.dot_general(
            r.key_ext[strip], dscore, contract_first, preferred_element_type=f32
        )
        for h in range(heads):
            r.query_grad[h * HD : (h + 1) * HD, t * WINDOW : (t + 1) * WINDOW] = query_grad[
                :, h * WINDOW : (h + 1) * WINDOW
            ]

    lane_head = lax.div(query_row, SLOTS)

    def head_hot(h):
        return jnp.where(lane_head == h, r.slot_hot[...], 0.0).astype(bf16)

    def slot_setup():
        slot_of = lax.rem(query_row, SLOTS)
        pos_row = jnp.full((1, WINDOW), -1, jnp.int32)
        for k in range(SLOTS):
            pos_row = jnp.where(slot_of == k, r.slot_pos[k], pos_row)
        sink_slot = jnp.zeros((1, WINDOW), f32)
        for h in range(heads):
            sink_slot = jnp.where(lane_head == h, r.sinks[h], sink_slot)
        used = lane_head < heads
        token_row = lax.broadcasted_iota(jnp.int32, (tokens, WINDOW), 0)
        r.slot_hot[...] = jnp.where((token_row == pos_row) & used, 1.0, 0.0)
        doc_row = jnp.zeros((1, WINDOW), f32)
        for t in range(tiles):
            hot = r.slot_hot[t * WINDOW : (t + 1) * WINDOW]
            doc_row += jnp.sum(hot * r.key_marks[t + 1], axis=0, keepdims=True)
        query, upper = 0.0, 0.0
        for h in range(heads):
            hot, span = head_hot(h), slice(h * HD, (h + 1) * HD)
            query += jnp.dot(r.query_t[span], hot, preferred_element_type=f32)
            upper += jnp.dot(r.upper_t[span].astype(bf16), hot, preferred_element_type=f32)
        r.slot_query[...] = query.astype(bf16)
        r.slot_upper[...] = upper
        scores = jnp.dot(r.key_ext[...], r.slot_query[...], preferred_element_type=f32)
        key_at = lax.broadcasted_iota(jnp.int32, scores.shape, 0)
        behind = pos_row + WINDOW - key_at
        marks = r.key_marks[...].reshape(scores.shape)
        allowed = (behind >= 0) & (behind < WINDOW) & (marks == doc_row) & used
        masked = jnp.where(allowed, scores * scale, masked_score)
        row_top = jnp.maximum(jnp.max(masked, axis=0, keepdims=True), sink_slot)
        exp_terms = jnp.where(allowed, jnp.exp(masked - row_top), 0.0)
        sink_term = jnp.exp(sink_slot - row_top)
        inverse = 1.0 / (jnp.sum(exp_terms, axis=0, keepdims=True) + sink_term)
        prob = exp_terms * inverse
        r.slot_prob[...] = prob
        r.slot_share[...] = jnp.where(used, sink_term * inverse, 0.0)
        r.slot_attended[...] = lax.dot_general(
            r.value_ext[...], prob.astype(bf16), contract_first, preferred_element_type=f32
        )

    r.key_grad[...] = jnp.zeros(r.key_grad.shape, f32)
    r.value_grad[...] = jnp.zeros(r.value_grad.shape, f32)
    r.sink_bulk[...] = jnp.zeros(r.sink_bulk.shape, f32)
    sent_x, sent_c, order = [[], []], [[], []], [[], []]

    def along(k, group, part, target):
        block = r.gathered.at[k, c, group, part]
        sent_x[k].append(send(block, block, r.gx, 6 * k + len(sent_x[k]), target))

    def cross_send(k, group, part):
        block = r.gathered.at[k, c, group, part]
        sent_c[k].append(send(block, block, r.gc, 8 * k + len(sent_c[k]), across))
        order[k].append((group, part))

    def arrange(k, half, group, part):
        block = r.gathered[k, half, group, part].astype(f32).reshape(PART, 2, SLOTS, QUARTER)
        start = pl.multiple_of((group * 2 + part) * (PART * SLOTS), PART * SLOTS)
        for low in range(2):
            r.rows[2 * half + low, pl.ds(start, PART * SLOTS), :] = (
                block[:, low].reshape(PART * SLOTS, QUARTER).astype(bf16)
            )

    def spread(k):
        wait_all(copies_y[k])
        along(k, x, 0, to_right)
        along(k, x, 1, to_left)
        along(k, x, 1, to_right)
        along(k, x, 0, to_left)
        cross_send(k, x, 0)
        cross_send(k, x, 1)

    def relay_on(k):
        sent_x[k][0].wait_recv()
        along(k, left, 0, to_right)
        cross_send(k, left, 0)
        sent_x[k][1].wait_recv()
        along(k, right, 1, to_left)
        cross_send(k, right, 1)

    def direct_rest(k):
        sent_x[k][2].wait_recv()
        cross_send(k, left, 1)
        sent_x[k][3].wait_recv()
        cross_send(k, right, 0)

    def far_rest(k):
        sent_x[k][4].wait_recv()
        cross_send(k, far, 0)
        sent_x[k][5].wait_recv()
        cross_send(k, far, 1)

    def arrange_own(k):
        for group, part in order[k]:
            arrange(k, c, group, part)

    spread(0)
    wait_all(metas_y)
    meta = r.meta_y[0]
    for k in range(1, NY):
        meta += r.meta_y[k]
    r.meta_x[x] = meta
    metas_x = [send(r.meta_x.at[x], r.meta_x.at[x], r.mx, d, along_x(d)) for d in range(1, NX)]
    attention_setup()
    relay_on(0)
    attention_forward(0)
    direct_rest(0)
    attention_forward(1)
    far_rest(0)
    attention_forward(2)
    arrange_own(0)
    for t in range(3, tiles):
        attention_forward(t)
    load_policy.wait()
    load_frozen.wait()

    def add_logits(half, first):
        for i, head in enumerate([r.policy, r.frozen]):
            result = 0.0
            for q in (2 * half, 2 * half + 1):
                width = quarter_stop(q) - q * QUARTER
                result += lax.dot_general(
                    head[:, q * QUARTER : quarter_stop(q)],
                    r.rows[q, :, :width],
                    contract_last,
                    preferred_element_type=f32,
                )
            r.logits[i] = result if first else r.logits[i] + result

    for half in range(2):
        pl.when(c == half)(lambda half=half: add_logits(half, True))
    for k in range(1):
        for copy, (group, part) in zip(sent_c[k], order[k]):
            copy.wait_recv()
            arrange(k, 1 - c, group, part)
    for half in range(2):
        pl.when(c != half)(lambda half=half: add_logits(half, False))
    for copy in sent_x[0] + sent_x[1] + sent_c[0] + sent_c[1]:
        copy.wait_send()
    wait_all(metas_x)
    meta = r.meta_x[0]
    for k in range(1, NX):
        meta += r.meta_x[k]

    policy_logits, frozen_logits = r.logits[0], r.logits[1]
    policy_peak = jnp.max(policy_logits, axis=0, keepdims=True)
    frozen_peak = jnp.max(frozen_logits, axis=0, keepdims=True)
    logit_diff = policy_logits - frozen_logits
    policy_terms = jnp.exp(policy_logits - policy_peak)
    mass = jnp.sum(policy_terms, axis=0, keepdims=True)
    mean = jnp.sum(policy_terms * logit_diff, axis=0, keepdims=True) / mass
    frozen_mass = jnp.sum(jnp.exp(frozen_logits - frozen_peak), axis=0, keepdims=True)
    stats = [policy_peak + jnp.log(mass), frozen_peak + jnp.log(frozen_mass), mean]

    r.stat_xc[0] = fold(stats)
    copies = [
        send(r.stat_xc.at[0], r.stat_xc.at[k + 1], r.sxc, k, along_x(d, o))
        for k, (d, o) in enumerate(xc_steps)
    ]
    wait_all(copies)
    r.stat_y[0] = merged([r.stat_xc[k] for k in range(NX * NC)])
    copies = [
        send(r.stat_y.at[0], r.stat_y.at[d], r.sy, d, along_y(d)) for d in far_first(NY)
    ]
    wait_all(copies)
    r.stat_z[0] = merged([r.stat_y[k] for k in range(NY)])
    copies = [
        send(r.stat_z.at[0], r.stat_z.at[d], r.sz, d, along_z(d)) for d in far_first(NZ)
    ]
    wait_all(copies)
    stats = merged([r.stat_z[k] for k in range(NZ)])
    policy_lognorm, frozen_lognorm, cross_total = [unfold(stats, k) for k in range(3)]

    divergence = cross_total - policy_lognorm + frozen_lognorm
    policy_prob = jnp.exp(policy_logits - policy_lognorm)
    first_id = (seq * (NZ * NC) + vocab) * vocab_rows
    ids_here = (first_id + lax.broadcasted_iota(jnp.int32, policy_logits.shape, 0)).astype(f32)
    picked = (ids_here == unfold(meta, 1)).astype(f32)
    weight = loss_scale * unfold(meta, 2)
    log_ratio = policy_logits - policy_lognorm - (frozen_logits - frozen_lognorm) - divergence
    logit_grad = (
        weight * (-unfold(meta, 0) * (picked - policy_prob) + kl_weight * policy_prob * log_ratio)
    ).astype(bf16)

    group_rows = NY * SLOTS
    r.total[3, :, :, D - 3 * QUARTER - 64 :] = jnp.zeros(
        (NX, group_rows, 4 * QUARTER - D + 64), f32
    )

    def product(half):
        stop = quarter_stop(2 * half + 1)
        whole = lax.dot_general(
            logit_grad,
            r.policy[:, half * HALF : stop],
            contract_first,
            preferred_element_type=f32,
        )
        for q in (2 * half, 2 * half + 1):
            width = quarter_stop(q) - q * QUARTER
            low = (q - 2 * half) * QUARTER
            r.total[q, :, :, :width] = whole[:, low : low + width].reshape(NX, group_rows, width)

    for half in range(2):
        pl.when(c != half)(lambda half=half: product(half))
    part_rows = PART * SLOTS
    low_part, high_part = slice(0, part_rows), slice(part_rows, 2 * part_rows)
    cores, reduced, copies_y, copies_z = [[], []], [[], []], [[], []], [[], []]
    for k in range(2):
        for i, group in enumerate([far, right, left, x]):
            r.outgoing[k, group] = r.total[2 * (1 - c) + k, group].astype(bf16)
            cores[k].append(
                send(r.outgoing.at[k, group], r.from_core.at[k, group], r.rc, NX * k + i, across)
            )

    for half in range(2):
        pl.when(c == half)(lambda half=half: product(half))

    def pass_on(k, src, dst, target):
        reduced[k].append(send(src, dst, r.rx, 6 * k + len(reduced[k]), target))

    def chip_sum(k, i, group):
        cores[k][i].wait_recv()
        return r.total[2 * c + k, group] + r.from_core[k, group].astype(f32)

    def start_far(k):
        both = chip_sum(k, 0, far)
        r.send_x[k, far, 0] = both[low_part].astype(bf16)
        r.send_x[k, far, 1] = both[high_part].astype(bf16)
        pass_on(k, r.send_x.at[k, far, 0], r.relay.at[k, 0], to_right)
        pass_on(k, r.send_x.at[k, far, 1], r.relay.at[k, 1], to_left)

    def start_direct(k):
        for_right = chip_sum(k, 1, right)
        r.send_x[k, right, 1] = for_right[high_part].astype(bf16)
        pass_on(k, r.send_x.at[k, right, 1], r.from_x.at[k, 0], to_right)
        r.total[2 * c + k, right, low_part] = for_right[low_part]
        for_left = chip_sum(k, 2, left)
        r.send_x[k, left, 0] = for_left[low_part].astype(bf16)
        pass_on(k, r.send_x.at[k, left, 0], r.from_x.at[k, 1], to_left)
        r.total[2 * c + k, left, high_part] = for_left[high_part]

    def start_summed(k):
        reduced[k][0].wait_recv()
        block = r.total[2 * c + k, right, low_part] + r.relay[k, 0].astype(f32)
        r.send_x[k, right, 0] = block.astype(bf16)
        pass_on(k, r.send_x.at[k, right, 0], r.from_x.at[k, 2], to_right)
        reduced[k][1].wait_recv()
        block = r.total[2 * c + k, left, high_part] + r.relay[k, 1].astype(f32)
        r.send_x[k, left, 1] = block.astype(bf16)
        pass_on(k, r.send_x.at[k, left, 1], r.from_x.at[k, 3], to_left)
        r.total[2 * c + k, x] = chip_sum(k, 3, x)

    def start_y(k):
        for copy in reduced[k][2:]:
            copy.wait_recv()
        for part, (rows, first, second) in enumerate([(low_part, 1, 2), (high_part, 0, 3)]):
            mine = r.total[2 * c + k, x, rows] + r.from_x[k, first].astype(f32)
            mine = (mine + r.from_x[k, second].astype(f32)).reshape(PART, SLOTS, QUARTER)
            packed = jnp.concatenate([mine[:, :, :CHUNK], mine[:, :, CHUNK:]], axis=1)
            r.send_y[k, part * PART : (part + 1) * PART] = packed.astype(bf16)
        for d in far_first(NY):
            copies_y[k].append(
                send(
                    r.send_y.at[k, wrap(y + d, NY)],
                    r.from_y.at[k, d],
                    r.ry,
                    NY * k + d,
                    along_y(d),
                )
            )

    def start_z(k):
        wait_all(copies_y[k])
        summed = r.send_y[k, y].astype(f32)
        for d in range(1, NY):
            summed += r.from_y[k, d].astype(f32)
        r.from_z[k, z] = summed.astype(bf16)
        block = r.from_z.at[k, z]
        for d in far_first(NZ):
            copies_z[k].append(send(block, block, r.rz, NZ * k + d, along_z(d)))

    def start_core(k):
        wait_all(copies_z[k])
        summed = r.from_z[k, 0].astype(f32)
        for d in range(1, NZ):
            summed += r.from_z[k, d].astype(f32)
        r.final[2 * c + k] = summed
        block = r.final.at[2 * c + k]
        return send(block, block, r.fc, k, across)

    start_far(0)
    start_direct(0)
    start_far(1)
    attention_backward(0)
    start_summed(0)
    start_direct(1)
    attention_backward(1)
    start_summed(1)
    attention_backward(2)
    start_y(0)
    for t in range(3, tiles):
        attention_backward(t)
    start_y(1)
    slot_setup()
    start_z(0)
    start_z(1)
    load_proj.wait()
    finals = [start_core(0), start_core(1)]
    slot_grad = 0.0
    for k in range(2):
        finals[k].wait()
        for q in (k, 2 + k):
            stop = quarter_stop(q)
            part = jnp.concatenate([r.final[q, :SLOTS, :], r.final[q, SLOTS:, :]], axis=1)
            part = part[:, : stop - q * QUARTER]
            r.hidden_grad[:, q * QUARTER : stop] = part
            slot_grad += jnp.dot(
                part.astype(bf16), r.proj[q * QUARTER : stop, :], preferred_element_type=f32
            )
    for copy in cores[0] + cores[1] + reduced[0] + reduced[1]:
        copy.wait_send()
    stores = []

    def store(src, dst):
        copy = pltpu.make_async_copy(src, dst, r.store_sem.at[len(stores)])
        copy.start()
        stores.append(copy)

    store(r.hidden_grad, r.hidden_grad_hbm)
    slot_at = lax.broadcasted_iota(jnp.int32, (SLOTS, WINDOW), 0)
    spread_out = lax.rem(lax.broadcasted_iota(jnp.int32, (SLOTS, WINDOW), 1), SLOTS) == slot_at
    wide_grad = lax.dot_general(
        slot_grad,
        spread_out.astype(f32),
        contract_first,
        precision=lax.Precision.HIGHEST,
        preferred_element_type=f32,
    )
    slot_out = r.slot_upper[...]
    for h in range(heads):
        slot_out += jnp.where(lane_head == h, wide_grad[h * HD : (h + 1) * HD], 0.0)
    slot_low = slot_out.astype(bf16)
    slot_delta = jnp.sum(slot_low.astype(f32) * r.slot_attended[...], axis=0, keepdims=True)
    slot_sink = r.slot_share[...] * slot_delta
    sink_heads = lax.broadcasted_iota(jnp.int32, (8, WINDOW), 0)
    sink_block = r.sink_bulk[...] - jnp.where(sink_heads == lane_head, slot_sink, 0.0)
    sink_sums = jnp.sum(sink_block, axis=1, keepdims=True)
    r.sink_y[y] = jnp.sum(jnp.where(sink_heads == query_row, sink_sums, 0.0), axis=0, keepdims=True)
    sinks_y = [
        send(r.sink_y.at[y], r.sink_y.at[y], r.ky, d, along_y(d)) for d in far_first(NY)
    ]
    slot_dprob = jnp.dot(r.value_ext[...], slot_low, preferred_element_type=f32)
    slot_dscore = (r.slot_prob[...] * (slot_dprob - slot_delta)).astype(bf16)
    r.key_grad[...] += lax.dot_general(
        r.slot_query[...], slot_dscore, contract_last, preferred_element_type=f32
    )
    r.value_grad[...] += lax.dot_general(
        slot_low, r.slot_prob[...].astype(bf16), contract_last, preferred_element_type=f32
    )
    half_width = HD // 2
    mine_rows = pl.ds(pl.multiple_of(c * half_width, half_width), half_width)
    other_rows = pl.ds(pl.multiple_of((1 - c) * half_width, half_width), half_width)
    both_grads = [(r.key_grad, scale), (r.value_grad, 1.0)]
    for k, (grad, factor) in enumerate(both_grads):
        r.kv_send[k] = (grad[other_rows, WINDOW:] * factor).astype(bf16)
        r.edge_send[0, k] = (grad[mine_rows, :WINDOW] * factor).astype(bf16)
        r.edge_send[1, k] = (grad[other_rows, :WINDOW] * factor).astype(bf16)
    kv_copies = [
        send(r.edge_send.at[0], r.edge_recv.at[0], r.kv, 0, (prev, vocab)),
        send(r.edge_send.at[1], r.edge_recv.at[1], r.kv, 1, (prev, z * NC + 1 - c)),
        send(r.kv_send, r.kv_recv, r.kv, 2, across),
    ]
    slot_query_grad = scale * lax.dot_general(
        r.key_ext[...], slot_dscore, contract_first, preferred_element_type=f32
    )
    slot_query_low = slot_query_grad.astype(bf16)
    for h in range(heads):
        r.query_grad[h * HD : (h + 1) * HD] += lax.dot_general(
            slot_query_low, head_hot(h), contract_last, preferred_element_type=f32
        )
    wait_all(sinks_y)
    sink_sum = r.sink_y[0]
    for k in range(1, NY):
        sink_sum += r.sink_y[k]
    r.sink_x[x] = sink_sum
    sinks_x = [send(r.sink_x.at[x], r.sink_x.at[x], r.kx, d, along_x(d)) for d in range(1, NX)]
    r.grad_queries[...] = jnp.transpose(r.query_grad[...]).astype(bf16)
    store(r.grad_queries, r.grad_queries_hbm)
    wait_all(kv_copies)
    for k, (grad, factor) in enumerate(both_grads):
        own = grad[mine_rows, WINDOW:] * factor + r.kv_recv[k].astype(f32)
        edge = r.edge_recv[0, k].astype(f32) + r.edge_recv[1, k].astype(f32)
        r.grad_kv[k] = jnp.concatenate(
            [own[:, : tokens - WINDOW], own[:, tokens - WINDOW :] + edge], axis=1
        ).astype(bf16)
    store(r.grad_kv, r.grad_kv_hbm)
    wait_all(sinks_x)
    sink_sum = r.sink_x[0]
    for k in range(1, NX):
        sink_sum += r.sink_x[k]
    for h in range(heads):
        r.grad_sinks[h] = jnp.sum(jnp.where(query_row == h, sink_sum, 0.0))
    wait_all(stores)


def hand_over(*refs):
    count = len(refs) // 2
    for source, result in zip(refs[: count - 1], refs[count:]):
        result[...] = source[...]
    for h in range(refs[-1].shape[0]):
        refs[-1][h] = refs[count - 1][h]


def shards(
    queries,
    keys,
    values,
    sinks,
    doc_ids,
    upper_grad,
    out_proj,
    final_hidden,
    advantages,
    slot_pos,
    slot_live,
    sampled_ids,
    policy_head,
    reference_head,
):
    vmem = pl.BlockSpec(memory_space=pltpu.VMEM)
    smem = pl.BlockSpec(memory_space=pltpu.SMEM)
    hbm = pl.BlockSpec(memory_space=pl.ANY)
    heads = sinks.shape[0]
    tokens = queries.shape[0]
    operands = [
        ("hidden_hbm", final_hidden),
        ("advantages_hbm", advantages.reshape(1, SLOTS)),
        ("sampled_hbm", sampled_ids),
        ("live_hbm", slot_live),
        ("slot_pos_hbm", slot_pos),
        ("sinks_hbm", sinks),
        ("docs_hbm", doc_ids.reshape(tokens // WINDOW, WINDOW)),
        ("queries_hbm", queries),
        ("upper_hbm", upper_grad),
        ("keys_hbm", keys),
        ("values_hbm", values),
        ("proj_hbm", out_proj.T),
        ("policy_hbm", policy_head),
        ("frozen_hbm", reference_head),
    ]
    results = [
        ("grad_queries_hbm", jax.ShapeDtypeStruct(queries.shape, bf16), vmem),
        ("grad_kv_hbm", jax.ShapeDtypeStruct((2, HD // 2, tokens), bf16), vmem),
        ("hidden_grad_hbm", jax.ShapeDtypeStruct(final_hidden.shape, f32), vmem),
        ("grad_sinks", jax.ShapeDtypeStruct((heads,), f32), smem),
    ]
    scratch = named_scratch(heads, tokens, policy_head.shape[0])
    names = [entry[0] for entry in operands + results] + list(scratch)
    shapes = [shape for _, shape, _ in results]
    made = pl.pallas_call(
        kernel_of(names),
        out_shape=shapes,
        in_specs=[hbm] * len(operands),
        out_specs=[hbm] * 3 + [smem],
        scratch_shapes=list(scratch.values()),
        compiler_params=pltpu.CompilerParams(
            collective_id=0, has_side_effects=True, vmem_limit_bytes=56 * 2**20
        ),
    )(*[value for _, value in operands])
    grad_queries, grad_kv, hidden_grad, grad_sinks = pl.pallas_call(
        hand_over,
        out_shape=shapes,
        in_specs=[spec for _, _, spec in results],
        out_specs=[spec for _, _, spec in results],
        compiler_params=pltpu.CompilerParams(vmem_limit_bytes=60 * 2**20),
    )(*made)
    return (grad_queries, grad_kv, grad_sinks, hidden_grad)


def solution(mesh):
    in_specs = (
        P("seq", "vocab"),
        P("seq", None),
        P("seq", None),
        P("vocab"),
        P("seq"),
        P("seq", "vocab"),
        P("vocab", None),
        P("seq", None),
        P("seq"),
        P("seq"),
        P("seq"),
        P("seq"),
        P(("seq", "vocab"), None),
        P(("seq", "vocab"), None),
    )
    out_specs = (P("seq", "vocab"), P(None, "vocab", "seq"), P("vocab"), P("seq", None))
    return jax.shard_map(shards, mesh=mesh, in_specs=in_specs, out_specs=out_specs, check_vma=False)
```
